32 devices in a mesh: dp: 8 (over y, x, core), mp: 4 (over z).
Axes of the slice: x: 2, y: 2, z: 4, core: 2. Of those that a mesh axis runs over, the one named last changes fastest.
Arguments:
- tokens: bfloat16 [64, 196, 768], P(('dp', 'mp')), may hold values from -6 to 6
- window_mask: int32 [64, 196], P(('dp', 'mp')), may hold values from 0 to 1, as said below
- out_grad: bfloat16 [64, 196, 768], P(('dp', 'mp')), may hold values from -6 to 6
- norm1_gain: bfloat16 [768], replicated, may hold values from 0.5 to 1.5
- norm1_shift: bfloat16 [768], replicated, may hold values from -0.625 to 0.625
- qkv_weight: bfloat16 [768, 2304], replicated, may hold values from -0.21875 to 0.21875
- qv_bias: bfloat16 [1536], replicated, may hold values from -0.625 to 0.625
- rel_height: bfloat16 [27, 64], replicated, may hold values from -0.625 to 0.625
- rel_width: bfloat16 [27, 64], replicated, may hold values from -0.625 to 0.625
- proj_weight: bfloat16 [768, 768], replicated, may hold values from -1.5 to 1.5
- proj_bias: bfloat16 [768], replicated, may hold values from -0.625 to 0.625
- norm2_gain: bfloat16 [768], replicated, may hold values from 0.5 to 1.5
- norm2_shift: bfloat16 [768], replicated, may hold values from -0.625 to 0.625
- up_weight: bfloat16 [768, 3072], P(None, 'mp'), may hold values from -0.21875 to 0.21875
- up_bias: bfloat16 [3072], P('mp'), may hold values from -0.625 to 0.625
- down_weight: bfloat16 [3072, 768], P('mp'), may hold values from -0.109375 to 0.109375
- down_bias: bfloat16 [768], replicated, may hold values from -0.625 to 0.625
Outputs:
- block_out: bfloat16 [64, 196, 768], P(('dp', 'mp'))
- tokens_grad: float32 [64, 196, 768], P(('dp', 'mp'))
- norm1_gain_grad: float32 [768], replicated
- norm1_shift_grad: float32 [768], replicated
- qkv_weight_grad: float32 [768, 2304], P('dp')
- qv_bias_grad: float32 [1536], replicated
- rel_height_grad: float32 [27, 64], replicated
- rel_width_grad: float32 [27, 64], replicated
- proj_weight_grad: float32 [768, 768], P('dp')
- proj_bias_grad: float32 [768], replicated
- norm2_gain_grad: float32 [768], replicated
- norm2_shift_grad: float32 [768], replicated
- up_weight_grad: float32 [768, 3072], P('dp', 'mp')
- up_bias_grad: float32 [3072], replicated
- down_weight_grad: float32 [3072, 768], P('mp', 'dp')
- down_bias_grad: float32 [768], replicated
The draws below stay inside these ranges and needn't reach their ends.
Inputs may be any that keep to these rules, and one draw needn't show every extreme that they name: `window_mask`: in each window the patches inside the image are those in the first h rows and the first w columns of its 14 x 14 grid, with h and w between 4 and 14 inclusive.
All inputs are finite; a program needn't handle non-finite values.
Results may differ from the reference program's by a relative error of at most 0.018.
Values may be sent and summed in bfloat16 or wider, within the bound.
No kernel may reach another device: no remote copies, remote signals or barrier semaphores. Data moves between devices by JAX's collectives and lax.ppermute only.
A program may use at most 256 MiB of HBM per device.

```python
import math
import jax
import jax.numpy as jnp
from jax import lax

D = 768
HEADS = 12
HEAD_DIM = 64
FF = 3072
WIN = 14
P_SIZE = 196
RELS = 27
WINDOWS = 64


def draw_window_mask(key, part):
    low_side = max(2, 2 * WIN // 7)
    heights = jax.random.randint(jax.random.fold_in(key, 11), (WINDOWS, 1), low_side, WIN + 1)
    widths = jax.random.randint(jax.random.fold_in(key, 12), (WINDOWS, 1), low_side, WIN + 1)
    places = jnp.arange(WIN * WIN)[None, :]
    return ((places // WIN < heights) & (places % WIN < widths)).astype(jnp.int32)


def block_levels(key, shape, pieces, least, largest):
    def one(dim, shards_of):
        steps = jax.random.uniform(jax.random.fold_in(jax.random.fold_in(key, 6), dim), (shards_of,), jnp.float32, least / len(pieces), largest / len(pieces))
        return jnp.repeat(jnp.exp(steps), shape[dim] // shards_of).reshape((-1,) + (1,) * (len(shape) - dim - 1))

    factor_of = one(*pieces[0])
    for cut in pieces[1:]:
        factor_of = factor_of * one(*cut)
    return factor_of


def gaussian(key, dims, spread, most, cuts=(), kind=jnp.bfloat16):
    values = spread * jax.random.normal(key, dims, jnp.float32)
    if cuts:
        values = values * block_levels(key, dims, cuts, -0.22, 0.18)
    return jnp.clip(values, -most, most).astype(kind)


def setup_inputs(seed: int = 0) -> dict:
    key_list = jax.random.split(jax.random.key(seed), 18)
    return {
        "tokens": gaussian(key_list[0], (WINDOWS, P_SIZE, D), 1.0, 6.0, ((0, 32),)),
        "window_mask": draw_window_mask(jax.random.fold_in(key_list[17], 71), 0),
        "out_grad": gaussian(key_list[2], (WINDOWS, P_SIZE, D), 1.0, 6.0, ((0, 32),)),
        "norm1_gain": jnp.clip(1.0 + 0.1 * jax.random.normal(key_list[3], (D,), jnp.float32), 0.5, 1.5).astype(jnp.bfloat16),
        "norm1_shift": gaussian(key_list[4], (D,), 0.1, 0.625),
        "qkv_weight": gaussian(key_list[5], (D, 3 * D), D ** -0.5, 0.21875),
        "qv_bias": gaussian(key_list[6], (2 * D,), 0.1, 0.625),
        "rel_height": gaussian(key_list[7], (RELS, HEAD_DIM), 0.1, 0.625),
        "rel_width": gaussian(key_list[8], (RELS, HEAD_DIM), 0.1, 0.625),
        "proj_weight": gaussian(key_list[9], (D, D), (max(1, D // 48)) ** -0.5, 1.5),
        "proj_bias": gaussian(key_list[10], (D,), 0.1, 0.625),
        "norm2_gain": jnp.clip(1.0 + 0.1 * jax.random.normal(key_list[11], (D,), jnp.float32), 0.5, 1.5).astype(jnp.bfloat16),
        "norm2_shift": gaussian(key_list[12], (D,), 0.1, 0.625),
        "up_weight": gaussian(key_list[13], (D, FF), D ** -0.5, 0.21875, ((1, 4),)),
        "up_bias": gaussian(key_list[14], (FF,), 0.1, 0.625, ((0, 4),)),
        "down_weight": gaussian(key_list[15], (FF, D), FF ** -0.5, 0.109375, ((0, 4),)),
        "down_bias": gaussian(key_list[16], (D,), 0.1, 0.625),
    }


HIGHEST = lax.Precision.HIGHEST
EPSILON = 1e-06

@jax.custom_vjp
def low(v):
    return lax.optimization_barrier(v.astype(jnp.bfloat16)).astype(jnp.float32)

@jax.custom_vjp
def low_back(v):
    return v

def low_keep(v):
    return (low(v), None)

def low_pass(kept, grad):
    return (grad,)

def back_keep(v):
    return (v, None)

def back_low(kept, grad):
    return (low(grad),)
low.defvjp(low_keep, low_pass)
low_back.defvjp(back_keep, back_low)

def normalize(values, norm_gain, norm_shift):
    average = lax.optimization_barrier(jnp.mean(values, axis=-1, keepdims=True))
    centred = values - average
    variance = lax.optimization_barrier(jnp.mean(centred * centred, axis=-1, keepdims=True))
    return centred * lax.rsqrt(variance + EPSILON) * norm_gain + norm_shift

def selection(side_len):
    offsets = jnp.arange(side_len)[:, None] - jnp.arange(side_len)[None, :] + side_len - 1
    return (offsets[:, :, None] == jnp.arange(2 * side_len - 1)[None, None, :]).astype(jnp.float32)

def window_group(params, group_tokens, group_mask):
    gain_one, shift_one, qkv_w, qkv_b, height_rel, width_rel, proj_w, proj_b, gain_two, shift_two, up_w, up_b, down_w, down_b = params
    win_count = group_tokens.shape[0]
    patches = WIN * WIN
    row_count = win_count * patches
    head_size = D // HEADS
    score_scale = head_size ** (-0.5)
    flat_rows = group_tokens.reshape(row_count, D)
    row_mask = group_mask.reshape(row_count, 1)
    first_low = low(normalize(flat_rows, gain_one, shift_one))
    projected = jnp.dot(first_low, qkv_w, precision=HIGHEST) + qkv_b
    projected = low_back(low(projected)).reshape(win_count, patches, 3, HEADS, head_size)
    queries = projected[:, :, 0]
    keys_all = projected[:, :, 1]
    values_all = projected[:, :, 2]
    products = jnp.einsum('wihc,wjhc->whij', queries, keys_all, precision=HIGHEST) * score_scale
    grid_q = queries.reshape(win_count, WIN, WIN, HEADS, head_size)
    along_h = jnp.einsum('wxyhc,xkc->whxyk', grid_q, height_rel, precision=HIGHEST)
    along_w = jnp.einsum('wxyhc,ykc->whxyk', grid_q, width_rel, precision=HIGHEST)
    combined = products.reshape(win_count, HEADS, WIN, WIN, WIN, WIN) + along_h[..., :, None] + along_w[..., None, :]
    combined = low_back(combined.reshape(win_count, HEADS, patches, patches))
    combined = jnp.where(group_mask[:, None, None, :] > 0.5, combined, -1000000000.0)
    soft_weights = low(jax.nn.softmax(combined, axis=-1))
    attended = jnp.einsum('whij,wjhc->wihc', soft_weights, values_all, precision=HIGHEST).reshape(row_count, D)
    attended = low_back(low(attended))
    attn_out = low_back(jnp.dot(attended, proj_w, precision=HIGHEST) + proj_b)
    middle = flat_rows + row_mask * attn_out
    second_low = low(normalize(middle, gain_two, shift_two))
    hidden_pre = low_back(jnp.dot(second_low, up_w, precision=HIGHEST) + up_b)
    hidden_low = low(jax.nn.gelu(hidden_pre, approximate=False))
    mlp_out = low_back(jnp.dot(hidden_low, down_w, precision=HIGHEST) + down_b)
    return (middle + row_mask * mlp_out).reshape(win_count, patches, D)

def reference(tokens, window_mask, out_grad, norm1_gain, norm1_shift, qkv_weight, qv_bias, rel_height, rel_width, proj_weight, proj_bias, norm2_gain, norm2_shift, up_weight, up_bias, down_weight, down_bias):
    tokens_f = tokens.astype(jnp.float32)
    mask_f = window_mask.astype(jnp.float32)
    float_params = tuple((item.astype(jnp.float32) for item in (norm1_gain, norm1_shift, qkv_weight, qv_bias, rel_height, rel_width, proj_weight, proj_bias, norm2_gain, norm2_shift, up_weight, up_bias, down_weight, down_bias)))
    window_total = tokens.shape[0]
    per_group = math.gcd(window_total, 16)
    group_count = window_total // per_group
    patches = WIN * WIN
    step_fn = jax.checkpoint(window_group)

    def forward(tokens_in, gain_one, shift_one, qkv_w, qv_b, rel_h, rel_w, proj_w, proj_b, gain_two, shift_two, up_w, up_b, down_w, down_b):
        select_table = selection(WIN)
        height_rel = jnp.einsum('xkr,rc->xkc', select_table, low(rel_h), precision=HIGHEST)
        width_rel = jnp.einsum('xkr,rc->xkc', select_table, low(rel_w), precision=HIGHEST)
        qkv_b = jnp.concatenate([qv_b[:D], jnp.zeros((D,), jnp.float32), qv_b[D:]])
        params = (gain_one, shift_one, qkv_w, qkv_b, height_rel, width_rel, proj_w, proj_b, gain_two, shift_two, up_w, up_b, down_w, down_b)

        def scan_step(carry_in, group_in):
            return (carry_in, step_fn(params, group_in[0], group_in[1]))
        grouped = (tokens_in.reshape(group_count, per_group, patches, D), mask_f.reshape(group_count, per_group, patches))
        unused, results = lax.scan(scan_step, jnp.zeros((), jnp.float32), grouped)
        return results.reshape(window_total, patches, D)
    result, pullback = jax.vjp(forward, tokens_f, *float_params)
    gradients = pullback(out_grad.astype(jnp.float32))
    return (result.astype(jnp.bfloat16), gradients[0], gradients[1], gradients[2], gradients[3], gradients[4], gradients[5], gradients[6], gradients[7], gradients[8], gradients[9], gradients[10], gradients[11], gradients[12], gradients[13], gradients[14])
```

```python
import functools

import jax
import jax.numpy as jnp
from jax import lax
from jax.experimental import pallas as pl
from jax.experimental.pallas import tpu as pltpu
from jax.sharding import PartitionSpec as P

D = 768
HEADS = 12
WIN = 14
PATCH = WIN * WIN
ROWS = 208
PAIRS = HEADS // 2
EPSILON = 1e-06
HALF = 384
F32 = jnp.float32
BF16 = jnp.bfloat16
AXES = ("dp", "mp")
VM = pl.BlockSpec(memory_space=pltpu.VMEM)
SMALL_ROWS = 48


def nn(a, b):
    return lax.dot_general(a, b, (((1,), (0,)), ((), ())), preferred_element_type=F32)


def nt(a, b):
    return lax.dot_general(a, b, (((1,), (1,)), ((), ())), preferred_element_type=F32)


def tn(a, b):
    return lax.dot_general(a, b, (((0,), (0,)), ((), ())), preferred_element_type=F32)


def iota(shape, dim):
    return lax.broadcasted_iota(jnp.int32, shape, dim)


def row(ref):
    return ref[...].astype(F32).reshape(1, -1)


def column_mask(mask_ref, w):
    line = mask_ref[w : w + 1, :].astype(F32)
    here = iota((ROWS, PATCH), 0) == iota((ROWS, PATCH), 1)
    return jnp.sum(jnp.where(here, line, 0.0), axis=1, keepdims=True)


def key_mask(column):
    here = iota((ROWS, ROWS), 0) == iota((ROWS, ROWS), 1)
    return jnp.sum(jnp.where(here, column, 0.0), axis=0, keepdims=True)


def norm(x):
    average = jnp.mean(x, axis=-1, keepdims=True)
    centred = x - average
    variance = jnp.mean(centred * centred, axis=-1, keepdims=True)
    inverse = lax.rsqrt(variance + EPSILON)
    return centred * inverse, inverse


def norm_back(e, n, s, gain):
    scaled = e * gain
    mean_grad = jnp.mean(scaled, axis=-1, keepdims=True)
    mean_proj = jnp.mean(scaled * n, axis=-1, keepdims=True)
    return s * (scaled - mean_grad - n * mean_proj)


def colsum(x):
    return jnp.sum(x, axis=0, keepdims=True)


def fill_tables(table, height_ref, width_ref):
    table[...] = jnp.zeros((128, 128), F32)
    height = height_ref[...].astype(F32)
    width = width_ref[...].astype(F32)
    none = jnp.zeros_like(height)
    rels = 2 * WIN - 1
    table[0:rels, :] = jnp.concatenate([height, none], axis=1)
    table[32 : 32 + rels, :] = jnp.concatenate([width, none], axis=1)
    table[64 : 64 + rels, :] = jnp.concatenate([none, height], axis=1)
    table[96 : 96 + rels, :] = jnp.concatenate([none, width], axis=1)


def shift_bits():
    place = iota((ROWS, 128), 0)
    high = place // WIN
    wide = place - high * WIN
    return jnp.where((iota((ROWS, 128), 1) & 32) == 0, high, wide)


def shift_rows(x, amount, left):
    for bit in range(4):
        step = 1 << bit
        moved = pltpu.roll(x, 128 - step if left else step, 1)
        x = jnp.where((amount & step) != 0, moved, x)
    return x


def one_hot(both):
    place = iota((ROWS, 128), 0)
    lane = iota((ROWS, 128), 1)
    high = place // WIN
    wide = place - high * WIN
    want = jnp.where((lane & 32) == 0, high, wide)
    sub = lane & 31
    slot = (sub & 15) if both else sub
    hit = (slot == (WIN - 1) - want) & (place < PATCH)
    return jnp.where(hit, 1.0, 0.0).astype(BF16)


def qkv_kernel(tok_ref, gain_ref, shift_ref, w_ref, bias_ref, first_ref, *refs):
    windows = tok_ref.shape[0]
    outs, xs = refs[:windows], refs[windows]
    gain, shift = row(gain_ref), row(shift_ref)
    xs[ROWS - 16 :, :] = jnp.zeros((16, D), F32)
    for w in range(windows):
        xs[0:PATCH, :] = tok_ref[w].astype(F32)
        n, _ = norm(xs[...])
        first_ref[w * ROWS : (w + 1) * ROWS, :] = (n * gain + shift).astype(BF16)
    bias = row(bias_ref)
    for part in range(3):
        cols = slice(part * D, (part + 1) * D)
        out = nn(first_ref[...], w_ref[:, cols])
        if part == 0:
            out = out + bias[:, :D]
        if part == 2:
            out = out + bias[:, D:]
        for w in range(windows):
            outs[w][:, cols] = out[w * ROWS : (w + 1) * ROWS].astype(BF16)


def attend_kernel(w, mask_ref, qkv_ref, height_ref, width_ref, dep, prob_ref, att_ref, table):
    fill_tables(table, height_ref, width_ref)
    tab = table[...].astype(BF16)
    amount = shift_bits()
    keys_hot = one_hot(True)
    lane = iota((ROWS, 128), 1)
    lower = lane < 64
    sub = lane & 31
    valid = key_mask(column_mask(mask_ref, w)) > 0.5

    def pair(p, carry):
        at = pl.multiple_of(p * 128, 128)
        q = qkv_ref[:, pl.ds(at, 128)]
        k = qkv_ref[:, pl.ds(D + at, 128)]
        v = qkv_ref[:, pl.ds(2 * D + at, 128)]
        terms = shift_rows(nt(q, tab), amount, True)
        coarse = terms.astype(BF16).astype(F32)
        fine = pltpu.roll(terms - coarse, 16, 1)
        terms = jnp.where(sub < WIN, coarse, jnp.where((sub >= 16) & (sub < 16 + WIN), fine, 0.0))
        qs = q.astype(F32) * 0.125
        top = jnp.concatenate([jnp.where(lower, qs, 0.0), jnp.where(lower, terms, 0.0)], axis=1)
        bottom = jnp.concatenate([jnp.where(lower, 0.0, qs), jnp.where(lower, 0.0, terms)], axis=1)
        left = jnp.concatenate([top, bottom], axis=0).astype(BF16)
        right = jnp.concatenate([k, keys_hot], axis=1)
        scores = jnp.where(valid, nt(left, right), -1000000000.0)
        most = jnp.max(scores, axis=1, keepdims=True)
        weight = jnp.exp(scores - most)
        total = jnp.sum(weight, axis=1, keepdims=True)
        prob = (weight * (1.0 / total)).astype(BF16)
        prob_ref[p] = prob
        out = nn(prob, v)
        att_ref[:, pl.ds(at, 128)] = jnp.where(lower, out[:ROWS], out[ROWS:]).astype(BF16)
        return carry

    lax.fori_loop(0, PAIRS, pair, 0, unroll=2)


def project_kernel(tok_ref, mask_ref, cot_ref, w_ref, bias_ref, gain_ref, shift_ref, *refs):
    windows = tok_ref.shape[0]
    atts, (mid_ref, xg_ref, sum_ref, all_ref, xs) = refs[:windows], refs[windows:]
    gain, shift, bias = row(gain_ref), row(shift_ref), row(bias_ref)
    xs[ROWS - 16 :, :] = jnp.zeros((16, D), F32)
    for w in range(windows):
        all_ref[w * ROWS : (w + 1) * ROWS, :] = atts[w][...]
    out = nn(all_ref[...], w_ref[...]) + bias
    total = jnp.zeros((1, D), F32)
    for w in range(windows):
        rows = slice(w * ROWS, (w + 1) * ROWS)
        m = column_mask(mask_ref, w)
        xs[0:PATCH, :] = tok_ref[w].astype(F32)
        mid = xs[...] + m * out[rows]
        mid_ref[rows, :] = mid
        n, _ = norm(mid)
        xg_ref[0, rows, :] = (n * gain + shift).astype(BF16)
        xs[0:PATCH, :] = cot_ref[w].astype(F32)
        g = (m * xs[...]).astype(BF16)
        xg_ref[1, rows, :] = g
        total = total + colsum(g.astype(F32))
    sum_ref[...] = total


def position(ring):
    dp, z = lax.axis_index("dp"), lax.axis_index("mp")
    c = lax.rem(dp, 2)
    if not ring:
        return c, 0, 0, 0, 0
    y, x = lax.div(dp, 4), lax.rem(lax.div(dp, 2), 2)
    return c, jnp.where(c == 0, x, y), y, x, z


def apart(a, b):
    return a ^ b if isinstance(b, int) else jnp.where(b == a, 0, 1)


def slot_of(ring, block, by_block):
    yb, xb, cb = block // 4, (block // 2) % 2, block % 2
    if not ring:
        return block // 4, (block // 2) % 2, block % 2
    c, _, y, x, _ = position(ring)
    over_y, over_x = apart(yb, y), apart(xb, x)
    if by_block:
        return apart(cb, c), *((over_y, over_x) if cb else (over_x, over_y))
    return apart(cb, c), jnp.where(c == 0, over_x, over_y), jnp.where(c == 0, over_y, over_x)


def pack_kernel(ring, up_ref, down_ref, bias_ref, pack_ref):
    c, j, *_ = position(ring)
    off = pl.multiple_of(c * HALF, HALF)

    @pl.when(j == 0)
    def _():
        pack_ref[0:D, :] = up_ref[:, pl.ds(off, HALF)]

    @pl.when(j != 0)
    def _():
        part = down_ref[pl.ds(off, HALF), :]
        pack_ref[0:HALF, :] = part[:, :HALF]
        pack_ref[HALF:D, :] = part[:, HALF:]

    bias = row(bias_ref)
    bias = jnp.where(c == 0, bias[:, :HALF], bias[:, HALF:])
    pack_ref[D : D + 16, :] = jnp.broadcast_to(bias, (16, HALF)).astype(BF16)


def mlp_kernel(ring, spots, own_ref, sib_ref, *refs):
    refs = list(refs)
    rows = own_ref.shape[1]
    blocks = rows // ROWS
    c, j, _, _, z = position(ring)
    initial, final = spots[0] == 0, spots[-1] == 3
    width = len(spots) * HALF
    packs = []
    if initial:
        up_ref, down_ref, upb_ref = refs[:3]
        del refs[:3]
    else:
        acc_in = refs.pop(0)
    for k, spot in enumerate(spots):
        if spot:
            packs.append((k, refs.pop(0), refs.pop(0)))
    dep = refs.pop(0)
    if final:
        mine_ref, theirs_ref = refs[:2]
        acc = acc_in
        del refs[:2]
    else:
        acc = refs.pop(0)
    keep_ref, send_ref, ub_ref, up, down, bias, hid, pre, grads = refs
    if initial:
        off = pl.multiple_of(c * HALF, HALF)
        up[:, 0:HALF] = up_ref[:, pl.ds(off, HALF)]
        down[0:HALF, :] = down_ref[pl.ds(off, HALF), :]
        line = row(upb_ref)
        bias[0:1, 0:HALF] = jnp.where(c == 0, line[:, :HALF], line[:, HALF:])
    for k, mine, other in packs:
        cols = slice(k * HALF, (k + 1) * HALF)
        bias[0:1, cols] = mine[D : D + 16, :].astype(F32)[0:1, :]

        def place(first, second, cols=cols):
            up[:, cols] = first[0:D, :]
            down[cols, 0:HALF] = second[0:HALF, :]
            down[cols, HALF:D] = second[HALF:D, :]

        @pl.when(j == 0)
        def _(place=place, mine=mine, other=other):
            place(mine, other)

        @pl.when(j != 0)
        def _(place=place, mine=mine, other=other):
            place(other, mine)

    up_c, down_c, bias_c = up[...], down[...], bias[0:1, :]
    bias_sum = jnp.zeros((1, width), F32)
    for block in range(2 * blocks):
        source = own_ref if block < blocks else sib_ref
        here = slice((block % blocks) * ROWS, (block % blocks + 1) * ROWS)
        there = slice(block * ROWS, (block + 1) * ROWS)
        x = source[0, here, :]
        g = source[1, here, :]
        u = nn(x, up_c) + bias_c
        phi = 0.5 + 0.5 * lax.erf(u * 0.7071067811865476)
        h = (u * phi).astype(BF16)
        slope = phi + u * jnp.exp(-0.5 * u * u) * 0.3989422804014327
        pg = (nt(g, down_c) * slope).astype(BF16)
        hid[there, :] = h
        pre[there, :] = pg
        bias_sum = bias_sum + colsum(pg.astype(F32))
        out = nn(h, down_c)
        back = nt(pg, up_c)
        if initial:
            acc[0, there, :] = out
            acc[1, there, :] = back
        elif not final:
            acc[0, there, :] = acc_in[0, there, :] + out
            acc[1, there, :] = acc_in[1, there, :] + back
        elif block < blocks:
            mine_ref[0, here, :] = acc[0, there, :] + out
            mine_ref[1, here, :] = acc[1, there, :] + back
        else:
            theirs_ref[0, here, :] = (acc[0, there, :] + out).astype(BF16)
            theirs_ref[1, here, :] = (acc[1, there, :] + back).astype(BF16)
    grads[0] = (tn(own_ref[0], pre[0:rows, :]) + tn(sib_ref[0], pre[rows:, :])).astype(BF16)
    grads[1] = (tn(own_ref[1], hid[0:rows, :]) + tn(sib_ref[1], hid[rows:, :])).astype(BF16)
    ub_ref[...] = jnp.zeros_like(ub_ref)
    for k, spot in enumerate(spots):
        s = lax.rem(z + 4 - spot, 4) if ring else spot
        ub_ref[pl.ds(2 * s + c, 1), :] = bias_sum[:, k * HALF : (k + 1) * HALF]
    for b in range(8):
        cr, first, second = slot_of(ring, b, False)
        lines = slice(b * 96, (b + 1) * 96)

        def move(target, cr=cr, second=second, lines=lines):
            for k in range(len(spots)):
                for which in range(2):
                    target[second, k, which, cr] = grads[which, lines, k * HALF : (k + 1) * HALF]

        either(first, lambda move=move: move(keep_ref), lambda move=move: move(send_ref))


def either(index, zero, one):
    if isinstance(index, int):
        return one() if index else zero()
    pl.when(index == 0)(zero)
    pl.when(index != 0)(one)


def store_blocks(keep_ref, send_ref, ring, index, ref):
    for b in range(8):
        cr, first, second = slot_of(ring, b, True)
        lines = slice(b * 96, (b + 1) * 96)

        def move(target, first=first, second=second, lines=lines):
            target[first, second, index] = ref[lines, :]

        either(cr, lambda move=move: move(keep_ref), lambda move=move: move(send_ref))


def heads_back(p, dout, lower, amount, hot, tab, q, k, v, prob_low, rel):
    none = jnp.zeros_like(dout)
    douts = jnp.concatenate([jnp.where(lower, dout, none), jnp.where(lower, none, dout)], axis=0)
    qs = (q.astype(F32) * 0.125).astype(BF16)
    queries = jnp.concatenate([jnp.where(lower, qs, none), jnp.where(lower, none, qs)], axis=0)
    prob = prob_low.astype(F32)
    dprob = nt(douts, v)
    delta = jnp.sum(prob * dprob, axis=1, keepdims=True)
    dscore = (prob * (dprob - delta)).astype(BF16)
    both = nn(dscore, jnp.concatenate([k, hot], axis=1))
    dq = jnp.where(lower, both[:ROWS, :128], both[ROWS:, :128]) * 0.125
    sums = shift_rows(jnp.where(lower, both[:ROWS, 128:], both[ROWS:, 128:]), amount, False).astype(BF16)
    dq = dq + nn(sums, tab)
    rel[...] += tn(sums, q)
    dk = tn(dscore, queries)
    dv = tn(prob_low, douts)
    return dq, dk, dv


def heads_kernel(ring, w, group, last, dout_ref, qkv_ref, prob_ref, height_ref, width_ref, *refs):
    refs = list(refs)
    rel_in = refs.pop(0) if w or group else None
    before = []
    if last:
        first_ref = refs.pop(0)
        before = [refs.pop(0) for _ in range(w)]
    dep, dqkv, rel = refs[:3]
    table = refs[-1]
    fill_tables(table, height_ref, width_ref)
    tab = table[...].astype(BF16)
    rel[...] = jnp.zeros_like(rel) if rel_in is None else rel_in[...]
    amount = shift_bits()
    hot = one_hot(False)
    lower = iota((ROWS, 128), 1) < 64
    rows = slice(w * ROWS, (w + 1) * ROWS)
    for step in range(PAIRS // 2):
        p = group * (PAIRS // 2) + step
        at = slice(p * 128, (p + 1) * 128)
        q, k, v = (qkv_ref[:, i * D + p * 128 : i * D + (p + 1) * 128] for i in range(3))
        parts = heads_back(p, dout_ref[rows, at], lower, amount, hot, tab, q, k, v, prob_ref[p], rel)
        for which, value in enumerate(parts):
            dqkv[:, which * HALF + step * 128 : which * HALF + (step + 1) * 128] = value.astype(BF16)
    if last:
        keep_ref, send_ref, grad = refs[3:6]
        for which in range(3):
            cols = slice(which * HALF, (which + 1) * HALF)
            total = tn(first_ref[rows, :], dqkv[:, cols])
            for other, ref in enumerate(before):
                total = total + tn(first_ref[other * ROWS : (other + 1) * ROWS, :], ref[:, cols])
            grad[which] = total.astype(BF16)
            store_blocks(keep_ref, send_ref, ring, which, grad.at[which])


def norm_two_kernel(ring, own_ref, sib_ref, mid_ref, cot_ref, mask_ref, att_ref, projw_ref, gain_ref, downb_ref,
                    dep, out_ref, midg_ref, dout_ref, keep_ref, send_ref, sum_ref, xs, low, both):
    windows = cot_ref.shape[0]
    gain, down_bias = row(gain_ref), row(downb_ref)
    xs[ROWS - 16 :, :] = jnp.zeros((16, D), F32)
    gain_sum = jnp.zeros((1, D), F32)
    shift_sum = jnp.zeros((1, D), F32)
    proj_sum = jnp.zeros((1, D), F32)
    for w in range(windows):
        rows = slice(w * ROWS, (w + 1) * ROWS)
        m = column_mask(mask_ref, w)
        mid = mid_ref[rows, :]
        mlp_out = own_ref[0, rows, :] + sib_ref[0, rows, :].astype(F32)
        out = mid + m * (mlp_out + down_bias)
        out_ref[w] = out[0:PATCH].astype(BF16)
        n, s = norm(mid)
        e = own_ref[1, rows, :] + sib_ref[1, rows, :].astype(F32)
        gain_sum = gain_sum + colsum(e * n)
        shift_sum = shift_sum + colsum(e)
        xs[0:PATCH, :] = cot_ref[w].astype(F32)
        grad = xs[...] + norm_back(e, n, s, gain)
        midg_ref[rows, :] = grad
        attn = (m * grad).astype(BF16)
        low[rows, :] = attn
        proj_sum = proj_sum + colsum(attn.astype(F32))
    sum_ref[...] = jnp.zeros_like(sum_ref)
    sum_ref[0:1, :] = gain_sum
    sum_ref[1:2, :] = shift_sum
    sum_ref[2:3, :] = proj_sum
    proj_grad = tn(att_ref[...], low[...])
    for half in range(2):
        both[half] = proj_grad[:, half * HALF : (half + 1) * HALF].astype(BF16)
        store_blocks(keep_ref, send_ref, ring, half, both.at[half])
    dout_ref[...] = nt(low[...], projw_ref[...]).astype(BF16)


def norm_one_kernel(tok_ref, midg_ref, *refs):
    windows = tok_ref.shape[0]
    dqkv, refs = refs[: 2 * windows], refs[2 * windows :]
    w_ref, gain_ref, down_sum_ref, ub0_ref, ub1_ref, ub2_ref, sum_ref, rel_ref, dep, tokg_ref, small_ref, xs = refs
    gain = row(gain_ref)
    xs[ROWS - 16 :, :] = jnp.zeros((16, D), F32)
    gain_sum = jnp.zeros((1, D), F32)
    shift_sum = jnp.zeros((1, D), F32)
    sums = [jnp.zeros((1, HALF), F32) for _ in range(4)]
    for w in range(windows):
        rows = slice(w * ROWS, (w + 1) * ROWS)
        e = jnp.zeros((ROWS, D), F32)
        for group in range(2):
            grad = dqkv[group * windows + w]
            for which in range(3):
                cols = slice(which * HALF, (which + 1) * HALF)
                at = which * D + group * HALF
                e = e + nt(grad[:, cols], w_ref[:, at : at + HALF])
                if which != 1:
                    sums[which + group] = sums[which + group] + colsum(grad[:, cols].astype(F32))
        xs[0:PATCH, :] = tok_ref[w].astype(F32)
        n, s = norm(xs[...])
        gain_sum = gain_sum + colsum(e * n)
        shift_sum = shift_sum + colsum(e)
        tokg_ref[w] = (midg_ref[rows, :] + norm_back(e, n, s, gain))[0:PATCH]

    small_ref[...] = jnp.zeros_like(small_ref)

    def put(at, value):
        small_ref[at : at + 1, :] = value[:, :HALF]
        small_ref[at + 1 : at + 2, :] = value[:, HALF:]

    put(0, down_sum_ref[...])
    small_ref[2:10, :] = ub0_ref[...] + ub1_ref[...] + ub2_ref[...]
    for i in range(3):
        put(10 + 2 * i, sum_ref[i : i + 1, :])
    for i in range(4):
        small_ref[16 + i : 17 + i, :] = sums[i]
    put(20, gain_sum)
    put(22, shift_sum)
    both = rel_ref[...]
    heads = both[0:64, 0:64] + both[64:128, 64:128]
    small_ref[24:40, 0:256] = jnp.concatenate([heads[0:16], heads[16:32], heads[32:48], heads[48:64]], axis=1)


def finish_kernel(own_ref, got_ref, tail_ref, early_ref, qkv_ref, *refs):
    n1g, n1s, qvb, relh, relw, pb, n2g, n2s, upb, db, small = refs
    for which in range(3):
        lines = slice(which * 96, (which + 1) * 96)
        total = own_ref[lines, :].astype(F32) + got_ref[lines, :].astype(F32)
        qkv_ref[:, which * D : which * D + HALF] = early_ref[2 + which].astype(F32)
        qkv_ref[:, which * D + HALF : (which + 1) * D] = total
    low, high = slice(0, SMALL_ROWS), slice(SMALL_ROWS, 2 * SMALL_ROWS)
    got = got_ref[3 * 96 :, :]
    small[...] = (tail_ref[low, :].astype(F32) + tail_ref[high, :].astype(F32)) + (got[low, :].astype(F32) + got[high, :].astype(F32))
    for ref, at, count in ((db, 0, 2), (upb, 2, 8), (n2g, 10, 2), (n2s, 12, 2), (pb, 14, 2), (qvb, 16, 4), (n1g, 20, 2), (n1s, 22, 2)):
        for i in range(count):
            ref[i * HALF : (i + 1) * HALF] = small[at + i : at + i + 1, :].reshape(HALF)
    rels = 2 * WIN - 1
    block = small[24:40, 0:256]
    for ref, at in ((relh, 0), (relw, 128)):
        ref[0:16, :] = block[:, at : at + 64]
        ref[16:rels, :] = block[0 : rels - 16, at + 64 : at + 128]


ANY = pl.BlockSpec(memory_space=pl.ANY)


def call(kernel, outs, ins, scratch=(), us=1.0, after=None, limit=20, aliases=None):
    shapes = tuple(jax.ShapeDtypeStruct(s, d) for s, d in outs)
    moved = sum(x.size * x.dtype.itemsize for x in ins) + sum(jnp.dtype(d).itemsize * functools.reduce(lambda a, b: a * b, s, 1) for s, d in outs)
    specs = [VM] * len(ins)
    if after is not None:
        ins, specs = [*ins, after], [*specs, ANY]
    return pl.pallas_call(
        kernel,
        out_shape=shapes,
        in_specs=specs,
        out_specs=tuple(VM for _ in outs),
        scratch_shapes=list(scratch),
        input_output_aliases=aliases or {},
        compiler_params=pltpu.CompilerParams(vmem_limit_bytes=limit * 2**20),
        cost_estimate=pl.CostEstimate(flops=int(us * 1.15e9), bytes_accessed=moved, transcendentals=0),
    )(*ins)


def add_low(a, b):
    return (a.astype(F32) + b.astype(F32)).astype(BF16)


def split(x):
    coarse = lax.reduce_precision(x, 8, 7)
    return jnp.concatenate([coarse, x - coarse], axis=0).astype(BF16)


def join(x):
    half = x.shape[0] // 2
    return x[:half].astype(F32) + x[half:].astype(F32)


def tie(*arrays):
    return lax.optimization_barrier(arrays)


def local(tokens, window_mask, out_grad, norm1_gain, norm1_shift, qkv_weight, qv_bias, rel_height, rel_width, proj_weight, proj_bias,
          norm2_gain, norm2_shift, up_weight, up_bias, down_weight, down_bias):
    dpn, mpn = lax.axis_size("dp"), lax.axis_size("mp")
    c = lax.axis_index("dp") % 2
    windows = tokens.shape[0]
    rows = windows * ROWS
    ring = dpn == 8 and mpn == 4

    def send(x, move):
        perm = []
        for d in range(dpn):
            for m in range(mpn):
                nd, nm = move(d, m)
                perm.append((d * mpn + m, nd * mpn + nm))
        return lax.ppermute(x, AXES, perm)

    core = lambda d, m: (d ^ 1, m)
    first = lambda d, m: (d ^ (4 if d & 1 else 2), m)
    second = lambda d, m: (d ^ (2 if d & 1 else 4), m)
    up_ring = lambda d, m: (d, (m + 1) % mpn)
    down_ring = lambda d, m: (d, (m + mpn - 1) % mpn)
    near = lambda d, m: (d, m ^ 1)
    far = lambda d, m: (d, m ^ 2)
    hold = tie if ring else lambda *arrays: arrays
    narrow = pltpu.VMEM((ROWS, D), F32)
    square = pltpu.VMEM((128, 128), F32)

    def make_qkv():
        outs = [((rows, D), BF16)] + [((ROWS, 3 * D), BF16)] * windows
        res = call(qkv_kernel, outs, [tokens, norm1_gain, norm1_shift, qkv_weight, qv_bias], [narrow], us=4.5)
        return res[0], res[1:]

    def attend(w, part, after):
        outs = [((PAIRS, 2 * ROWS, ROWS), BF16), ((ROWS, D), BF16)]
        return call(functools.partial(attend_kernel, w), outs, [window_mask, part, rel_height, rel_width], [square], us=8.0, after=after)

    def project(atts):
        outs = [((rows, D), F32), ((2, rows, D), BF16), ((1, D), F32), ((rows, D), BF16)]
        ins = [tokens, window_mask, out_grad, proj_weight, proj_bias, norm2_gain, norm2_shift, *atts]
        return call(project_kernel, outs, ins, [narrow], us=3.5)

    def mlp(spots, xg, xg_sib, acc, packs, after):
        n, final = len(spots), spots[-1] == 3
        wide = ((2, n, 2, 2, 96, HALF), BF16)
        outs = [((2, rows, D), F32), ((2, rows, D), BF16)] if final else [((2, 2 * rows, D), F32)]
        outs += [wide, wide, ((8, HALF), F32)]
        scratch = [pltpu.VMEM((D, n * HALF), BF16), pltpu.VMEM((n * HALF, D), BF16), pltpu.VMEM((8, n * HALF), F32),
                   pltpu.VMEM((2 * rows, n * HALF), BF16), pltpu.VMEM((2 * rows, n * HALF), BF16), pltpu.VMEM((2, D, n * HALF), BF16)]
        ins = [xg, xg_sib, *acc, *packs]
        aliases = {2: 0} if spots[0] and not final else None
        return call(functools.partial(mlp_kernel, ring, spots), outs, ins, scratch, us=6.0 * n, after=after, limit=30, aliases=aliases)

    def norm_two(mine, sib, mid, att, after):
        half = ((2, 2, 2, 96, HALF), BF16)
        outs = [((windows, PATCH, D), BF16), ((rows, D), F32), ((rows, D), BF16), half, half, ((8, D), F32)]
        ins = [mine, sib, mid, out_grad, window_mask, att, proj_weight, norm2_gain, down_bias]
        scratch = [narrow, pltpu.VMEM((rows, D), BF16), pltpu.VMEM((2, D, HALF), BF16)]
        return call(functools.partial(norm_two_kernel, ring), outs, ins, scratch, us=5.0, after=after)

    def heads(group, w, dout, rel, before, after):
        last = w == windows - 1
        half = ((2, 2, 3, 96, HALF), BF16)
        outs = [((ROWS, 3 * HALF), BF16), ((128, 128), F32)] + ([half, half] if last else [])
        ins = [dout, qkvs[w], probs[w], rel_height, rel_width] + ([rel] if w or group else []) + ([first_low, *before] if last else [])
        scratch = ([pltpu.VMEM((3, D, HALF), BF16)] if last else []) + [square]
        return call(functools.partial(heads_kernel, ring, w, group, last), outs, ins, scratch, us=6.5 if last else 4.5, after=after)

    def norm_one(mid_grad, dqkv, ubs, down_sum, sums, rel, after):
        outs = [((windows, PATCH, D), F32), ((SMALL_ROWS, HALF), F32)]
        ins = [tokens, mid_grad, *dqkv, qkv_weight, norm1_gain, down_sum, *ubs, sums, rel]
        return call(norm_one_kernel, outs, ins, [narrow], us=6.0, after=after)

    if not ring:
        up_all = lax.all_gather(up_weight, "mp", axis=1, tiled=True)
        down_all = lax.all_gather(down_weight, "mp", axis=0, tiled=True)
        bias_all = lax.all_gather(up_bias, "mp", axis=0, tiled=True)
        packs = [up_all[:, :D], down_all[:D], bias_all[:D]]
        for k in range(1, 4):
            off = k * D + c * HALF
            u_part = lax.dynamic_slice(up_all, (0, off), (D, HALF))
            d_part = lax.dynamic_slice(down_all, (off, 0), (HALF, D))
            d_part = jnp.concatenate([d_part[:, :HALF], d_part[:, HALF:]], axis=0)
            b_part = jnp.broadcast_to(lax.dynamic_slice(bias_all, (off,), (HALF,))[None], (16, HALF))
            packs += [jnp.concatenate([u_part, b_part], axis=0), jnp.concatenate([d_part, b_part], axis=0)]
        first_low, qkvs = make_qkv()
        probs, atts = zip(*[attend(w, qkvs[w], first_low) for w in range(windows)])
        mid, xg, down_sum, att = project(atts)
        xg_sib = send(xg, core)
        acc, keep0, send0, ub0 = mlp((0, 1), xg, xg_sib, [], packs[0:5], mid)
        acc, keep1, send1, ub1 = mlp((2,), xg, xg_sib, [acc], packs[5:7], mid)
        mine, theirs, keep2, send2, ub2 = mlp((3,), xg, xg_sib, [acc], packs[7:9], mid)
        block_out, mid_grad, dout, keepp, sendp, sums = norm_two(mine, send(theirs, core), mid, att, mid)
        dqkv, kept, sent, rel = [], [keepp], [sendp], None
        for group in range(2):
            for w in range(windows):
                part, rel, *weights = heads(group, w, dout, rel, dqkv[group * windows :], mid_grad)
                dqkv.append(part)
            kept.append(weights[0])
            sent.append(weights[1])
        tokens_grad, small = norm_one(mid_grad, dqkv, (ub0, ub1, ub2), down_sum, sums, rel, mid_grad)
        dw = jnp.stack([jnp.concatenate([keep0, keep1, keep2], axis=1), jnp.concatenate([send0, send1, send2], axis=1)])
        halves = dw.transpose(4, 0, 1, 5, 3, 2, 6).reshape(D, 2, 4, HALF)
        full = jnp.zeros((D, 2, 4, 2, HALF), BF16)
        full = lax.dynamic_update_slice(full, halves[:, :, :, None], (0, 0, 0, c, 0)).reshape(D, 2, 4 * D)
        full = lax.psum_scatter(full, "dp", scatter_dimension=0, tiled=True)
        full = lax.psum_scatter(full, "mp", scatter_dimension=2, tiled=True).astype(F32)
        up_grad, down_grad = full[:, 0], full[:, 1].T
        weights = jnp.stack([jnp.concatenate(kept, axis=2), jnp.concatenate(sent, axis=2)])
        weights = weights.transpose(0, 1, 2, 4, 3, 5).reshape(D, 8 * HALF)
        weights = lax.psum(weights, "mp")
        weights = lax.psum_scatter(weights, "dp", scatter_dimension=0, tiled=True).astype(F32)
        parts = [weights[:, i * HALF : (i + 1) * HALF] for i in range(8)]
        proj_grad = jnp.concatenate(parts[0:2], axis=1)
        qkv_grad = jnp.concatenate([parts[2], parts[5], parts[3], parts[6], parts[4], parts[7]], axis=1)
        small = lax.psum(small, AXES)
        vec = lambda start, count: small[start : start + count].reshape(count * HALF)
        table = small[24:40, 0:256].reshape(16, 4, 64).transpose(1, 0, 2).reshape(64, 64)
        rels = 2 * WIN - 1
        return (
            block_out, tokens_grad, vec(20, 2), vec(22, 2), qkv_grad, vec(16, 4), table[0:rels], table[32 : 32 + rels], proj_grad,
            vec(14, 2), vec(10, 2), vec(12, 2), up_grad, vec(2, 8), down_grad, vec(0, 2),
        )

    (pack,) = call(functools.partial(pack_kernel, ring), [((D + 16, HALF), BF16)], [up_weight, down_weight, up_bias])
    m1 = send(pack, up_ring)
    first_low, qkvs = make_qkv()
    prob0, att0 = attend(0, qkvs[0], pack)
    m1, att0 = tie(m1, att0)

    m2 = send(m1, up_ring)
    o1 = send(m1, first)
    probs, atts = [prob0], [att0]
    for w in range(1, windows):
        prob, att = attend(w, qkvs[w], m1)
        probs.append(prob)
        atts.append(att)
    mid, xg, down_sum, att = project(atts)
    m2, o1, xg = tie(m2, o1, xg)

    m3 = send(m2, up_ring)
    o2 = send(m2, first)
    xg_sib = send(xg, core)
    acc, keep0, send0, ub0 = mlp((0, 1), xg, xg_sib, [], [up_weight, down_weight, up_bias, m1, o1], m2)
    m3, o2, acc, send0 = tie(m3, o2, acc, send0)

    o3 = send(m3, first)
    a1 = send(send0, first)
    acc, keep1, send1, ub1 = mlp((2,), xg, xg_sib, [acc], [m2, o2], m3)
    o3, acc = tie(o3, acc)

    mine, theirs, keep2, send2, ub2 = mlp((3,), xg, xg_sib, [acc], [m3, o3], o3)
    a1, theirs, send1, send2 = tie(a1, theirs, send1, send2)

    mlp_sib = send(theirs, core)
    a_keep, a_send = add_low(keep0[0], a1[0]), add_low(keep0[1], a1[1])
    a2 = send(a_send, second)
    b1 = send(jnp.concatenate([send1, send2], axis=1), first)
    block_out, mid_grad, dout, keepp, sendp, sums = norm_two(mine, mlp_sib, mid, att, a1)
    a2, dout, sendp = tie(a2, dout, sendp)

    a_part = add_low(a_keep, a2)
    got1 = send(a_part[1], down_ring)
    gotp = send(sendp, core)
    part, rel = heads(0, 0, dout, None, [], a2)
    dqkv = [part]
    b1, got1, gotp, rel = tie(b1, got1, gotp, rel)

    keep_b = jnp.concatenate([keep1, keep2], axis=1)
    b_keep, b_send = add_low(keep_b[0], b1[0]), add_low(keep_b[1], b1[1])
    b2 = send(b_send, second)
    for w in range(1, windows):
        part, rel, *weights = heads(0, w, dout, rel, dqkv, b1)
        dqkv.append(part)
    keepq, sendq = weights
    b2, rel, sendq = tie(b2, rel, sendq)

    b_part = add_low(b_keep, b2)
    got2 = send(b_part[0], far)
    got3 = send(b_part[1], up_ring)
    gotq = send(sendq, core)
    part, rel = heads(1, 0, dout, rel, [], b2)
    dqkv.append(part)
    gotq, rel, got3 = tie(gotq, rel, got3)

    flat = lambda x: x.reshape(-1, HALF)
    keep = jnp.concatenate([add_low(keepp, gotp), add_low(keepq, gotq)], axis=2)
    q1 = send(keep[1], first)
    for w in range(1, windows):
        part, rel, *weights = heads(1, w, dout, rel, dqkv[windows:], gotq)
        dqkv.append(part)
    keepr, sendr = weights
    q1, rel, sendr, got2 = tie(q1, rel, sendr, got2)

    gotr = send(sendr, core)
    q_keep = add_low(keep[0], q1)
    q2 = send(q_keep[1], second)
    mlp_part = add_low(a_part[0].astype(F32) + got1.astype(F32), got2.astype(F32) + got3.astype(F32))
    other = send(mlp_part[:, 1], core)
    tokens_grad, small = norm_one(mid_grad, dqkv, (ub0, ub1, ub2), down_sum, sums, rel, q1)
    q2, gotr, small = tie(q2, gotr, small)

    kept = mlp_part[:, 0]
    mlp_grads = jnp.where(c == 0, jnp.concatenate([kept, other], axis=2), jnp.concatenate([other, kept], axis=2)).astype(F32)
    q_part = add_low(q_keep[0], q2)
    tail = split(small)
    r_keep = add_low(keepr, gotr)
    tail = split(join(tail) + join(send(tail, core)))
    q3 = send(q_part, near)
    r1 = send(jnp.concatenate([flat(r_keep[1]), tail], axis=0), first)
    size = r1.shape[0] - 2 * SMALL_ROWS
    r_keep = add_low(flat(r_keep[0]), r1[:size])
    tail = split(join(tail) + join(r1[size:]))
    size //= 2
    r2 = send(jnp.concatenate([r_keep[size:], tail], axis=0), second)
    r_keep = add_low(r_keep[:size], r2[:size])
    tail = split(join(tail) + join(r2[size:]))
    q_part = add_low(q_part, q3)
    q4 = send(q_part, far)
    r3 = send(jnp.concatenate([r_keep, tail], axis=0), near)
    r_keep = add_low(r_keep, r3[:size])
    tail = split(join(tail) + join(r3[size:]))
    r4 = send(jnp.concatenate([r_keep, tail], axis=0), far)
    q_part = q_part.astype(F32) + q4.astype(F32)
    proj_grad = jnp.concatenate([q_part[0], q_part[1]], axis=1)
    vec = lambda n: ((n,), F32)
    table = ((2 * WIN - 1, 64), F32)
    outs = [((96, 3 * D), F32), vec(D), vec(D), vec(2 * D), table, table, vec(D), vec(D), vec(D), vec(4 * D), vec(D)]
    qkv_grad, n1g, n1s, qvb, relh, relw, pb, n2g, n2s, upb, db = call(
        finish_kernel, outs, [r_keep, r4, tail, q_part], [pltpu.VMEM((SMALL_ROWS, HALF), F32)], us=2.0)
    return block_out, tokens_grad, n1g, n1s, qkv_grad, qvb, relh, relw, proj_grad, pb, n2g, n2s, mlp_grads[0], upb, mlp_grads[1].T, db


def solution(mesh):
    split_rows = P(AXES, None, None)
    in_specs = (split_rows, P(AXES, None), split_rows) + (P(),) * 10 + (P(None, "mp"), P("mp"), P("mp", None), P())
    out_specs = (split_rows, split_rows, P(), P(), P("dp", None), P(), P(), P(), P("dp", None), P(), P(), P(), P("dp", "mp"), P(), P("mp", "dp"), P())
    return jax.shard_map(local, mesh=mesh, in_specs=in_specs, out_specs=out_specs, check_vma=False)
```

```python
import functools

import jax
import jax.numpy as jnp
from jax import lax
from jax.experimental import pallas as pl
from jax.experimental.pallas import tpu as pltpu
from jax.sharding import PartitionSpec as P

D = 768
HEADS = 12
WIN = 14
PATCH = WIN * WIN
ROWS = 208
PAIRS = HEADS // 2
EPSILON = 1e-06
HALF = 384
F32 = jnp.float32
BF16 = jnp.bfloat16
AXES = ("dp", "mp")
VM = pl.BlockSpec(memory_space=pltpu.VMEM)
SMALL_ROWS = 40


def nn(a, b):
    return lax.dot_general(a, b, (((1,), (0,)), ((), ())), preferred_element_type=F32)


def nt(a, b):
    return lax.dot_general(a, b, (((1,), (1,)), ((), ())), preferred_element_type=F32)


def tn(a, b):
    return lax.dot_general(a, b, (((0,), (0,)), ((), ())), preferred_element_type=F32)


def iota(shape, dim):
    return lax.broadcasted_iota(jnp.int32, shape, dim)


def row(ref):
    return ref[...].astype(F32).reshape(1, -1)


def column_mask(mask_ref, w):
    line = mask_ref[w : w + 1, :].astype(F32)
    here = iota((ROWS, PATCH), 0) == iota((ROWS, PATCH), 1)
    return jnp.sum(jnp.where(here, line, 0.0), axis=1, keepdims=True)


def key_mask(column):
    here = iota((ROWS, ROWS), 0) == iota((ROWS, ROWS), 1)
    return jnp.sum(jnp.where(here, column, 0.0), axis=0, keepdims=True)


def norm(x):
    average = jnp.mean(x, axis=-1, keepdims=True)
    centred = x - average
    variance = jnp.mean(centred * centred, axis=-1, keepdims=True)
    inverse = lax.rsqrt(variance + EPSILON)
    return centred * inverse, inverse


def norm_back(e, n, s, gain):
    scaled = e * gain
    mean_grad = jnp.mean(scaled, axis=-1, keepdims=True)
    mean_proj = jnp.mean(scaled * n, axis=-1, keepdims=True)
    return s * (scaled - mean_grad - n * mean_proj)


def colsum(x):
    return jnp.sum(x, axis=0, keepdims=True)


def fill_tables(table, height_ref, width_ref):
    table[...] = jnp.zeros((128, 128), F32)
    height = height_ref[...].astype(F32)
    width = width_ref[...].astype(F32)
    none = jnp.zeros_like(height)
    rels = 2 * WIN - 1
    table[0:rels, :] = jnp.concatenate([height, none], axis=1)
    table[32 : 32 + rels, :] = jnp.concatenate([width, none], axis=1)
    table[64 : 64 + rels, :] = jnp.concatenate([none, height], axis=1)
    table[96 : 96 + rels, :] = jnp.concatenate([none, width], axis=1)


def shift_bits():
    place = iota((ROWS, 128), 0)
    high = place // WIN
    wide = place - high * WIN
    return jnp.where((iota((ROWS, 128), 1) & 32) == 0, high, wide)


def shift_rows(x, amount, left):
    for bit in range(4):
        step = 1 << bit
        moved = pltpu.roll(x, 128 - step if left else step, 1)
        x = jnp.where((amount & step) != 0, moved, x)
    return x


def one_hot(both):
    place = iota((ROWS, 128), 0)
    lane = iota((ROWS, 128), 1)
    high = place // WIN
    wide = place - high * WIN
    want = jnp.where((lane & 32) == 0, high, wide)
    sub = lane & 31
    slot = (sub & 15) if both else sub
    hit = (slot == (WIN - 1) - want) & (place < PATCH)
    return jnp.where(hit, 1.0, 0.0).astype(BF16)


def qkv_kernel(tok_ref, mask_ref, cot_ref, gain_ref, shift_ref, w_ref, bias_ref, dep, first_ref, sum_ref, *refs):
    windows = tok_ref.shape[0]
    outs, gs, xs = refs[:windows], refs[windows:-1], refs[-1]
    sums = jnp.zeros((1, D), F32)
    gain, shift = row(gain_ref), row(shift_ref)
    xs[ROWS - 16 :, :] = jnp.zeros((16, D), F32)
    for w in range(windows):
        xs[0:PATCH, :] = tok_ref[w].astype(F32)
        n, _ = norm(xs[...])
        first_ref[w * ROWS : (w + 1) * ROWS, :] = (n * gain + shift).astype(BF16)
        xs[0:PATCH, :] = cot_ref[w].astype(F32)
        g = (column_mask(mask_ref, w) * xs[...]).astype(BF16)
        gs[w][...] = g
        sums = sums + colsum(g.astype(F32))
    sum_ref[...] = sums
    bias = row(bias_ref)
    for part in range(3):
        cols = slice(part * D, (part + 1) * D)
        out = nn(first_ref[...], w_ref[:, cols])
        if part == 0:
            out = out + bias[:, :D]
        if part == 2:
            out = out + bias[:, D:]
        for w in range(windows):
            outs[w][:, cols] = out[w * ROWS : (w + 1) * ROWS].astype(BF16)


def attend_kernel(w, mask_ref, qkv_ref, height_ref, width_ref, dep, prob_ref, att_ref, table):
    fill_tables(table, height_ref, width_ref)
    tab = table[...].astype(BF16)
    amount = shift_bits()
    keys_hot = one_hot(True)
    lane = iota((ROWS, 128), 1)
    lower = lane < 64
    sub = lane & 31
    valid = key_mask(column_mask(mask_ref, w)) > 0.5

    def pair(p, carry):
        at = pl.multiple_of(p * 128, 128)
        q = qkv_ref[:, pl.ds(at, 128)]
        k = qkv_ref[:, pl.ds(D + at, 128)]
        v = qkv_ref[:, pl.ds(2 * D + at, 128)]
        terms = shift_rows(nt(q, tab), amount, True)
        coarse = terms.astype(BF16).astype(F32)
        fine = pltpu.roll(terms - coarse, 16, 1)
        terms = jnp.where(sub < WIN, coarse, jnp.where((sub >= 16) & (sub < 16 + WIN), fine, 0.0))
        qs = q.astype(F32) * 0.125
        top = jnp.concatenate([jnp.where(lower, qs, 0.0), jnp.where(lower, terms, 0.0)], axis=1)
        bottom = jnp.concatenate([jnp.where(lower, 0.0, qs), jnp.where(lower, 0.0, terms)], axis=1)
        left = jnp.concatenate([top, bottom], axis=0).astype(BF16)
        right = jnp.concatenate([k, keys_hot], axis=1)
        scores = jnp.where(valid, nt(left, right), -1000000000.0)
        most = jnp.max(scores, axis=1, keepdims=True)
        weight = jnp.exp(scores - most)
        total = jnp.sum(weight, axis=1, keepdims=True)
        prob = (weight * (1.0 / total)).astype(BF16)
        prob_ref[p] = prob
        out = nn(prob, v)
        att_ref[:, pl.ds(at, 128)] = jnp.where(lower, out[:ROWS], out[ROWS:]).astype(BF16)
        return carry

    lax.fori_loop(0, PAIRS, pair, 0, unroll=2)


def project_kernel(tok_ref, mask_ref, w_ref, bias_ref, gain_ref, shift_ref, *refs):
    windows = tok_ref.shape[0]
    atts, lows = refs[:windows], refs[windows : 2 * windows]
    mid_ref, all_ref, xs = refs[2 * windows :]
    gain, shift, bias = row(gain_ref), row(shift_ref), row(bias_ref)
    xs[ROWS - 16 :, :] = jnp.zeros((16, D), F32)
    for w in range(windows):
        all_ref[w * ROWS : (w + 1) * ROWS, :] = atts[w][...]
    out = nn(all_ref[...], w_ref[...]) + bias
    for w in range(windows):
        rows = slice(w * ROWS, (w + 1) * ROWS)
        xs[0:PATCH, :] = tok_ref[w].astype(F32)
        mid = xs[...] + column_mask(mask_ref, w) * out[rows]
        mid_ref[rows, :] = mid
        n, _ = norm(mid)
        lows[w][...] = (n * gain + shift).astype(BF16)


def position(ring):
    dp, z = lax.axis_index("dp"), lax.axis_index("mp")
    c = lax.rem(dp, 2)
    if not ring:
        return c, 0, 0, 0, 0
    y, x = lax.div(dp, 4), lax.rem(lax.div(dp, 2), 2)
    return c, jnp.where(c == 0, x, y), y, x, z


def apart(a, b):
    return a ^ b if isinstance(b, int) else jnp.where(b == a, 0, 1)


def slot_of(ring, block, by_block):
    yb, xb, cb = block // 4, (block // 2) % 2, block % 2
    if not ring:
        return block // 4, (block // 2) % 2, block % 2
    c, _, y, x, _ = position(ring)
    over_y, over_x = apart(yb, y), apart(xb, x)
    if by_block:
        return apart(cb, c), *((over_y, over_x) if cb else (over_x, over_y))
    return apart(cb, c), jnp.where(c == 0, over_x, over_y), jnp.where(c == 0, over_y, over_x)


def pack_kernel(ring, up_ref, down_ref, bias_ref, pack_ref, again_ref, sems):
    c, j, *_ = position(ring)
    off = pl.multiple_of(c * HALF, HALF)
    ups, downs = [], []
    for i, ref in enumerate((pack_ref, again_ref)):
        ups.append(pltpu.make_async_copy(up_ref.at[:, pl.ds(off, HALF)], ref.at[0:D], sems.at[3 * i]))
        for half in range(2):
            cols = slice(half * HALF, (half + 1) * HALF)
            downs.append(pltpu.make_async_copy(down_ref.at[pl.ds(off, HALF), cols], ref.at[cols], sems.at[3 * i + 1 + half]))

    def each(copies, start):
        for copy in copies:
            copy.start() if start else copy.wait()

    either(j, lambda: each(ups, True), lambda: each(downs, True))
    bias = row(bias_ref)
    bias = jnp.where(c == 0, bias[:, :HALF], bias[:, HALF:])
    for ref in (pack_ref, again_ref):
        ref[D:, :] = jnp.broadcast_to(bias, (ref.shape[0] - D, HALF)).astype(BF16)
    either(j, lambda: each(ups, False), lambda: each(downs, False))


def mlp_kernel(ring, spots, windows, *refs):
    refs = list(refs)
    blocks = 2 * windows
    grefs = [refs.pop(0) for _ in range(blocks)]
    xrefs = [refs.pop(0) for _ in range(blocks)]
    c, j, _, _, z = position(ring)
    initial, final = spots[0] == 0, spots[-1] == 2
    width = len(spots) * HALF
    packs = []
    if initial:
        up_ref, down_ref, upb_ref = refs[:3]
        del refs[:3]
    else:
        acc_in = refs.pop(0)
    for k, spot in enumerate(spots):
        if spot:
            packs.append((k, refs.pop(0), refs.pop(0)))
    dep = refs.pop(0)
    if final:
        mine_ref, tout_ref, tback_ref = refs[:3]
        acc = acc_in
        del refs[:3]
    else:
        acc = refs.pop(0)
    outs = [(refs.pop(0),) if spot == 3 else (refs.pop(0), refs.pop(0)) for spot in spots]
    ub_ref, up, down, bias, hid, pre, grads = refs
    if initial:
        off = pl.multiple_of(c * HALF, HALF)
        up[:, 0:HALF] = up_ref[:, pl.ds(off, HALF)]
        down[0:HALF, :] = down_ref[pl.ds(off, HALF), :]
        line = row(upb_ref)
        bias[0:1, 0:HALF] = jnp.where(c == 0, line[:, :HALF], line[:, HALF:])
    for k, mine, other in packs:
        cols = slice(k * HALF, (k + 1) * HALF)
        bias[0:1, cols] = mine[D : D + 16, :].astype(F32)[0:1, :]

        def place(first, second, cols=cols):
            up[:, cols] = first[0:D, :]
            down[cols, 0:HALF] = second[0:HALF, :]
            down[cols, HALF:D] = second[HALF:D, :]

        @pl.when(j == 0)
        def _(place=place, mine=mine, other=other):
            place(mine, other)

        @pl.when(j != 0)
        def _(place=place, mine=mine, other=other):
            place(other, mine)

    up_c, down_c, bias_c = up[...], down[...], bias[0:1, :]
    bias_sum = jnp.zeros((1, width), F32)
    for block in range(blocks):
        here = slice((block % windows) * ROWS, (block % windows + 1) * ROWS)
        there = slice(block * ROWS, (block + 1) * ROWS)
        x = xrefs[block][...]
        g = grefs[block][...]
        u = nn(x, up_c) + bias_c
        phi = 0.5 + 0.5 * lax.erf(u * 0.7071067811865476)
        h = (u * phi).astype(BF16)
        slope = phi + u * jnp.exp(-0.5 * u * u) * 0.3989422804014327
        pg = (nt(g, down_c) * slope).astype(BF16)
        hid[there, :] = h
        pre[there, :] = pg
        bias_sum = bias_sum + colsum(pg.astype(F32))
        out = nn(h, down_c)
        back = nt(pg, up_c)
        if initial:
            acc[0, there, :] = out
            acc[1, there, :] = back
        elif not final:
            acc[0, there, :] = acc_in[0, there, :] + out
            acc[1, there, :] = acc_in[1, there, :] + back
        elif block < windows:
            mine_ref[0, here, :] = acc[0, there, :] + out
            mine_ref[1, here, :] = acc[1, there, :] + back
        else:
            tout_ref[here, :] = (acc[0, there, :] + out).astype(BF16)
            tback_ref[here, :] = (acc[1, there, :] + back).astype(BF16)
    for which, (left, right) in enumerate(((xrefs, pre), (grefs, hid))):
        total = jnp.zeros((D, width), F32)
        for block in range(blocks):
            total = total + tn(left[block][...], right[block * ROWS : (block + 1) * ROWS, :])
        grads[which] = total.astype(BF16)
    ub_ref[...] = jnp.zeros_like(ub_ref)
    for k, spot in enumerate(spots):
        s = lax.rem(z + 4 - spot, 4) if ring else spot
        ub_ref[pl.ds(2 * s + c, 1), :] = bias_sum[:, k * HALF : (k + 1) * HALF]
    for b in range(8):
        cr, first, second = slot_of(ring, b, False)
        lines = slice(b * 96, (b + 1) * 96)

        for k in range(len(spots)):
            part = slice(k * HALF, (k + 1) * HALF)

            def move(target, cr=cr, second=second, lines=lines, part=part):
                for which in range(2):
                    target[second, which, cr] = grads[which, lines, part]

            if len(outs[k]) == 1:
                move(outs[k][0].at[first])
            else:
                either(first, lambda k=k, move=move: move(outs[k][0]), lambda k=k, move=move: move(outs[k][1]))


def either(index, zero, one):
    if isinstance(index, int):
        return one() if index else zero()
    pl.when(index == 0)(zero)
    pl.when(index != 0)(one)


def store_blocks(keep_ref, send_ref, ring, index, ref):
    for b in range(8):
        cr, first, second = slot_of(ring, b, True)
        lines = slice(b * 96, (b + 1) * 96)

        def move(target, first=first, second=second, lines=lines):
            target[first, second, index] = ref[lines, :]

        either(cr, lambda move=move: move(keep_ref), lambda move=move: move(send_ref))


def heads_back(p, dout, lower, amount, hot, tab, q, k, v, prob_low, rel):
    none = jnp.zeros_like(dout)
    douts = jnp.concatenate([jnp.where(lower, dout, none), jnp.where(lower, none, dout)], axis=0)
    qs = (q.astype(F32) * 0.125).astype(BF16)
    queries = jnp.concatenate([jnp.where(lower, qs, none), jnp.where(lower, none, qs)], axis=0)
    prob = prob_low.astype(F32)
    dprob = nt(douts, v)
    delta = jnp.sum(prob * dprob, axis=1, keepdims=True)
    dscore = (prob * (dprob - delta)).astype(BF16)
    both = nn(dscore, jnp.concatenate([k, hot], axis=1))
    dq = jnp.where(lower, both[:ROWS, :128], both[ROWS:, :128]) * 0.125
    sums = shift_rows(jnp.where(lower, both[:ROWS, 128:], both[ROWS:, 128:]), amount, False).astype(BF16)
    dq = dq + nn(sums, tab)
    rel[...] += tn(sums, q)
    dk = tn(dscore, queries)
    dv = tn(prob_low, douts)
    return dq, dk, dv


def heads_kernel(ring, w, group, last, dout_ref, qkv_ref, prob_ref, height_ref, width_ref, *refs):
    refs = list(refs)
    rel_in = refs.pop(0) if w or group else None
    before = []
    if last:
        first_ref = refs.pop(0)
        before = [refs.pop(0) for _ in range(w)]
        early = [] if group else [refs.pop(0)]
    dep, dqkv, rel = refs[:3]
    table = refs[-1]
    fill_tables(table, height_ref, width_ref)
    tab = table[...].astype(BF16)
    rel[...] = jnp.zeros_like(rel) if rel_in is None else rel_in[...]
    amount = shift_bits()
    hot = one_hot(False)
    lower = iota((ROWS, 128), 1) < 64
    rows = slice(w * ROWS, (w + 1) * ROWS)
    for step in range(PAIRS // 2):
        p = group * (PAIRS // 2) + step
        at = slice(p * 128, (p + 1) * 128)
        q, k, v = (qkv_ref[:, i * D + p * 128 : i * D + (p + 1) * 128] for i in range(3))
        parts = heads_back(p, dout_ref[rows, at], lower, amount, hot, tab, q, k, v, prob_ref[p], rel)
        for which, value in enumerate(parts):
            dqkv[:, which * HALF + step * 128 : which * HALF + (step + 1) * 128] = value.astype(BF16)
    if last:
        keep_ref, send_ref, grad = refs[3:6]
        for ref in early:
            for which in range(2):
                store_blocks(keep_ref, send_ref, ring, which, ref.at[which])
        for which in range(3):
            cols = slice(which * HALF, (which + 1) * HALF)
            total = tn(first_ref[rows, :], dqkv[:, cols])
            for other, ref in enumerate(before):
                total = total + tn(first_ref[other * ROWS : (other + 1) * ROWS, :], ref[:, cols])
            grad[which] = total.astype(BF16)
            store_blocks(keep_ref, send_ref, ring, 2 * len(early) + which, grad.at[which])


def norm_two_kernel(ring, own_ref, mid_ref, cot_ref, mask_ref, att_ref, projw_ref, gain_ref, *refs):
    sibs, refs = refs[: cot_ref.shape[0]], refs[cot_ref.shape[0] :]
    dep, midg_ref, dout_ref, proj_ref, sum_ref, xs, low = refs
    windows = cot_ref.shape[0]
    gain = row(gain_ref)
    xs[ROWS - 16 :, :] = jnp.zeros((16, D), F32)
    gain_sum = jnp.zeros((1, D), F32)
    shift_sum = jnp.zeros((1, D), F32)
    proj_sum = jnp.zeros((1, D), F32)
    for w in range(windows):
        rows = slice(w * ROWS, (w + 1) * ROWS)
        n, s = norm(mid_ref[rows, :])
        e = own_ref[1, rows, :] + sibs[w][...].astype(F32)
        gain_sum = gain_sum + colsum(e * n)
        shift_sum = shift_sum + colsum(e)
        xs[0:PATCH, :] = cot_ref[w].astype(F32)
        grad = xs[...] + norm_back(e, n, s, gain)
        midg_ref[rows, :] = grad
        attn = (column_mask(mask_ref, w) * grad).astype(BF16)
        low[rows, :] = attn
        proj_sum = proj_sum + colsum(attn.astype(F32))
    sum_ref[...] = jnp.zeros_like(sum_ref)
    sum_ref[0:1, :] = gain_sum
    sum_ref[1:2, :] = shift_sum
    sum_ref[2:3, :] = proj_sum
    proj_grad = tn(att_ref[...], low[...])
    for half in range(2):
        proj_ref[half] = proj_grad[:, half * HALF : (half + 1) * HALF].astype(BF16)
    dout_ref[...] = nt(low[...], projw_ref[...]).astype(BF16)


def norm_one_kernel(tok_ref, midg_ref, mask_ref, own_ref, sib_ref, mid_ref, downb_ref, *refs):
    windows = tok_ref.shape[0]
    dqkv, refs = refs[: 2 * windows], refs[2 * windows :]
    w_ref, gain_ref, down_sum_ref, ub0_ref, ub1_ref, ub2_ref, sum_ref, rel_ref, dep, tokg_ref, tail_ref, out_ref, xs, small_ref = refs
    down_bias = row(downb_ref)
    gain = row(gain_ref)
    xs[ROWS - 16 :, :] = jnp.zeros((16, D), F32)
    gain_sum = jnp.zeros((1, D), F32)
    shift_sum = jnp.zeros((1, D), F32)
    sums = [jnp.zeros((1, HALF), F32) for _ in range(4)]
    for w in range(windows):
        rows = slice(w * ROWS, (w + 1) * ROWS)
        e = jnp.zeros((ROWS, D), F32)
        for group in range(2):
            grad = dqkv[group * windows + w]
            for which in range(3):
                cols = slice(which * HALF, (which + 1) * HALF)
                at = which * D + group * HALF
                e = e + nt(grad[:, cols], w_ref[:, at : at + HALF])
                if which != 1:
                    sums[which + group] = sums[which + group] + colsum(grad[:, cols].astype(F32))
        xs[0:PATCH, :] = tok_ref[w].astype(F32)
        n, s = norm(xs[...])
        gain_sum = gain_sum + colsum(e * n)
        shift_sum = shift_sum + colsum(e)
        tokg_ref[w] = (midg_ref[rows, :] + norm_back(e, n, s, gain))[0:PATCH]
        mlp_out = own_ref[0, rows, :] + sib_ref[rows, :].astype(F32)
        out = mid_ref[rows, :] + column_mask(mask_ref, w) * (mlp_out + down_bias)
        out_ref[w] = out[0:PATCH].astype(BF16)

    small_ref[...] = jnp.zeros_like(small_ref)

    def put(at, value):
        small_ref[at : at + 1, :] = value[:, :HALF]
        small_ref[at + 1 : at + 2, :] = value[:, HALF:]

    put(0, down_sum_ref[...])
    small_ref[2:10, :] = ub0_ref[...] + ub1_ref[...] + ub2_ref[...]
    for i in range(3):
        put(10 + 2 * i, sum_ref[i : i + 1, :])
    for i in range(4):
        small_ref[16 + i : 17 + i, :] = sums[i]
    put(20, gain_sum)
    put(22, shift_sum)
    both = rel_ref[...]
    heads = both[0:64, 0:64] + both[64:128, 64:128]
    small_ref[24:40, 0:256] = jnp.concatenate([heads[0:16], heads[16:32], heads[32:48], heads[48:64]], axis=1)
    tail_ref[...] = split(small_ref[...])


def split(x):
    coarse = x.astype(BF16)
    return jnp.concatenate([coarse.astype(F32), x - coarse.astype(F32)], axis=0).astype(BF16)


def join(x):
    half = x.shape[0] // 2
    return x[:half].astype(F32) + x[half:].astype(F32)


def sums_kernel(plan, count, *refs):
    outs = refs[len(refs) - len(plan) :]
    for terms, out in zip(plan, outs):
        total = None
        for which, part in terms:
            value = (refs[which][...] if part is None else refs[which][part]).astype(F32)
            total = value if total is None else total + value
        out[...] = total.astype(out.dtype)


def halve_kernel(keep_ref, got_ref, stay_ref, away_ref):
    size = stay_ref.shape[0]

    def place(mine, other):
        stay_ref[...] = (keep_ref[mine, :].astype(F32) + got_ref[mine, :].astype(F32)).astype(BF16)
        away_ref[0:size, :] = (keep_ref[other, :].astype(F32) + got_ref[other, :].astype(F32)).astype(BF16)

    low, high = slice(0, size), slice(size, 2 * size)
    either(lax.rem(lax.axis_index("mp"), 2), lambda: place(low, high), lambda: place(high, low))


def tail_kernel(tail_ref, got_ref, out_ref):
    out_ref[...] = split(join(tail_ref[...]) + join(got_ref[...]))


def second_kernel(keep_ref, got_ref, tail_ref, other_ref, stay_ref, away_ref):
    size = stay_ref.shape[0]
    stay_ref[...] = (keep_ref[0:size, :].astype(F32) + got_ref[0:size, :].astype(F32)).astype(BF16)
    away_ref[0:size, :] = (keep_ref[size:, :].astype(F32) + got_ref[size:, :].astype(F32)).astype(BF16)
    away_ref[size:, :] = split(join(tail_ref[...]) + join(other_ref[...]))


def near_kernel(keep_ref, got_ref, sent_ref, stay_ref, away_ref):
    halve_kernel(keep_ref, got_ref, stay_ref, away_ref)
    size, tail = stay_ref.shape[0], keep_ref.shape[0]
    away_ref[size:, :] = split(join(sent_ref[tail:, :]) + join(got_ref[tail:, :]))


def far_kernel(keep_ref, got_ref, sent_ref, away_ref):
    size = keep_ref.shape[0]
    away_ref[0:size, :] = (keep_ref[...].astype(F32) + got_ref[0:size, :].astype(F32)).astype(BF16)
    away_ref[size:, :] = split(join(sent_ref[size:, :]) + join(got_ref[size:, :]))


def finish_kernel(own_ref, got_ref, tail_ref, last_ref, early_ref, qkv_ref, *refs):
    n1g, n1s, qvb, relh, relw, pb, n2g, n2s, upb, db, small, both = refs
    size = own_ref.shape[0]
    odd = lax.rem(lax.axis_index("mp"), 2)

    def place(first, second):
        both[0:size, :] = first[...].astype(F32)
        both[size:, :] = second[...].astype(F32)

    either(odd, lambda: place(own_ref, got_ref), lambda: place(got_ref, own_ref))
    for which in range(3):
        qkv_ref[:, which * D : which * D + HALF] = early_ref[2 + which].astype(F32)
        qkv_ref[:, which * D + HALF : (which + 1) * D] = both[which * 96 : (which + 1) * 96, :]
    total = jnp.zeros((SMALL_ROWS, HALF), F32)
    for ref in (tail_ref, last_ref):
        at = ref.shape[0] - 2 * SMALL_ROWS
        total = total + (ref[at : at + SMALL_ROWS, :].astype(F32) + ref[at + SMALL_ROWS :, :].astype(F32))
    small[...] = total
    for ref, at, count in ((db, 0, 2), (upb, 2, 8), (n2g, 10, 2), (n2s, 12, 2), (pb, 14, 2), (qvb, 16, 4), (n1g, 20, 2), (n1s, 22, 2)):
        for i in range(count):
            ref[i * HALF : (i + 1) * HALF] = small[at + i : at + i + 1, :].reshape(HALF)
    rels = 2 * WIN - 1
    block = small[24:40, 0:256]
    for ref, at in ((relh, 0), (relw, 128)):
        ref[0:16, :] = block[:, at : at + 64]
        ref[16:rels, :] = block[0 : rels - 16, at + 64 : at + 128]


ANY = pl.BlockSpec(memory_space=pl.ANY)
HBM = pl.BlockSpec(memory_space=pltpu.HBM)


def call(kernel, outs, ins, scratch=(), us=1.0, after=None, limit=12, aliases=None, loose=0):
    shapes = tuple(jax.ShapeDtypeStruct(s, d) for s, d in outs)
    moved = sum(x.size * x.dtype.itemsize for x in ins) + sum(jnp.dtype(d).itemsize * functools.reduce(lambda a, b: a * b, s, 1) for s, d in outs)
    specs = [HBM] * loose + [VM] * (len(ins) - loose)
    if after is not None:
        ins, specs = [*ins, after], [*specs, ANY]
    return pl.pallas_call(
        kernel,
        out_shape=shapes,
        in_specs=specs,
        out_specs=tuple(VM for _ in outs),
        scratch_shapes=list(scratch),
        input_output_aliases=aliases or {},
        compiler_params=pltpu.CompilerParams(vmem_limit_bytes=limit * 2**20),
        cost_estimate=pl.CostEstimate(flops=int(us * 1.15e9), bytes_accessed=moved, transcendentals=0),
    )(*ins)


def tie(*arrays):
    return lax.optimization_barrier(arrays)


def local(tokens, window_mask, out_grad, norm1_gain, norm1_shift, qkv_weight, qv_bias, rel_height, rel_width, proj_weight, proj_bias,
          norm2_gain, norm2_shift, up_weight, up_bias, down_weight, down_bias):
    dpn, mpn = lax.axis_size("dp"), lax.axis_size("mp")
    c = lax.axis_index("dp") % 2
    windows = tokens.shape[0]
    rows = windows * ROWS
    ring = dpn == 8 and mpn == 4

    def send(x, move):
        perm = []
        for d in range(dpn):
            for m in range(mpn):
                nd, nm = move(d, m)
                perm.append((d * mpn + m, nd * mpn + nm))
        return lax.ppermute(x, AXES, perm)

    core = lambda d, m: (d ^ 1, m)
    first = lambda d, m: (d ^ (4 if d & 1 else 2), m)
    second = lambda d, m: (d ^ (2 if d & 1 else 4), m)
    up_ring = lambda d, m: (d, (m + 1) % mpn)
    down_ring = lambda d, m: (d, (m + mpn - 1) % mpn)
    near = lambda d, m: (d, m ^ 1)
    far = lambda d, m: (d, m ^ 2)
    hold = tie if ring else lambda *arrays: arrays
    narrow = pltpu.VMEM((ROWS, D), F32)
    square = pltpu.VMEM((128, 128), F32)

    def make_qkv(after):
        outs = [((rows, D), BF16), ((1, D), F32)] + [((ROWS, 3 * D), BF16)] * windows + [((ROWS, D), BF16)] * windows
        ins = [tokens, window_mask, out_grad, norm1_gain, norm1_shift, qkv_weight, qv_bias]
        res = call(qkv_kernel, outs, ins, [narrow], us=4.5, after=after)
        return res[0], res[1], res[2 : 2 + windows], res[2 + windows :]

    def attend(w, part, after):
        outs = [((PAIRS, 2 * ROWS, ROWS), BF16), ((ROWS, D), BF16)]
        return call(functools.partial(attend_kernel, w), outs, [window_mask, part, rel_height, rel_width], [square], us=8.0, after=after)

    def project(atts):
        outs = [((ROWS, D), BF16)] * windows + [((rows, D), F32), ((rows, D), BF16)]
        ins = [tokens, window_mask, proj_weight, proj_bias, norm2_gain, norm2_shift, *atts]
        res = call(project_kernel, outs, ins, [narrow], us=3.5)
        return res[:windows], *res[windows:]

    def mlp(spots, g, g_sib, x, x_sib, acc, packs, after):
        n, final = len(spots), spots[-1] == 2
        outs = [((2, rows, D), F32), ((rows, D), BF16), ((rows, D), BF16)] if final else [((2, 2 * rows, D), F32)]
        part = (2, 2, 2, 96, HALF)
        for spot in spots:
            outs += [((2, *part), BF16)] if spot == 3 else [(part, BF16)] * 2
        outs += [((8, HALF), F32)]
        scratch = [pltpu.VMEM((D, n * HALF), BF16), pltpu.VMEM((n * HALF, D), BF16), pltpu.VMEM((8, n * HALF), F32),
                   pltpu.VMEM((2 * rows, n * HALF), BF16), pltpu.VMEM((2 * rows, n * HALF), BF16), pltpu.VMEM((2, D, n * HALF), BF16)]
        ins = [*g, *g_sib, *x, *x_sib, *acc, *packs]
        aliases = {4 * windows: 0} if spots[0] and not final else None
        return call(functools.partial(mlp_kernel, ring, spots, windows), outs, ins, scratch, us=0.01 if n == 2 else 5.0, after=after, limit=12 + 6 * n, aliases=aliases)

    def norm_two(mine, sib, mid, att, after):
        outs = [((rows, D), F32), ((rows, D), BF16), ((2, D, HALF), BF16), ((8, D), F32)]
        ins = [mine, mid, out_grad, window_mask, att, proj_weight, norm2_gain, *sib]
        scratch = [narrow, pltpu.VMEM((rows, D), BF16)]
        return call(functools.partial(norm_two_kernel, ring), outs, ins, scratch, us=0.01, after=after)

    def heads(group, w, dout, rel, before, after):
        last = w == windows - 1
        before = before if group else [*before, proj]
        half = ((2, 2, 3 if group else 5, 96, HALF), BF16)
        outs = [((ROWS, 3 * HALF), BF16), ((128, 128), F32)] + ([half, half] if last else [])
        ins = [dout, qkvs[w], probs[w], rel_height, rel_width] + ([rel] if w or group else []) + ([first_low, *before] if last else [])
        scratch = ([pltpu.VMEM((3, D, HALF), BF16)] if last else []) + [square]
        return call(functools.partial(heads_kernel, ring, w, group, last), outs, ins, scratch, us=(6.0 if last else 3.0) if group else 0.01, after=after)

    def norm_one(mid_grad, mine, sib, mid, dqkv, ubs, down_sum, sums, rel, after):
        outs = [((windows, PATCH, D), F32), ((2 * SMALL_ROWS, HALF), BF16), ((windows, PATCH, D), BF16)]
        ins = [tokens, mid_grad, window_mask, mine, sib, mid, down_bias, *dqkv, qkv_weight, norm1_gain, down_sum, *ubs, sums, rel]
        return call(norm_one_kernel, outs, ins, [narrow, pltpu.VMEM((SMALL_ROWS, HALF), F32)], us=6.0, after=after)

    def adds(*plan, kind=BF16):
        ins, numbered, outs = [], [], []
        for terms in plan:
            row_of = []
            for term in terms:
                array, part = term if isinstance(term, tuple) else (term, None)
                known = [i for i, other in enumerate(ins) if other is array]
                if not known:
                    ins.append(array)
                row_of.append((known[0] if known else len(ins) - 1, part))
            first_term = terms[0]
            outs.append((first_term[0].shape[1:] if isinstance(first_term, tuple) else first_term.shape, kind))
            numbered.append(row_of)
        return call(functools.partial(sums_kernel, numbered, len(ins)), outs, ins, us=0.5)

    lines = lambda x: x.reshape(-1, HALF)

    if not ring:
        up_all = lax.all_gather(up_weight, "mp", axis=1, tiled=True)
        down_all = lax.all_gather(down_weight, "mp", axis=0, tiled=True)
        bias_all = lax.all_gather(up_bias, "mp", axis=0, tiled=True)
        packs = [up_all[:, :D], down_all[:D], bias_all[:D]]
        for k in range(1, 4):
            off = k * D + c * HALF
            u_part = lax.dynamic_slice(up_all, (0, off), (D, HALF))
            d_part = lax.dynamic_slice(down_all, (off, 0), (HALF, D))
            d_part = jnp.concatenate([d_part[:, :HALF], d_part[:, HALF:]], axis=0)
            b_part = jnp.broadcast_to(lax.dynamic_slice(bias_all, (off,), (HALF,))[None], (16, HALF))
            packs += [jnp.concatenate([u_part, b_part], axis=0), jnp.concatenate([d_part, b_part], axis=0)]
        first_low, down_sum, qkvs, g = make_qkv(packs[2])
        probs, atts = zip(*[attend(w, qkvs[w], first_low) for w in range(windows)])
        x, mid, att = project(atts)
        rows_of = (g, [send(part, core) for part in g], x, [send(part, core) for part in x])
        acc, keep0, send0, keep1, send1, ub0 = mlp((0, 1), *rows_of, [], packs[0:5], mid)
        acc, both3, ub1 = mlp((3,), *rows_of, [acc], packs[7:9], mid)
        mine, theirs, back, keep2, send2, ub2 = mlp((2,), *rows_of, [acc], packs[5:7], mid)
        mid_grad, dout, proj, sums = norm_two(mine, [send(back[w * ROWS : (w + 1) * ROWS], core) for w in range(windows)], mid, att, mid)
        dqkv, kept, sent, rel = [], [], [], None
        for group in range(2):
            for w in range(windows):
                part, rel, *weights = heads(group, w, dout, rel, dqkv[group * windows :], mid_grad)
                dqkv.append(part)
            kept.append(weights[0])
            sent.append(weights[1])
        tokens_grad, small, block_out = norm_one(mid_grad, mine, send(theirs, core), mid, dqkv, (ub0, ub1, ub2), down_sum, sums, rel, mid_grad)
        dw = jnp.stack([jnp.stack([keep0, keep1, keep2, both3[0]]), jnp.stack([send0, send1, send2, both3[1]])])
        halves = dw.transpose(4, 0, 2, 5, 3, 1, 6).reshape(D, 2, 4, HALF)
        full = jnp.zeros((D, 2, 4, 2, HALF), BF16)
        full = lax.dynamic_update_slice(full, halves[:, :, :, None], (0, 0, 0, c, 0)).reshape(D, 2, 4 * D)
        full = lax.psum_scatter(full, "dp", scatter_dimension=0, tiled=True)
        full = lax.psum_scatter(full, "mp", scatter_dimension=2, tiled=True).astype(F32)
        up_grad, down_grad = full[:, 0], full[:, 1].T
        weights = jnp.stack([jnp.concatenate(kept, axis=2), jnp.concatenate(sent, axis=2)])
        weights = weights.transpose(0, 1, 2, 4, 3, 5).reshape(D, 8 * HALF)
        weights = lax.psum(weights, "mp")
        weights = lax.psum_scatter(weights, "dp", scatter_dimension=0, tiled=True).astype(F32)
        parts = [weights[:, i * HALF : (i + 1) * HALF] for i in range(8)]
        proj_grad = jnp.concatenate(parts[0:2], axis=1)
        qkv_grad = jnp.concatenate([parts[2], parts[5], parts[3], parts[6], parts[4], parts[7]], axis=1)
        small = lax.psum(join(small), AXES)
        vec = lambda start, count: small[start : start + count].reshape(count * HALF)
        table = small[24:40, 0:256].reshape(16, 4, 64).transpose(1, 0, 2).reshape(64, 64)
        rels = 2 * WIN - 1
        return (
            block_out, tokens_grad, vec(20, 2), vec(22, 2), qkv_grad, vec(16, 4), table[0:rels], table[32 : 32 + rels], proj_grad,
            vec(14, 2), vec(10, 2), vec(12, 2), up_grad, vec(2, 8), down_grad, vec(0, 2),
        )

    pack, again = call(functools.partial(pack_kernel, ring), [((D + 32, HALF), BF16), ((D + 16, HALF), BF16)],
                       [up_weight, down_weight, up_bias], [pltpu.SemaphoreType.DMA((6,))], loose=2)
    m1 = send(pack, up_ring)
    m3 = send(again, down_ring)
    first_low, down_sum, qkvs, g = make_qkv(pack)
    probs, atts = zip(*[attend(w, qkvs[w], pack) for w in range(windows)])
    x, mid, att = project(atts)
    m1, *gx = tie(m1, *g, *x)
    g, x = gx[:windows], gx[windows:]

    m2 = send(m1, up_ring)
    o1 = send(m1, first)
    sib = [send(part, core) for part in gx]
    m3, o1, *sib = tie(m3, o1, *sib)
    rows_of = (g, sib[:windows], x, sib[windows:])

    o3 = send(m3, first)
    acc, keep0, send0, keep1, send1, ub0 = mlp((0, 1), *rows_of, [], [up_weight, down_weight, up_bias, m1, o1], o1)
    m2, o3, acc = tie(m2, o3, acc)

    o2 = send(m2, first)
    f1 = send(send1, first)
    acc, both3, ub1 = mlp((3,), *rows_of, [acc], [m3, o3], m2)
    o2, acc = tie(o2, acc)

    got3 = send(both3, up_ring)
    mine, theirs, back, keep2, send2, ub2 = mlp((2,), *rows_of, [acc], [m2, o2], o2)
    f1, back, send2 = tie(f1, back, send2)

    back_sib = [send(back[w * ROWS : (w + 1) * ROWS], core) for w in range(windows)]
    mid_grad, dout, proj, sums = norm_two(mine, back_sib, mid, att, f1)

    f2 = send(send2, first)
    s1_keep, s1_send = adds([(keep1, 0), (f1, 0)], [(keep1, 1), (f1, 1)])
    s1 = send(s1_send, second)
    part, rel = heads(0, 0, dout, None, [], dout)
    dqkv = [part]
    for w in range(1, windows):
        part, rel, *weights = heads(0, w, dout, rel, dqkv, dout)
        dqkv.append(part)
    keepq, sendq = weights
    f2, s1, got3, theirs, sendq, rel = tie(f2, s1, got3, theirs, sendq, rel)

    gotq = send(sendq, core)
    a_keep, a_send, s2_keep, s2_send, s1_keep = adds(
        [keep0, (got3, 0)], [send0, (got3, 1)], [(keep2, 0), (f2, 0)], [(keep2, 1), (f2, 1)], [s1_keep, s1])
    s2 = send(s2_send, second)
    got1 = send(s1_keep, down_ring)
    theirs_sib = send(theirs, core)
    q_keep, q_send = adds([(keepq, 0), (gotq, 0)], [(keepq, 1), (gotq, 1)])
    q1 = send(q_send, first)
    a1 = send(a_send, first)
    for w in range(windows):
        part, rel, *weights = heads(1, w, dout, rel, dqkv[windows:], q_send)
        dqkv.append(part)
    keepr, sendr = weights
    q1, s2, a1, got1, theirs_sib, rel, sendr = tie(q1, s2, a1, got1, theirs_sib, rel, sendr)

    gotr = send(sendr, core)
    r_keep, r_send = adds([(keepr, 0), (gotr, 0)], [(keepr, 1), (gotr, 1)])
    r1 = send(lines(r_send), first)
    q_keep, q_send, s2_keep = adds([(q_keep, 0), (q1, 0)], [(q_keep, 1), (q1, 1)], [s2_keep, s2])
    got2 = send(s2_keep, far)
    q2 = send(lines(q_send), second)
    tokens_grad, tail, block_out = norm_one(mid_grad, mine, theirs_sib, mid, dqkv, (ub0, ub1, ub2), down_sum, sums, rel, r_send)
    stretch = [((2 * SMALL_ROWS, HALF), BF16)]
    (tail,) = call(tail_kernel, stretch, [tail, send(tail, core)], us=0.5)
    other = send(tail, first)
    r1, q2, other, got2 = tie(r1, q2, other, got2)

    size = r1.shape[0] // 2
    stay, away = call(second_kernel, [((size, HALF), BF16), ((size + 2 * SMALL_ROWS, HALF), BF16)], [lines(r_keep), r1, tail, other], us=0.5)
    r2 = send(away, second)
    half = q2.shape[0] // 2
    q_stay, q_away = call(halve_kernel, [((half, HALF), BF16)] * 2, [lines(q_keep), q2], us=0.5)
    q3 = send(q_away, near)
    turned = [lax.transpose(x, (1, 0, 2)) for x in (tokens_grad, block_out)]
    r2, q3, *turned = tie(r2, q3, *turned)
    tokens_grad, block_out = [lax.transpose(x, (1, 0, 2)) for x in turned]

    size //= 2
    shapes = [((size, HALF), BF16), ((size + 2 * SMALL_ROWS, HALF), BF16)]
    stay, away = call(near_kernel, shapes, [stay, r2, away], us=0.5)
    r3 = send(away, near)
    (q_stay,) = adds([q_stay, q3])
    q4 = send(q_stay, far)
    a_keep, a_send = adds([(a_keep, 0), (a1, 0)], [(a_keep, 1), (a1, 1)])
    a2 = send(a_send, second)
    r3, q_stay, a2 = tie(r3, q_stay, a2)

    (away,) = call(far_kernel, shapes[1:], [stay, r3, away], us=0.5)
    r4 = send(away, far)
    (q_stay,) = adds([q_stay, q4])
    q5 = send(q_stay, near)
    (r_half,) = adds([away[:size], r4[:size]])
    r5 = send(r_half, near)
    mlp_part, = adds([a_keep, a2, got1, got2])
    other = send(mlp_part[:, 1], core)
    kept = mlp_part[:, 0]
    mlp_grads = jnp.where(c == 0, jnp.concatenate([kept, other], axis=2), jnp.concatenate([other, kept], axis=2)).astype(F32)
    odd = lax.axis_index("mp") % 2 == 1
    q_part = jnp.where(odd, jnp.concatenate([q5, q_stay], axis=0), jnp.concatenate([q_stay, q5], axis=0)).astype(F32)
    q_part = q_part.reshape(5, 96, HALF)
    proj_grad = jnp.concatenate([q_part[0], q_part[1]], axis=1)
    vec = lambda n: ((n,), F32)
    table = ((2 * WIN - 1, 64), F32)
    outs = [((96, 3 * D), F32), vec(D), vec(D), vec(2 * D), table, table, vec(D), vec(D), vec(D), vec(4 * D), vec(D)]
    qkv_grad, n1g, n1s, qvb, relh, relw, pb, n2g, n2s, upb, db = call(
        finish_kernel, outs, [r_half, r5, away, r4, q_part],
        [pltpu.VMEM((SMALL_ROWS, HALF), F32), pltpu.VMEM((3 * 96, HALF), F32)], us=2.0)
    return block_out, tokens_grad, n1g, n1s, qkv_grad, qvb, relh, relw, proj_grad, pb, n2g, n2s, mlp_grads[0], upb, mlp_grads[1].T, db


def solution(mesh):
    split_rows = P(AXES, None, None)
    in_specs = (split_rows, P(AXES, None), split_rows) + (P(),) * 10 + (P(None, "mp"), P("mp"), P("mp", None), P())
    out_specs = (split_rows, split_rows, P(), P(), P("dp", None), P(), P(), P(), P("dp", None), P(), P(), P(), P("dp", "mp"), P(), P("mp", "dp"), P())
    return jax.shard_map(local, mesh=mesh, in_specs=in_specs, out_specs=out_specs, check_vma=False)
```

```python
import functools

import jax
import jax.numpy as jnp
from jax import lax
from jax.experimental import pallas as pl
from jax.experimental.pallas import tpu as pltpu
from jax.sharding import PartitionSpec as P

D = 768
HEADS = 12
WIN = 14
PATCH = WIN * WIN
ROWS = 208
PAIRS = HEADS // 2
EPSILON = 1e-06
HALF = 384
F32 = jnp.float32
BF16 = jnp.bfloat16
AXES = ("dp", "mp")
VM = pl.BlockSpec(memory_space=pltpu.VMEM)
SMALL_ROWS = 40


def nn(a, b):
    return lax.dot_general(a, b, (((1,), (0,)), ((), ())), preferred_element_type=F32)


def nt(a, b):
    return lax.dot_general(a, b, (((1,), (1,)), ((), ())), preferred_element_type=F32)


def tn(a, b):
    return lax.dot_general(a, b, (((0,), (0,)), ((), ())), preferred_element_type=F32)


def iota(shape, dim):
    return lax.broadcasted_iota(jnp.int32, shape, dim)


def row(ref):
    return ref[...].astype(F32).reshape(1, -1)


def column_mask(mask_ref, w):
    line = mask_ref[w : w + 1, :].astype(F32)
    here = iota((ROWS, PATCH), 0) == iota((ROWS, PATCH), 1)
    return jnp.sum(jnp.where(here, line, 0.0), axis=1, keepdims=True)


def key_mask(column):
    here = iota((ROWS, ROWS), 0) == iota((ROWS, ROWS), 1)
    return jnp.sum(jnp.where(here, column, 0.0), axis=0, keepdims=True)


def norm(x):
    average = jnp.mean(x, axis=-1, keepdims=True)
    centred = x - average
    variance = jnp.mean(centred * centred, axis=-1, keepdims=True)
    inverse = lax.rsqrt(variance + EPSILON)
    return centred * inverse, inverse


def norm_back(e, n, s, gain):
    scaled = e * gain
    mean_grad = jnp.mean(scaled, axis=-1, keepdims=True)
    mean_proj = jnp.mean(scaled * n, axis=-1, keepdims=True)
    return s * (scaled - mean_grad - n * mean_proj)


def colsum(x):
    return jnp.sum(x, axis=0, keepdims=True)


def fill_tables(table, height_ref, width_ref):
    table[...] = jnp.zeros((128, 128), F32)
    height = height_ref[...].astype(F32)
    width = width_ref[...].astype(F32)
    none = jnp.zeros_like(height)
    rels = 2 * WIN - 1
    table[0:rels, :] = jnp.concatenate([height, none], axis=1)
    table[32 : 32 + rels, :] = jnp.concatenate([width, none], axis=1)
    table[64 : 64 + rels, :] = jnp.concatenate([none, height], axis=1)
    table[96 : 96 + rels, :] = jnp.concatenate([none, width], axis=1)


def shift_bits():
    place = iota((ROWS, 128), 0)
    high = place // WIN
    wide = place - high * WIN
    return jnp.where((iota((ROWS, 128), 1) & 32) == 0, high, wide)


def shift_rows(x, amount, left):
    for bit in range(4):
        step = 1 << bit
        moved = pltpu.roll(x, 128 - step if left else step, 1)
        x = jnp.where((amount & step) != 0, moved, x)
    return x


def one_hot(both):
    place = iota((ROWS, 128), 0)
    lane = iota((ROWS, 128), 1)
    high = place // WIN
    wide = place - high * WIN
    want = jnp.where((lane & 32) == 0, high, wide)
    sub = lane & 31
    slot = (sub & 15) if both else sub
    hit = (slot == (WIN - 1) - want) & (place < PATCH)
    return jnp.where(hit, 1.0, 0.0).astype(BF16)


def qkv_kernel(tok_ref, mask_ref, cot_ref, gain_ref, shift_ref, w_ref, bias_ref, dep, first_ref, sum_ref, *refs):
    windows = tok_ref.shape[0]
    outs, gs, xs = refs[:windows], refs[windows:-1], refs[-1]
    sums = jnp.zeros((1, D), F32)
    gain, shift = row(gain_ref), row(shift_ref)
    xs[ROWS - 16 :, :] = jnp.zeros((16, D), F32)
    for w in range(windows):
        xs[0:PATCH, :] = tok_ref[w].astype(F32)
        n, _ = norm(xs[...])
        first_ref[w * ROWS : (w + 1) * ROWS, :] = (n * gain + shift).astype(BF16)
        xs[0:PATCH, :] = cot_ref[w].astype(F32)
        g = (column_mask(mask_ref, w) * xs[...]).astype(BF16)
        gs[w][...] = g
        sums = sums + colsum(g.astype(F32))
    sum_ref[...] = sums
    bias = row(bias_ref)
    for part in range(3):
        cols = slice(part * D, (part + 1) * D)
        out = nn(first_ref[...], w_ref[:, cols])
        if part == 0:
            out = out + bias[:, :D]
        if part == 2:
            out = out + bias[:, D:]
        for w in range(windows):
            outs[w][:, cols] = out[w * ROWS : (w + 1) * ROWS].astype(BF16)


def attend_kernel(w, mask_ref, qkv_ref, height_ref, width_ref, dep, prob_ref, att_ref, table):
    fill_tables(table, height_ref, width_ref)
    tab = table[...].astype(BF16)
    amount = shift_bits()
    keys_hot = one_hot(True)
    lane = iota((ROWS, 128), 1)
    lower = lane < 64
    sub = lane & 31
    valid = key_mask(column_mask(mask_ref, w)) > 0.5

    def pair(p, carry):
        at = pl.multiple_of(p * 128, 128)
        q = qkv_ref[:, pl.ds(at, 128)]
        k = qkv_ref[:, pl.ds(D + at, 128)]
        v = qkv_ref[:, pl.ds(2 * D + at, 128)]
        terms = shift_rows(nt(q, tab), amount, True)
        coarse = terms.astype(BF16).astype(F32)
        fine = pltpu.roll(terms - coarse, 16, 1)
        terms = jnp.where(sub < WIN, coarse, jnp.where((sub >= 16) & (sub < 16 + WIN), fine, 0.0))
        qs = q.astype(F32) * 0.125
        top = jnp.concatenate([jnp.where(lower, qs, 0.0), jnp.where(lower, terms, 0.0)], axis=1)
        bottom = jnp.concatenate([jnp.where(lower, 0.0, qs), jnp.where(lower, 0.0, terms)], axis=1)
        left = jnp.concatenate([top, bottom], axis=0).astype(BF16)
        right = jnp.concatenate([k, keys_hot], axis=1)
        scores = jnp.where(valid, nt(left, right), -1000000000.0)
        most = jnp.max(scores, axis=1, keepdims=True)
        weight = jnp.exp(scores - most)
        total = jnp.sum(weight, axis=1, keepdims=True)
        prob = (weight * (1.0 / total)).astype(BF16)
        prob_ref[p] = prob
        out = nn(prob, v)
        att_ref[:, pl.ds(at, 128)] = jnp.where(lower, out[:ROWS], out[ROWS:]).astype(BF16)
        return carry

    lax.fori_loop(0, PAIRS, pair, 0, unroll=2)


def project_kernel(tok_ref, mask_ref, w_ref, bias_ref, gain_ref, shift_ref, *refs):
    windows = tok_ref.shape[0]
    atts, lows = refs[:windows], refs[windows : 2 * windows]
    mid_ref, all_ref, xs = refs[2 * windows :]
    gain, shift, bias = row(gain_ref), row(shift_ref), row(bias_ref)
    xs[ROWS - 16 :, :] = jnp.zeros((16, D), F32)
    for w in range(windows):
        all_ref[w * ROWS : (w + 1) * ROWS, :] = atts[w][...]
    out = nn(all_ref[...], w_ref[...]) + bias
    for w in range(windows):
        rows = slice(w * ROWS, (w + 1) * ROWS)
        xs[0:PATCH, :] = tok_ref[w].astype(F32)
        mid = xs[...] + column_mask(mask_ref, w) * out[rows]
        mid_ref[rows, :] = mid
        n, _ = norm(mid)
        lows[w][...] = (n * gain + shift).astype(BF16)


def position(ring):
    dp, z = lax.axis_index("dp"), lax.axis_index("mp")
    c = lax.rem(dp, 2)
    if not ring:
        return c, 0, 0, 0, 0
    y, x = lax.div(dp, 4), lax.rem(lax.div(dp, 2), 2)
    return c, jnp.where(c == 0, x, y), y, x, z


def apart(a, b):
    return a ^ b if isinstance(b, int) else jnp.where(b == a, 0, 1)


def slot_of(ring, block, by_block):
    yb, xb, cb = block // 4, (block // 2) % 2, block % 2
    if not ring:
        return block // 4, (block // 2) % 2, block % 2
    c, _, y, x, _ = position(ring)
    over_y, over_x = apart(yb, y), apart(xb, x)
    if by_block:
        return apart(cb, c), *((over_y, over_x) if cb else (over_x, over_y))
    return apart(cb, c), jnp.where(c == 0, over_x, over_y), jnp.where(c == 0, over_y, over_x)


def load_half(j, k, mine, other, up, down, bias):
    cols = slice(k * HALF, (k + 1) * HALF)
    bias[0:1, cols] = mine[D : D + 16, :].astype(F32)[0:1, :]

    def place(first, second):
        up[:, cols] = first[0:D, :]
        down[cols, 0:HALF] = second[0:HALF, :]
        down[cols, HALF:D] = second[HALF:D, :]

    either(j, lambda: place(mine, other), lambda: place(other, mine))


def hidden(x, g, up, down, bias):
    u = nn(x, up) + bias
    phi = 0.5 + 0.5 * lax.erf(u * 0.7071067811865476)
    slope = phi + u * jnp.exp(-0.5 * u * u) * 0.3989422804014327
    return (u * phi).astype(BF16), (nt(g, down) * slope).astype(BF16)


def weight_grads(ring, spots, grefs, xrefs, hid, pre, outs, ub_ref, grads):
    c, _, _, _, z = position(ring)
    width = len(spots) * HALF
    blocks = [slice(block * ROWS, (block + 1) * ROWS) for block in range(len(xrefs))]
    sums = jnp.zeros((1, width), F32)
    for block in blocks:
        sums = sums + colsum(pre[block, :].astype(F32))
    for which, (left, right) in enumerate(((xrefs, pre), (grefs, hid))):
        total = jnp.zeros((D, width), F32)
        for ref, block in zip(left, blocks):
            total = total + tn(ref[...], right[block, :])
        grads[which] = total.astype(BF16)
    ub_ref[...] = jnp.zeros_like(ub_ref)
    for k, spot in enumerate(spots):
        s = lax.rem(z + 4 - spot, 4) if ring else spot
        ub_ref[pl.ds(2 * s + c, 1), :] = sums[:, k * HALF : (k + 1) * HALF]
    for b in range(8):
        cr, first, second = slot_of(ring, b, False)
        lines = slice(b * 96, (b + 1) * 96)
        for k in range(len(spots)):
            part = slice(k * HALF, (k + 1) * HALF)

            def move(target, cr=cr, second=second, lines=lines, part=part):
                for which in range(2):
                    target[second, which, cr] = grads[which, lines, part]

            if len(outs[k]) == 1:
                move(outs[k][0].at[first])
            else:
                either(first, lambda k=k, move=move: move(outs[k][0]), lambda k=k, move=move: move(outs[k][1]))


def mlp_kernel(ring, spots, windows, *refs):
    refs = list(refs)
    blocks = 2 * windows
    grefs = [refs.pop(0) for _ in range(blocks)]
    xrefs = [refs.pop(0) for _ in range(blocks)]
    c, j, *_ = position(ring)
    if spots[0] == 0:
        acc_in = None
        up_ref, down_ref, upb_ref = (refs.pop(0) for _ in range(3))
    else:
        acc_in = refs.pop(0)
    packs = [(k, refs.pop(0), refs.pop(0)) for k, spot in enumerate(spots) if spot]
    dep, acc = refs.pop(0), refs.pop(0)
    outs = [(refs.pop(0),) if spot == 1 else (refs.pop(0), refs.pop(0)) for spot in spots]
    ub_ref, up, down, bias, hid, pre, grads = refs
    if acc_in is None:
        off = pl.multiple_of(c * HALF, HALF)
        up[:, 0:HALF] = up_ref[:, pl.ds(off, HALF)]
        down[0:HALF, :] = down_ref[pl.ds(off, HALF), :]
        line = row(upb_ref)
        bias[0:1, 0:HALF] = jnp.where(c == 0, line[:, :HALF], line[:, HALF:])
    for k, mine, other in packs:
        load_half(j, k, mine, other, up, down, bias)
    up_c, down_c, bias_c = up[...], down[...], bias[0:1, :]
    for block in range(blocks):
        there = slice(block * ROWS, (block + 1) * ROWS)
        h, pg = hidden(xrefs[block][...], grefs[block][...], up_c, down_c, bias_c)
        hid[there, :] = h
        pre[there, :] = pg
        for which, value in enumerate((nn(h, down_c), nt(pg, up_c))):
            acc[which, there, :] = value if acc_in is None else acc_in[which, there, :] + value
    weight_grads(ring, spots, grefs, xrefs, hid, pre, outs, ub_ref, grads)


def mlp_front_kernel(ring, windows, *refs):
    blocks = 2 * windows
    grefs, xrefs, refs = refs[:blocks], refs[blocks : 2 * blocks], refs[2 * blocks :]
    acc, mine, other, dep, back_ref, tback_ref, hid, pre, down, up, bias = refs
    load_half(position(ring)[1], 0, mine, other, up, down, bias)
    up_c, down_c, bias_c = up[...], down[...], bias[0:1, :]
    for block in range(blocks):
        here = slice((block % windows) * ROWS, (block % windows + 1) * ROWS)
        there = slice(block * ROWS, (block + 1) * ROWS)
        h, pg = hidden(xrefs[block][...], grefs[block][...], up_c, down_c, bias_c)
        hid[there, :] = h
        pre[there, :] = pg
        back = acc[1, there, :] + nt(pg, up_c)
        if block < windows:
            back_ref[here, :] = back
        else:
            tback_ref[block - windows] = back.astype(BF16)


def mlp_rear_kernel(ring, windows, *refs):
    blocks = 2 * windows
    grefs, xrefs, refs = refs[:blocks], refs[blocks : 2 * blocks], refs[2 * blocks :]
    acc, hid, pre, down, out_ref, tout_ref, keep_ref, send_ref, ub_ref, grads = refs
    weight_grads(ring, (3,), grefs, xrefs, hid, pre, [(keep_ref, send_ref)], ub_ref, grads)
    for block in range(blocks):
        here = slice((block % windows) * ROWS, (block % windows + 1) * ROWS)
        there = slice(block * ROWS, (block + 1) * ROWS)
        out = acc[0, there, :] + nn(hid[there, :], down[...])
        if block < windows:
            out_ref[here, :] = out
        else:
            tout_ref[here, :] = out.astype(BF16)


def either(index, zero, one):
    if isinstance(index, int):
        return one() if index else zero()
    pl.when(index == 0)(zero)
    pl.when(index != 0)(one)


def store_blocks(keep_ref, send_ref, ring, index, ref):
    for b in range(8):
        cr, first, second = slot_of(ring, b, True)
        lines = slice(b * 96, (b + 1) * 96)

        def move(target, first=first, second=second, lines=lines):
            target[first, second, index] = ref[lines, :]

        either(cr, lambda move=move: move(keep_ref), lambda move=move: move(send_ref))


def heads_back(p, dout, lower, amount, hot, tab, q, k, v, prob_low, rel):
    none = jnp.zeros_like(dout)
    douts = jnp.concatenate([jnp.where(lower, dout, none), jnp.where(lower, none, dout)], axis=0)
    qs = (q.astype(F32) * 0.125).astype(BF16)
    queries = jnp.concatenate([jnp.where(lower, qs, none), jnp.where(lower, none, qs)], axis=0)
    prob = prob_low.astype(F32)
    dprob = nt(douts, v)
    delta = jnp.sum(prob * dprob, axis=1, keepdims=True)
    dscore = (prob * (dprob - delta)).astype(BF16)
    both = nn(dscore, jnp.concatenate([k, hot], axis=1))
    dq = jnp.where(lower, both[:ROWS, :128], both[ROWS:, :128]) * 0.125
    sums = shift_rows(jnp.where(lower, both[:ROWS, 128:], both[ROWS:, 128:]), amount, False).astype(BF16)
    dq = dq + nn(sums, tab)
    rel[...] += tn(sums, q)
    dk = tn(dscore, queries)
    dv = tn(prob_low, douts)
    return dq, dk, dv


def heads_kernel(ring, w, group, last, dout_ref, qkv_ref, prob_ref, height_ref, width_ref, *refs):
    refs = list(refs)
    rel_in = refs.pop(0) if w or group else None
    before = []
    if last:
        first_ref = refs.pop(0)
        before = [refs.pop(0) for _ in range(w)]
        early = [] if group else [refs.pop(0)]
    dep, dqkv, rel = refs[:3]
    table = refs[-1]
    fill_tables(table, height_ref, width_ref)
    tab = table[...].astype(BF16)
    rel[...] = jnp.zeros_like(rel) if rel_in is None else rel_in[...]
    amount = shift_bits()
    hot = one_hot(False)
    lower = iota((ROWS, 128), 1) < 64
    rows = slice(w * ROWS, (w + 1) * ROWS)
    for step in range(PAIRS // 2):
        p = group * (PAIRS // 2) + step
        at = slice(p * 128, (p + 1) * 128)
        q, k, v = (qkv_ref[:, i * D + p * 128 : i * D + (p + 1) * 128] for i in range(3))
        parts = heads_back(p, dout_ref[rows, at], lower, amount, hot, tab, q, k, v, prob_ref[p], rel)
        for which, value in enumerate(parts):
            dqkv[:, which * HALF + step * 128 : which * HALF + (step + 1) * 128] = value.astype(BF16)
    if last:
        keep_ref, send_ref, grad = refs[3:6]
        for ref in early:
            for which in range(2):
                store_blocks(keep_ref, send_ref, ring, which, ref.at[which])
        for which in range(3):
            cols = slice(which * HALF, (which + 1) * HALF)
            total = tn(first_ref[rows, :], dqkv[:, cols])
            for other, ref in enumerate(before):
                total = total + tn(first_ref[other * ROWS : (other + 1) * ROWS, :], ref[:, cols])
            grad[which] = total.astype(BF16)
            store_blocks(keep_ref, send_ref, ring, 2 * len(early) + which, grad.at[which])


def norm_two_kernel(ring, own_ref, mid_ref, cot_ref, mask_ref, att_ref, projw_ref, gain_ref, *refs):
    sibs, refs = refs[: cot_ref.shape[0]], refs[cot_ref.shape[0] :]
    dep, midg_ref, dout_ref, proj_ref, sum_ref, xs, low = refs
    windows = cot_ref.shape[0]
    gain = row(gain_ref)
    xs[ROWS - 16 :, :] = jnp.zeros((16, D), F32)
    gain_sum = jnp.zeros((1, D), F32)
    shift_sum = jnp.zeros((1, D), F32)
    proj_sum = jnp.zeros((1, D), F32)
    for w in range(windows):
        rows = slice(w * ROWS, (w + 1) * ROWS)
        n, s = norm(mid_ref[rows, :])
        e = own_ref[rows, :] + sibs[w][...].astype(F32)
        gain_sum = gain_sum + colsum(e * n)
        shift_sum = shift_sum + colsum(e)
        xs[0:PATCH, :] = cot_ref[w].astype(F32)
        grad = xs[...] + norm_back(e, n, s, gain)
        midg_ref[rows, :] = grad
        attn = (column_mask(mask_ref, w) * grad).astype(BF16)
        low[rows, :] = attn
        proj_sum = proj_sum + colsum(attn.astype(F32))
    sum_ref[...] = jnp.zeros_like(sum_ref)
    sum_ref[0:1, :] = gain_sum
    sum_ref[1:2, :] = shift_sum
    sum_ref[2:3, :] = proj_sum
    proj_grad = tn(att_ref[...], low[...])
    for half in range(2):
        proj_ref[half] = proj_grad[:, half * HALF : (half + 1) * HALF].astype(BF16)
    dout_ref[...] = nt(low[...], projw_ref[...]).astype(BF16)


def norm_one_kernel(tok_ref, midg_ref, *refs):
    windows = tok_ref.shape[0]
    dqkv, refs = refs[: 2 * windows], refs[2 * windows :]
    w_ref, gain_ref, down_sum_ref, ub0_ref, ub1_ref, ub2_ref, ub3_ref, sum_ref, rel_ref, dep, tokg_ref, tail_ref, xs, small_ref = refs
    gain = row(gain_ref)
    xs[ROWS - 16 :, :] = jnp.zeros((16, D), F32)
    gain_sum = jnp.zeros((1, D), F32)
    shift_sum = jnp.zeros((1, D), F32)
    sums = [jnp.zeros((1, HALF), F32) for _ in range(4)]
    for w in range(windows):
        rows = slice(w * ROWS, (w + 1) * ROWS)
        e = jnp.zeros((ROWS, D), F32)
        for group in range(2):
            grad = dqkv[group * windows + w]
            for which in range(3):
                cols = slice(which * HALF, (which + 1) * HALF)
                at = which * D + group * HALF
                e = e + nt(grad[:, cols], w_ref[:, at : at + HALF])
                if which != 1:
                    sums[which + group] = sums[which + group] + colsum(grad[:, cols].astype(F32))
        xs[0:PATCH, :] = tok_ref[w].astype(F32)
        n, s = norm(xs[...])
        gain_sum = gain_sum + colsum(e * n)
        shift_sum = shift_sum + colsum(e)
        tokg_ref[rows, :] = midg_ref[rows, :] + norm_back(e, n, s, gain)

    small_ref[...] = jnp.zeros_like(small_ref)

    def put(at, value):
        small_ref[at : at + 1, :] = value[:, :HALF]
        small_ref[at + 1 : at + 2, :] = value[:, HALF:]

    put(0, down_sum_ref[...])
    small_ref[2:10, :] = ub0_ref[...] + ub1_ref[...] + ub2_ref[...] + ub3_ref[...]
    for i in range(3):
        put(10 + 2 * i, sum_ref[i : i + 1, :])
    for i in range(4):
        small_ref[16 + i : 17 + i, :] = sums[i]
    put(20, gain_sum)
    put(22, shift_sum)
    both = rel_ref[...]
    heads = both[0:64, 0:64] + both[64:128, 64:128]
    small_ref[24:40, 0:256] = jnp.concatenate([heads[0:16], heads[16:32], heads[32:48], heads[48:64]], axis=1)
    tail_ref[...] = split(small_ref[...])


def outputs_kernel(tokg_ref, mask_ref, own_ref, sib_ref, mid_ref, downb_ref, dep, grad_ref, out_ref):
    windows = mask_ref.shape[0]
    down_bias = row(downb_ref)
    outs = []
    for w in range(windows):
        rows = slice(w * ROWS, (w + 1) * ROWS)
        grad_ref[:, w, :] = tokg_ref[w * ROWS : w * ROWS + PATCH, :]
        mlp_out = own_ref[rows, :] + sib_ref[rows, :].astype(F32)
        outs.append((mid_ref[rows, :] + column_mask(mask_ref, w) * (mlp_out + down_bias))[0:PATCH])
    out_ref[...] = jnp.stack(outs, axis=1).astype(BF16)


def split(x):
    coarse = x.astype(BF16)
    return jnp.concatenate([coarse.astype(F32), x - coarse.astype(F32)], axis=0).astype(BF16)


def join(x):
    half = x.shape[0] // 2
    return x[:half].astype(F32) + x[half:].astype(F32)


def sums_kernel(plan, count, *refs):
    outs = refs[len(refs) - len(plan) :]
    for terms, out in zip(plan, outs):
        total = None
        for which, part in terms:
            value = (refs[which][...] if part is None else refs[which][part]).astype(F32)
            total = value if total is None else total + value
        out[...] = total.astype(out.dtype)


def halve_kernel(keep_ref, got_ref, stay_ref, away_ref):
    size = stay_ref.shape[0]

    def place(mine, other):
        stay_ref[...] = (keep_ref[mine, :].astype(F32) + got_ref[mine, :].astype(F32)).astype(BF16)
        away_ref[0:size, :] = (keep_ref[other, :].astype(F32) + got_ref[other, :].astype(F32)).astype(BF16)

    low, high = slice(0, size), slice(size, 2 * size)
    either(lax.rem(lax.axis_index("mp"), 2), lambda: place(low, high), lambda: place(high, low))


def tail_kernel(tail_ref, got_ref, out_ref):
    out_ref[...] = split(join(tail_ref[...]) + join(got_ref[...]))


def second_kernel(keep_ref, got_ref, tail_ref, other_ref, stay_ref, away_ref):
    size = stay_ref.shape[0]
    stay_ref[...] = (keep_ref[0:size, :].astype(F32) + got_ref[0:size, :].astype(F32)).astype(BF16)
    away_ref[0:size, :] = (keep_ref[size:, :].astype(F32) + got_ref[size:, :].astype(F32)).astype(BF16)
    away_ref[size:, :] = split(join(tail_ref[...]) + join(other_ref[...]))


def near_kernel(keep_ref, got_ref, sent_ref, stay_ref, away_ref):
    halve_kernel(keep_ref, got_ref, stay_ref, away_ref)
    size, tail = stay_ref.shape[0], keep_ref.shape[0]
    away_ref[size:, :] = split(join(sent_ref[tail:, :]) + join(got_ref[tail:, :]))


def far_kernel(keep_ref, got_ref, sent_ref, away_ref):
    size = keep_ref.shape[0]
    away_ref[0:size, :] = (keep_ref[...].astype(F32) + got_ref[0:size, :].astype(F32)).astype(BF16)
    away_ref[size:, :] = split(join(sent_ref[size:, :]) + join(got_ref[size:, :]))


def finish_kernel(own_ref, got_ref, tail_ref, last_ref, stay_ref, away_ref, qkv_ref, proj_ref, *refs):
    n1g, n1s, qvb, relh, relw, pb, n2g, n2s, upb, db, small, late, early = refs
    odd = lax.rem(lax.axis_index("mp"), 2)

    def place(into, first, second):
        size = first.shape[0]
        into[0:size, :] = first[...].astype(F32)
        into[size:, :] = second[...].astype(F32)

    for into, own, got in ((late, own_ref, got_ref), (early, stay_ref, away_ref)):
        either(odd, lambda into=into, own=own, got=got: place(into, own, got), lambda into=into, own=own, got=got: place(into, got, own))
    for half in range(2):
        proj_ref[:, half * HALF : (half + 1) * HALF] = early[half * 96 : (half + 1) * 96, :]
    for which in range(3):
        qkv_ref[:, which * D : which * D + HALF] = early[(2 + which) * 96 : (3 + which) * 96, :]
        qkv_ref[:, which * D + HALF : (which + 1) * D] = late[which * 96 : (which + 1) * 96, :]
    total = jnp.zeros((SMALL_ROWS, HALF), F32)
    for ref in (tail_ref, last_ref):
        at = ref.shape[0] - 2 * SMALL_ROWS
        total = total + (ref[at : at + SMALL_ROWS, :].astype(F32) + ref[at + SMALL_ROWS :, :].astype(F32))
    small[...] = total
    for ref, at, count in ((db, 0, 2), (upb, 2, 8), (n2g, 10, 2), (n2s, 12, 2), (pb, 14, 2), (qvb, 16, 4), (n1g, 20, 2), (n1s, 22, 2)):
        for i in range(count):
            ref[i * HALF : (i + 1) * HALF] = small[at + i : at + i + 1, :].reshape(HALF)
    rels = 2 * WIN - 1
    block = small[24:40, 0:256]
    for ref, at in ((relh, 0), (relw, 128)):
        ref[0:16, :] = block[:, at : at + 64]
        ref[16:rels, :] = block[0 : rels - 16, at + 64 : at + 128]


ANY = pl.BlockSpec(memory_space=pl.ANY)


def call(kernel, outs, ins, scratch=(), us=1.0, after=None, limit=12, aliases=None):
    shapes = tuple(jax.ShapeDtypeStruct(s, d) for s, d in outs)
    moved = sum(x.size * x.dtype.itemsize for x in ins) + sum(jnp.dtype(d).itemsize * functools.reduce(lambda a, b: a * b, s, 1) for s, d in outs)
    specs = [VM] * len(ins)
    if after is not None:
        ins, specs = [*ins, after], [*specs, ANY]
    return pl.pallas_call(
        kernel,
        out_shape=shapes,
        in_specs=specs,
        out_specs=tuple(VM for _ in outs),
        scratch_shapes=list(scratch),
        input_output_aliases=aliases or {},
        compiler_params=pltpu.CompilerParams(vmem_limit_bytes=limit * 2**20),
        cost_estimate=pl.CostEstimate(flops=int(us * 1.15e9), bytes_accessed=moved, transcendentals=0),
    )(*ins)


def tie(*arrays):
    return lax.optimization_barrier(arrays)


def local(tokens, window_mask, out_grad, norm1_gain, norm1_shift, qkv_weight, qv_bias, rel_height, rel_width, proj_weight, proj_bias,
          norm2_gain, norm2_shift, up_weight, up_bias, down_weight, down_bias):
    dpn, mpn = lax.axis_size("dp"), lax.axis_size("mp")
    c = lax.axis_index("dp") % 2
    windows = tokens.shape[0]
    rows = windows * ROWS
    ring = dpn == 8 and mpn == 4

    def send(x, move):
        perm = []
        for d in range(dpn):
            for m in range(mpn):
                nd, nm = move(d, m)
                perm.append((d * mpn + m, nd * mpn + nm))
        return lax.ppermute(x, AXES, perm)

    core = lambda d, m: (d ^ 1, m)
    first = lambda d, m: (d ^ (4 if d & 1 else 2), m)
    second = lambda d, m: (d ^ (2 if d & 1 else 4), m)
    up_ring = lambda d, m: (d, (m + 1) % mpn)
    down_ring = lambda d, m: (d, (m + mpn - 1) % mpn)
    near = lambda d, m: (d, m ^ 1)
    far = lambda d, m: (d, m ^ 2)
    hold = tie if ring else lambda *arrays: arrays
    narrow = pltpu.VMEM((ROWS, D), F32)
    square = pltpu.VMEM((128, 128), F32)

    def make_qkv(after):
        outs = [((rows, D), BF16), ((1, D), F32)] + [((ROWS, 3 * D), BF16)] * windows + [((ROWS, D), BF16)] * windows
        ins = [tokens, window_mask, out_grad, norm1_gain, norm1_shift, qkv_weight, qv_bias]
        res = call(qkv_kernel, outs, ins, [narrow], us=4.5, after=after)
        return res[0], res[1], res[2 : 2 + windows], res[2 + windows :]

    def attend(w, part, after):
        outs = [((PAIRS, 2 * ROWS, ROWS), BF16), ((ROWS, D), BF16)]
        return call(functools.partial(attend_kernel, w), outs, [window_mask, part, rel_height, rel_width], [square], us=0.01 if w else 8.0, after=after)

    def project(atts):
        outs = [((ROWS, D), BF16)] * windows + [((rows, D), F32), ((rows, D), BF16)]
        ins = [tokens, window_mask, proj_weight, proj_bias, norm2_gain, norm2_shift, *atts]
        res = call(project_kernel, outs, ins, [narrow], us=0.01)
        return res[:windows], *res[windows:]

    part = ((2, 2, 2, 96, HALF), BF16)

    def mlp(spots, g, g_sib, x, x_sib, acc, packs, after):
        n = len(spots)
        outs = [((2, 2 * rows, D), F32)]
        for spot in spots:
            outs += [((2, *part[0]), BF16)] if spot == 1 else [part] * 2
        outs += [((8, HALF), F32)]
        scratch = [pltpu.VMEM((D, n * HALF), BF16), pltpu.VMEM((n * HALF, D), BF16), pltpu.VMEM((8, n * HALF), F32),
                   pltpu.VMEM((2 * rows, n * HALF), BF16), pltpu.VMEM((2 * rows, n * HALF), BF16), pltpu.VMEM((2, D, n * HALF), BF16)]
        ins = [*g, *g_sib, *x, *x_sib, *acc, *packs]
        aliases = {4 * windows: 0} if spots[0] else None
        return call(functools.partial(mlp_kernel, ring, spots, windows), outs, ins, scratch, us=0.01, after=after,
                    limit=12 + 6 * n, aliases=aliases)

    def mlp_front(g, g_sib, x, x_sib, acc, packs, after):
        wide = ((2 * rows, HALF), BF16)
        outs = [((rows, D), F32), ((windows, ROWS, D), BF16), wide, wide, ((HALF, D), BF16)]
        return call(functools.partial(mlp_front_kernel, ring, windows), outs, [*g, *g_sib, *x, *x_sib, acc, *packs],
                    [pltpu.VMEM((D, HALF), BF16), pltpu.VMEM((8, HALF), F32)], us=0.01, after=after, limit=16)

    def mlp_rear(g, g_sib, x, x_sib, acc, hid, pre, down):
        outs = [((rows, D), F32), ((rows, D), BF16), part, part, ((8, HALF), F32)]
        return call(functools.partial(mlp_rear_kernel, ring, windows), outs, [*g, *g_sib, *x, *x_sib, acc, hid, pre, down],
                    [pltpu.VMEM((2, D, HALF), BF16)], us=0.01, limit=16)

    def norm_two(mine, sib, mid, att, after):
        outs = [((rows, D), F32), ((rows, D), BF16), ((2, D, HALF), BF16), ((8, D), F32)]
        ins = [mine, mid, out_grad, window_mask, att, proj_weight, norm2_gain, *sib]
        scratch = [narrow, pltpu.VMEM((rows, D), BF16)]
        return call(functools.partial(norm_two_kernel, ring), outs, ins, scratch, us=0.01, after=after)

    def heads(group, w, dout, rel, before, after):
        last = w == windows - 1
        before = before if group else [*before, proj]
        half = ((2, 2, 3 if group else 5, 96, HALF), BF16)
        outs = [((ROWS, 3 * HALF), BF16), ((128, 128), F32)] + ([half, half] if last else [])
        ins = [dout, qkvs[w], probs[w], rel_height, rel_width] + ([rel] if w or group else []) + ([first_low, *before] if last else [])
        scratch = ([pltpu.VMEM((3, D, HALF), BF16)] if last else []) + [square]
        return call(functools.partial(heads_kernel, ring, w, group, last), outs, ins, scratch, us=(6.0 if last else 3.0) if group else 0.01, after=after)

    def norm_one(mid_grad, dqkv, ubs, down_sum, sums, rel, after):
        outs = [((rows, D), F32), ((2 * SMALL_ROWS, HALF), BF16)]
        ins = [tokens, mid_grad, *dqkv, qkv_weight, norm1_gain, down_sum, *ubs, sums, rel]
        return call(norm_one_kernel, outs, ins, [narrow, pltpu.VMEM((SMALL_ROWS, HALF), F32)], us=6.0, after=after)

    def outputs(tokens_grad, mine, sib, mid, after):
        outs = [((PATCH, windows, D), F32), ((PATCH, windows, D), BF16)]
        return call(outputs_kernel, outs, [tokens_grad, window_mask, mine, sib, mid, down_bias], us=2.0, after=after)

    turn = lambda x: lax.transpose(x, (1, 0, 2))

    def adds(*plan, kind=BF16):
        ins, numbered, outs = [], [], []
        for terms in plan:
            row_of = []
            for term in terms:
                array, part = term if isinstance(term, tuple) else (term, None)
                known = [i for i, other in enumerate(ins) if other is array]
                if not known:
                    ins.append(array)
                row_of.append((known[0] if known else len(ins) - 1, part))
            first_term = terms[0]
            outs.append((first_term[0].shape[1:] if isinstance(first_term, tuple) else first_term.shape, kind))
            numbered.append(row_of)
        return call(functools.partial(sums_kernel, numbered, len(ins)), outs, ins, us=0.5)

    lines = lambda x: x.reshape(-1, HALF)

    if not ring:
        up_all = lax.all_gather(up_weight, "mp", axis=1, tiled=True)
        down_all = lax.all_gather(down_weight, "mp", axis=0, tiled=True)
        bias_all = lax.all_gather(up_bias, "mp", axis=0, tiled=True)
        packs = [up_all[:, :D], down_all[:D], bias_all[:D]]
        for k in range(1, 4):
            off = k * D + c * HALF
            u_part = lax.dynamic_slice(up_all, (0, off), (D, HALF))
            d_part = lax.dynamic_slice(down_all, (off, 0), (HALF, D))
            d_part = jnp.concatenate([d_part[:, :HALF], d_part[:, HALF:]], axis=0)
            b_part = jnp.broadcast_to(lax.dynamic_slice(bias_all, (off,), (HALF,))[None], (16, HALF))
            packs += [jnp.concatenate([u_part, b_part], axis=0), jnp.concatenate([d_part, b_part], axis=0)]
        first_low, down_sum, qkvs, g = make_qkv(packs[2])
        probs, atts = zip(*[attend(w, qkvs[w], first_low) for w in range(windows)])
        x, mid, att = project(atts)
        rows_of = (g, [send(part, core) for part in g], x, [send(part, core) for part in x])
        acc, keep0, send0, ub0 = mlp((0,), *rows_of, [], packs[0:3], mid)
        acc, both1, ub1 = mlp((1,), *rows_of, [acc], packs[3:5], mid)
        acc, keep2, send2, ub2 = mlp((2,), *rows_of, [acc], packs[5:7], mid)
        mine_back, back, *kept = mlp_front(*rows_of, acc, packs[7:9], mid)
        mine_out, theirs, keep3, send3, ub3 = mlp_rear(*rows_of, acc, *kept)
        mid_grad, dout, proj, sums = norm_two(mine_back, [send(back[w], core) for w in range(windows)], mid, att, mid)
        dqkv, kept, sent, rel = [], [], [], None
        for group in range(2):
            for w in range(windows):
                part, rel, *weights = heads(group, w, dout, rel, dqkv[group * windows :], mid_grad)
                dqkv.append(part)
            kept.append(weights[0])
            sent.append(weights[1])
        tokens_grad, small = norm_one(mid_grad, dqkv, (ub0, ub1, ub2, ub3), down_sum, sums, rel, mid_grad)
        tokens_grad, block_out = (turn(x) for x in outputs(tokens_grad, mine_out, send(theirs, core), mid, mid))
        dw = jnp.stack([jnp.stack([keep0, both1[0], keep2, keep3]), jnp.stack([send0, both1[1], send2, send3])])
        halves = dw.transpose(4, 0, 2, 5, 3, 1, 6).reshape(D, 2, 4, HALF)
        full = jnp.zeros((D, 2, 4, 2, HALF), BF16)
        full = lax.dynamic_update_slice(full, halves[:, :, :, None], (0, 0, 0, c, 0)).reshape(D, 2, 4 * D)
        full = lax.psum_scatter(full, "dp", scatter_dimension=0, tiled=True)
        full = lax.psum_scatter(full, "mp", scatter_dimension=2, tiled=True).astype(F32)
        up_grad, down_grad = full[:, 0], full[:, 1].T
        weights = jnp.stack([jnp.concatenate(kept, axis=2), jnp.concatenate(sent, axis=2)])
        weights = weights.transpose(0, 1, 2, 4, 3, 5).reshape(D, 8 * HALF)
        weights = lax.psum(weights, "mp")
        weights = lax.psum_scatter(weights, "dp", scatter_dimension=0, tiled=True).astype(F32)
        parts = [weights[:, i * HALF : (i + 1) * HALF] for i in range(8)]
        proj_grad = jnp.concatenate(parts[0:2], axis=1)
        qkv_grad = jnp.concatenate([parts[2], parts[5], parts[3], parts[6], parts[4], parts[7]], axis=1)
        small = lax.psum(join(small), AXES)
        vec = lambda start, count: small[start : start + count].reshape(count * HALF)
        table = small[24:40, 0:256].reshape(16, 4, 64).transpose(1, 0, 2).reshape(64, 64)
        rels = 2 * WIN - 1
        return (
            block_out, tokens_grad, vec(20, 2), vec(22, 2), qkv_grad, vec(16, 4), table[0:rels], table[32 : 32 + rels], proj_grad,
            vec(14, 2), vec(10, 2), vec(12, 2), up_grad, vec(2, 8), down_grad, vec(0, 2),
        )

    dp = lax.axis_index("dp")
    j = jnp.where(c == 0, dp // 2 % 2, dp // 4)
    off = c * HALF
    u_part = lax.dynamic_slice(up_weight, (0, off), (D, HALF))
    d_part = lax.dynamic_slice(down_weight, (off, 0), (HALF, D))
    b_part = jnp.broadcast_to(lax.dynamic_slice(up_bias, (off,), (HALF,))[None], (32, HALF))
    halves = [jnp.where(j == 0, u_part[i * HALF : (i + 1) * HALF], d_part[:, i * HALF : (i + 1) * HALF]) for i in range(2)]
    pack = jnp.concatenate([*halves, b_part], axis=0)
    again = jnp.concatenate([*halves, b_part[:16]], axis=0)
    m1 = send(pack, up_ring)
    first_low, down_sum, qkvs, g = make_qkv(pack)
    prob0, att0 = attend(0, qkvs[0], pack)
    m1, att0 = tie(m1, att0)

    m2 = send(m1, up_ring)
    o1 = send(m1, first)
    probs, atts = zip((prob0, att0), *[attend(w, qkvs[w], m1) for w in range(1, windows)])
    x, mid, att = project(atts)
    gx = [*g, *x]
    sib = [send(part, core) for part in gx]
    m2, o1, *sib = tie(m2, o1, *sib)
    m3 = send(tie(again, m2)[0], down_ring)
    rows_of = (g, sib[:windows], x, sib[windows:])

    o2 = send(m2[:D], first)
    acc, keep0, send0, ub0 = mlp((0,), *rows_of, [], [up_weight, down_weight, up_bias], m2)
    acc, both1, ub1 = mlp((1,), *rows_of, [acc], [m1, o1], acc)
    m3, o2, acc = tie(m3, o2, acc)

    o3 = send(m3, first)
    got1 = send(both1, down_ring)
    acc, keep2, send2, ub2 = mlp((2,), *rows_of, [acc], [m2, o2], m3)
    o3, acc = tie(o3, acc)

    f2 = [send(send2[i], first) for i in range(2)]
    mine_back, back, *kept = mlp_front(*rows_of, acc, [m3, o3], o3)
    back_sib = [send(back[w], core) for w in range(windows)]
    mine_out, theirs, keep3, send3, ub3 = mlp_rear(*rows_of, acc, *kept)
    *f2, send3 = tie(*f2, send3)
    mid_grad, dout, proj, sums = norm_two(mine_back, back_sib, mid, att, f2[0])

    f3 = send(send3, first)
    s2_keep, s2_send = adds([(keep2, 0), f2[0]], [(keep2, 1), f2[1]])
    s2 = send(s2_send, second)
    part, rel = heads(0, 0, dout, None, [], dout)
    dqkv = [part]
    for w in range(1, windows):
        part, rel, *weights = heads(0, w, dout, rel, dqkv, dout)
        dqkv.append(part)
    keepq, sendq = weights
    f3, s2, got1, theirs, sendq, rel = tie(f3, s2, got1, theirs, sendq, rel)

    gotq = send(sendq, core)
    a_keep, a_send, s3_keep, s3_send, s2_keep = adds(
        [keep0, (got1, 0)], [send0, (got1, 1)], [(keep3, 0), (f3, 0)], [(keep3, 1), (f3, 1)], [s2_keep, s2])
    s3 = send(s3_send, second)
    got2 = send(s2_keep, far)
    theirs_sib = send(theirs, core)
    q_keep, q_send = adds([(keepq, 0), (gotq, 0)], [(keepq, 1), (gotq, 1)])
    q1 = send(q_send, first)
    for w in range(windows):
        part, rel, *weights = heads(1, w, dout, rel, dqkv[windows:], q_send)
        dqkv.append(part)
    keepr, sendr = weights
    q1, s3, got2, theirs_sib, rel, sendr = tie(q1, s3, got2, theirs_sib, rel, sendr)

    gotr = send(sendr, core)
    r_keep, r_send = adds([(keepr, 0), (gotr, 0)], [(keepr, 1), (gotr, 1)])
    r1 = send(lines(r_send), first)
    q_keep, q_send, s3_keep = adds([(q_keep, 0), (q1, 0)], [(q_keep, 1), (q1, 1)], [s3_keep, s3])
    got3 = send(s3_keep, up_ring)
    q2 = send(lines(q_send), second)
    tokens_grad, tail = norm_one(mid_grad, dqkv, (ub0, ub1, ub2, ub3), down_sum, sums, rel, r_send)
    stretch = [((2 * SMALL_ROWS, HALF), BF16)]
    (tail,) = call(tail_kernel, stretch, [tail, send(tail, core)], us=0.5)
    other = send(tail, first)
    r1, q2, other, got3 = tie(r1, q2, other, got3)

    size = r1.shape[0] // 2
    stay, away = call(second_kernel, [((size, HALF), BF16), ((size + 2 * SMALL_ROWS, HALF), BF16)], [lines(r_keep), r1, tail, other], us=0.5)
    r2 = send(away, second)
    half = q2.shape[0] // 2
    q_stay, q_away = call(halve_kernel, [((half, HALF), BF16)] * 2, [lines(q_keep), q2], us=0.5)
    q3 = send(q_away, near)
    tokens_grad, block_out = outputs(tokens_grad, mine_out, theirs_sib, mid, r1)
    r2, q3, tokens_grad = tie(r2, q3, tokens_grad)
    a1 = send(tie(a_send, r2)[0], first)

    size //= 2
    shapes = [((size, HALF), BF16), ((size + 2 * SMALL_ROWS, HALF), BF16)]
    stay, away = call(near_kernel, shapes, [stay, r2, away], us=0.5)
    r3 = send(away, near)
    (q_stay,) = adds([q_stay, q3])
    q4 = send(q_stay, far)
    r3, q4, a1 = tie(r3, q4, a1)

    (away,) = call(far_kernel, shapes[1:], [stay, r3, away], us=0.5)
    r4 = send(away, far)
    (q_stay,) = adds([q_stay, q4])
    q5 = send(q_stay, near)
    a_keep, a_send = adds([(a_keep, 0), (a1, 0)], [(a_keep, 1), (a1, 1)])
    a2 = send(a_send, second)
    r4, a2 = tie(r4, a2)

    (r_half,) = adds([away[:size], r4[:size]])
    r5 = send(r_half, near)
    mlp_part, = adds([a_keep, a2, got2, got3])
    other = send(mlp_part[:, 1], core)
    kept = mlp_part[:, 0]
    mlp_grads = jnp.where(c == 0, jnp.concatenate([kept, other], axis=2), jnp.concatenate([other, kept], axis=2)).astype(F32)
    vec = lambda n: ((n,), F32)
    table = ((2 * WIN - 1, 64), F32)
    outs = [((96, 3 * D), F32), ((96, D), F32), vec(D), vec(D), vec(2 * D), table, table, vec(D), vec(D), vec(D), vec(4 * D), vec(D)]
    qkv_grad, proj_grad, n1g, n1s, qvb, relh, relw, pb, n2g, n2s, upb, db = call(
        finish_kernel, outs, [r_half, r5, away, r4, q_stay, q5],
        [pltpu.VMEM((SMALL_ROWS, HALF), F32), pltpu.VMEM((3 * 96, HALF), F32), pltpu.VMEM((5 * 96, HALF), F32)], us=2.0)
    return turn(block_out), turn(tokens_grad), n1g, n1s, qkv_grad, qvb, relh, relw, proj_grad, pb, n2g, n2s, mlp_grads[0], upb, mlp_grads[1].T, db


def solution(mesh):
    split_rows = P(AXES, None, None)
    in_specs = (split_rows, P(AXES, None), split_rows) + (P(),) * 10 + (P(None, "mp"), P("mp"), P("mp", None), P())
    out_specs = (split_rows, split_rows, P(), P(), P("dp", None), P(), P(), P(), P("dp", None), P(), P(), P(), P("dp", "mp"), P(), P("mp", "dp"), P())
    return jax.shard_map(local, mesh=mesh, in_specs=in_specs, out_specs=out_specs, check_vma=False)
```

```python
import functools

import jax
import jax.numpy as jnp
from jax import lax
from jax.experimental import pallas as pl
from jax.experimental.pallas import tpu as pltpu
from jax.sharding import PartitionSpec as P

D = 768
HEADS = 12
WIN = 14
PATCH = WIN * WIN
ROWS = 208
PAIRS = HEADS // 2
EPSILON = 1e-06
HALF = 384
F32 = jnp.float32
BF16 = jnp.bfloat16
AXES = ("dp", "mp")
VM = pl.BlockSpec(memory_space=pltpu.VMEM)
SMALL_ROWS = 40


def nn(a, b):
    return lax.dot_general(a, b, (((1,), (0,)), ((), ())), preferred_element_type=F32)


def nt(a, b):
    return lax.dot_general(a, b, (((1,), (1,)), ((), ())), preferred_element_type=F32)


def tn(a, b):
    return lax.dot_general(a, b, (((0,), (0,)), ((), ())), preferred_element_type=F32)


def iota(shape, dim):
    return lax.broadcasted_iota(jnp.int32, shape, dim)


def row(ref):
    return ref[...].astype(F32).reshape(1, -1)


def column_mask(mask_ref, w):
    line = mask_ref[w : w + 1, :].astype(F32)
    here = iota((ROWS, PATCH), 0) == iota((ROWS, PATCH), 1)
    return jnp.sum(jnp.where(here, line, 0.0), axis=1, keepdims=True)


def key_mask(column):
    here = iota((ROWS, ROWS), 0) == iota((ROWS, ROWS), 1)
    return jnp.sum(jnp.where(here, column, 0.0), axis=0, keepdims=True)


def norm(x):
    average = jnp.mean(x, axis=-1, keepdims=True)
    centred = x - average
    variance = jnp.mean(centred * centred, axis=-1, keepdims=True)
    inverse = lax.rsqrt(variance + EPSILON)
    return centred * inverse, inverse


def norm_back(e, n, s, gain):
    scaled = e * gain
    mean_grad = jnp.mean(scaled, axis=-1, keepdims=True)
    mean_proj = jnp.mean(scaled * n, axis=-1, keepdims=True)
    return s * (scaled - mean_grad - n * mean_proj)


def colsum(x):
    return jnp.sum(x, axis=0, keepdims=True)


def fill_tables(table, height_ref, width_ref):
    table[...] = jnp.zeros((128, 128), F32)
    height = height_ref[...].astype(F32)
    width = width_ref[...].astype(F32)
    none = jnp.zeros_like(height)
    rels = 2 * WIN - 1
    table[0:rels, :] = jnp.concatenate([height, none], axis=1)
    table[32 : 32 + rels, :] = jnp.concatenate([width, none], axis=1)
    table[64 : 64 + rels, :] = jnp.concatenate([none, height], axis=1)
    table[96 : 96 + rels, :] = jnp.concatenate([none, width], axis=1)


def shift_bits():
    place = iota((ROWS, 128), 0)
    high = place // WIN
    wide = place - high * WIN
    return jnp.where((iota((ROWS, 128), 1) & 32) == 0, high, wide)


def shift_rows(x, amount, left):
    for bit in range(4):
        step = 1 << bit
        moved = pltpu.roll(x, 128 - step if left else step, 1)
        x = jnp.where((amount & step) != 0, moved, x)
    return x


def one_hot(both):
    place = iota((ROWS, 128), 0)
    lane = iota((ROWS, 128), 1)
    high = place // WIN
    wide = place - high * WIN
    want = jnp.where((lane & 32) == 0, high, wide)
    sub = lane & 31
    slot = (sub & 15) if both else sub
    hit = (slot == (WIN - 1) - want) & (place < PATCH)
    return jnp.where(hit, 1.0, 0.0).astype(BF16)


def qkv_kernel(tok_ref, mask_ref, cot_ref, gain_ref, shift_ref, w_ref, bias_ref, dep, first_ref, sum_ref, *refs):
    windows = tok_ref.shape[0]
    outs, gs, xs = refs[:windows], refs[windows:-1], refs[-1]
    sums = jnp.zeros((1, D), F32)
    gain, shift = row(gain_ref), row(shift_ref)
    xs[ROWS - 16 :, :] = jnp.zeros((16, D), F32)
    for w in range(windows):
        xs[0:PATCH, :] = tok_ref[w].astype(F32)
        n, _ = norm(xs[...])
        first_ref[w * ROWS : (w + 1) * ROWS, :] = (n * gain + shift).astype(BF16)
        xs[0:PATCH, :] = cot_ref[w].astype(F32)
        g = (column_mask(mask_ref, w) * xs[...]).astype(BF16)
        gs[w][...] = g
        sums = sums + colsum(g.astype(F32))
    sum_ref[...] = sums
    bias = row(bias_ref)
    for part in range(3):
        cols = slice(part * D, (part + 1) * D)
        out = nn(first_ref[...], w_ref[:, cols])
        if part == 0:
            out = out + bias[:, :D]
        if part == 2:
            out = out + bias[:, D:]
        for w in range(windows):
            outs[w][:, cols] = out[w * ROWS : (w + 1) * ROWS].astype(BF16)


def attend_kernel(w, mask_ref, qkv_ref, height_ref, width_ref, dep, prob_ref, att_ref, table):
    fill_tables(table, height_ref, width_ref)
    tab = table[...].astype(BF16)
    amount = shift_bits()
    keys_hot = one_hot(True)
    lane = iota((ROWS, 128), 1)
    lower = lane < 64
    sub = lane & 31
    valid = key_mask(column_mask(mask_ref, w)) > 0.5

    def pair(p, carry):
        at = pl.multiple_of(p * 128, 128)
        q = qkv_ref[:, pl.ds(at, 128)]
        k = qkv_ref[:, pl.ds(D + at, 128)]
        v = qkv_ref[:, pl.ds(2 * D + at, 128)]
        terms = shift_rows(nt(q, tab), amount, True)
        coarse = terms.astype(BF16).astype(F32)
        fine = pltpu.roll(terms - coarse, 16, 1)
        terms = jnp.where(sub < WIN, coarse, jnp.where((sub >= 16) & (sub < 16 + WIN), fine, 0.0))
        qs = q.astype(F32) * 0.125
        top = jnp.concatenate([jnp.where(lower, qs, 0.0), jnp.where(lower, terms, 0.0)], axis=1)
        bottom = jnp.concatenate([jnp.where(lower, 0.0, qs), jnp.where(lower, 0.0, terms)], axis=1)
        left = jnp.concatenate([top, bottom], axis=0).astype(BF16)
        right = jnp.concatenate([k, keys_hot], axis=1)
        scores = jnp.where(valid, nt(left, right), -1000000000.0)
        most = jnp.max(scores, axis=1, keepdims=True)
        weight = jnp.exp(scores - most)
        total = jnp.sum(weight, axis=1, keepdims=True)
        prob = (weight * (1.0 / total)).astype(BF16)
        prob_ref[p] = prob
        out = nn(prob, v)
        att_ref[:, pl.ds(at, 128)] = jnp.where(lower, out[:ROWS], out[ROWS:]).astype(BF16)
        return carry

    lax.fori_loop(0, PAIRS, pair, 0, unroll=2)


def project_kernel(tok_ref, mask_ref, w_ref, bias_ref, gain_ref, shift_ref, *refs):
    windows = tok_ref.shape[0]
    atts, lows = refs[:windows], refs[windows : 2 * windows]
    mid_ref, all_ref, xs = refs[2 * windows :]
    gain, shift, bias = row(gain_ref), row(shift_ref), row(bias_ref)
    xs[ROWS - 16 :, :] = jnp.zeros((16, D), F32)
    for w in range(windows):
        all_ref[w * ROWS : (w + 1) * ROWS, :] = atts[w][...]
    out = nn(all_ref[...], w_ref[...]) + bias
    for w in range(windows):
        rows = slice(w * ROWS, (w + 1) * ROWS)
        xs[0:PATCH, :] = tok_ref[w].astype(F32)
        mid = xs[...] + column_mask(mask_ref, w) * out[rows]
        mid_ref[rows, :] = mid
        n, _ = norm(mid)
        lows[w][...] = (n * gain + shift).astype(BF16)


def position(ring):
    dp, z = lax.axis_index("dp"), lax.axis_index("mp")
    c = lax.rem(dp, 2)
    if not ring:
        return c, 0, 0, 0, 0
    y, x = lax.div(dp, 4), lax.rem(lax.div(dp, 2), 2)
    return c, jnp.where(c == 0, x, y), y, x, z


def apart(a, b):
    return a ^ b if isinstance(b, int) else jnp.where(b == a, 0, 1)


def slot_of(ring, block, by_block):
    yb, xb, cb = block // 4, (block // 2) % 2, block % 2
    if not ring:
        return block // 4, (block // 2) % 2, block % 2
    c, _, y, x, _ = position(ring)
    over_y, over_x = apart(yb, y), apart(xb, x)
    if by_block:
        return apart(cb, c), *((over_y, over_x) if cb else (over_x, over_y))
    return apart(cb, c), jnp.where(c == 0, over_x, over_y), jnp.where(c == 0, over_y, over_x)


def load_half(j, k, mine, other, up, down, bias):
    cols = slice(k * HALF, (k + 1) * HALF)
    bias[0:1, cols] = mine[D : D + 16, :].astype(F32)[0:1, :]

    def place(first, second):
        up[:, cols] = first[0:D, :]
        down[cols, 0:HALF] = second[0:HALF, :]
        down[cols, HALF:D] = second[HALF:D, :]

    either(j, lambda: place(mine, other), lambda: place(other, mine))


def hidden(x, g, up, down, bias):
    u = nn(x, up) + bias
    phi = 0.5 + 0.5 * lax.erf(u * 0.7071067811865476)
    slope = phi + u * jnp.exp(-0.5 * u * u) * 0.3989422804014327
    return (u * phi).astype(BF16), (nt(g, down) * slope).astype(BF16)


def weight_grads(ring, spots, grefs, xrefs, hid, pre, outs, ub_ref, grads):
    c, _, _, _, z = position(ring)
    width = len(spots) * HALF
    blocks = [slice(block * ROWS, (block + 1) * ROWS) for block in range(len(xrefs))]
    sums = jnp.zeros((1, width), F32)
    for block in blocks:
        sums = sums + colsum(pre[block, :].astype(F32))
    for which, (left, right) in enumerate(((xrefs, pre), (grefs, hid))):
        total = jnp.zeros((D, width), F32)
        for ref, block in zip(left, blocks):
            total = total + tn(ref[...], right[block, :])
        grads[which] = total.astype(BF16)
    ub_ref[...] = jnp.zeros_like(ub_ref)
    for k, spot in enumerate(spots):
        s = lax.rem(z + 4 - spot, 4) if ring else spot
        ub_ref[pl.ds(2 * s + c, 1), :] = sums[:, k * HALF : (k + 1) * HALF]
    for b in range(8):
        cr, first, second = slot_of(ring, b, False)
        lines = slice(b * 96, (b + 1) * 96)
        for k in range(len(spots)):
            part = slice(k * HALF, (k + 1) * HALF)

            def move(target, cr=cr, second=second, lines=lines, part=part):
                for which in range(2):
                    target[second, which, cr] = grads[which, lines, part]

            if len(outs[k]) == 1:
                move(outs[k][0].at[first])
            else:
                either(first, lambda k=k, move=move: move(outs[k][0]), lambda k=k, move=move: move(outs[k][1]))


def mlp_kernel(ring, spots, windows, *refs):
    refs = list(refs)
    blocks = 2 * windows
    grefs = [refs.pop(0) for _ in range(blocks)]
    xrefs = [refs.pop(0) for _ in range(blocks)]
    c, j, *_ = position(ring)
    if spots[0] == 0:
        acc_in = None
        up_ref, down_ref, upb_ref = (refs.pop(0) for _ in range(3))
    else:
        acc_in = refs.pop(0)
    packs = [(k, refs.pop(0), refs.pop(0)) for k, spot in enumerate(spots) if spot]
    dep, acc = refs.pop(0), refs.pop(0)
    outs = [(refs.pop(0),) if spot == 1 else (refs.pop(0), refs.pop(0)) for spot in spots]
    ub_ref, up, down, bias, hid, pre, grads = refs
    if acc_in is None:
        off = pl.multiple_of(c * HALF, HALF)
        up[:, 0:HALF] = up_ref[:, pl.ds(off, HALF)]
        down[0:HALF, :] = down_ref[pl.ds(off, HALF), :]
        line = row(upb_ref)
        bias[0:1, 0:HALF] = jnp.where(c == 0, line[:, :HALF], line[:, HALF:])
    for k, mine, other in packs:
        load_half(j, k, mine, other, up, down, bias)
    up_c, down_c, bias_c = up[...], down[...], bias[0:1, :]
    for block in range(blocks):
        there = slice(block * ROWS, (block + 1) * ROWS)
        h, pg = hidden(xrefs[block][...], grefs[block][...], up_c, down_c, bias_c)
        hid[there, :] = h
        pre[there, :] = pg
        for which, value in enumerate((nn(h, down_c), nt(pg, up_c))):
            acc[which, there, :] = value if acc_in is None else acc_in[which, there, :] + value
    weight_grads(ring, spots, grefs, xrefs, hid, pre, outs, ub_ref, grads)


def mlp_front_kernel(ring, windows, *refs):
    blocks = 2 * windows
    grefs, xrefs, refs = refs[:blocks], refs[blocks : 2 * blocks], refs[2 * blocks :]
    acc, mine, other, dep, back_ref, tback_ref, hid, pre, down, up, bias = refs
    load_half(position(ring)[1], 0, mine, other, up, down, bias)
    up_c, down_c, bias_c = up[...], down[...], bias[0:1, :]
    for block in range(blocks):
        here = slice((block % windows) * ROWS, (block % windows + 1) * ROWS)
        there = slice(block * ROWS, (block + 1) * ROWS)
        h, pg = hidden(xrefs[block][...], grefs[block][...], up_c, down_c, bias_c)
        hid[there, :] = h
        pre[there, :] = pg
        back = acc[1, there, :] + nt(pg, up_c)
        if block < windows:
            back_ref[here, :] = back
        else:
            tback_ref[block - windows] = back.astype(BF16)


def mlp_rear_kernel(ring, windows, *refs):
    blocks = 2 * windows
    grefs, xrefs, refs = refs[:blocks], refs[blocks : 2 * blocks], refs[2 * blocks :]
    acc, hid, pre, down, out_ref, tout_ref, keep_ref, send_ref, ub_ref, grads = refs
    weight_grads(ring, (3,), grefs, xrefs, hid, pre, [(keep_ref, send_ref)], ub_ref, grads)
    for block in range(blocks):
        here = slice((block % windows) * ROWS, (block % windows + 1) * ROWS)
        there = slice(block * ROWS, (block + 1) * ROWS)
        out = acc[0, there, :] + nn(hid[there, :], down[...])
        if block < windows:
            out_ref[here, :] = out
        else:
            tout_ref[here, :] = out.astype(BF16)


def either(index, zero, one):
    if isinstance(index, int):
        return one() if index else zero()
    pl.when(index == 0)(zero)
    pl.when(index != 0)(one)


def store_blocks(keep_ref, send_ref, ring, index, ref):
    for b in range(8):
        cr, first, second = slot_of(ring, b, True)
        lines = slice(b * 96, (b + 1) * 96)

        def move(target, first=first, second=second, lines=lines):
            target[first, second, index] = ref[lines, :]

        either(cr, lambda move=move: move(keep_ref), lambda move=move: move(send_ref))


def heads_back(p, dout, lower, amount, hot, tab, q, k, v, prob_low, rel):
    none = jnp.zeros_like(dout)
    douts = jnp.concatenate([jnp.where(lower, dout, none), jnp.where(lower, none, dout)], axis=0)
    qs = (q.astype(F32) * 0.125).astype(BF16)
    queries = jnp.concatenate([jnp.where(lower, qs, none), jnp.where(lower, none, qs)], axis=0)
    prob = prob_low.astype(F32)
    dprob = nt(douts, v)
    delta = jnp.sum(prob * dprob, axis=1, keepdims=True)
    dscore = (prob * (dprob - delta)).astype(BF16)
    both = nn(dscore, jnp.concatenate([k, hot], axis=1))
    dq = jnp.where(lower, both[:ROWS, :128], both[ROWS:, :128]) * 0.125
    sums = shift_rows(jnp.where(lower, both[:ROWS, 128:], both[ROWS:, 128:]), amount, False).astype(BF16)
    dq = dq + nn(sums, tab)
    rel[...] += tn(sums, q)
    dk = tn(dscore, queries)
    dv = tn(prob_low, douts)
    return dq, dk, dv


def heads_kernel(ring, w, group, last, dout_ref, qkv_ref, prob_ref, height_ref, width_ref, *refs):
    refs = list(refs)
    rel_in = refs.pop(0) if w or group else None
    before = []
    if last:
        first_ref = refs.pop(0)
        before = [refs.pop(0) for _ in range(w)]
        early = [] if group else [refs.pop(0)]
    dep, dqkv, rel = refs[:3]
    table = refs[-1]
    fill_tables(table, height_ref, width_ref)
    tab = table[...].astype(BF16)
    rel[...] = jnp.zeros_like(rel) if rel_in is None else rel_in[...]
    amount = shift_bits()
    hot = one_hot(False)
    lower = iota((ROWS, 128), 1) < 64
    rows = slice(w * ROWS, (w + 1) * ROWS)
    for step in range(PAIRS // 2):
        p = group * (PAIRS // 2) + step
        at = slice(p * 128, (p + 1) * 128)
        q, k, v = (qkv_ref[:, i * D + p * 128 : i * D + (p + 1) * 128] for i in range(3))
        parts = heads_back(p, dout_ref[rows, at], lower, amount, hot, tab, q, k, v, prob_ref[p], rel)
        for which, value in enumerate(parts):
            dqkv[:, which * HALF + step * 128 : which * HALF + (step + 1) * 128] = value.astype(BF16)
    if last:
        keep_ref, send_ref, grad = refs[3:6]
        for ref in early:
            for which in range(2):
                store_blocks(keep_ref, send_ref, ring, which, ref.at[which])
        for which in range(3):
            cols = slice(which * HALF, (which + 1) * HALF)
            total = tn(first_ref[rows, :], dqkv[:, cols])
            for other, ref in enumerate(before):
                total = total + tn(first_ref[other * ROWS : (other + 1) * ROWS, :], ref[:, cols])
            grad[which] = total.astype(BF16)
            store_blocks(keep_ref, send_ref, ring, 2 * len(early) + which, grad.at[which])


def norm_two_kernel(ring, own_ref, mid_ref, cot_ref, mask_ref, att_ref, projw_ref, gain_ref, *refs):
    sibs, refs = refs[: cot_ref.shape[0]], refs[cot_ref.shape[0] :]
    dep, midg_ref, dout_ref, proj_ref, sum_ref, xs, low = refs
    windows = cot_ref.shape[0]
    gain = row(gain_ref)
    xs[ROWS - 16 :, :] = jnp.zeros((16, D), F32)
    gain_sum = jnp.zeros((1, D), F32)
    shift_sum = jnp.zeros((1, D), F32)
    proj_sum = jnp.zeros((1, D), F32)
    for w in range(windows):
        rows = slice(w * ROWS, (w + 1) * ROWS)
        n, s = norm(mid_ref[rows, :])
        e = own_ref[rows, :] + sibs[w][...].astype(F32)
        gain_sum = gain_sum + colsum(e * n)
        shift_sum = shift_sum + colsum(e)
        xs[0:PATCH, :] = cot_ref[w].astype(F32)
        grad = xs[...] + norm_back(e, n, s, gain)
        midg_ref[rows, :] = grad
        attn = (column_mask(mask_ref, w) * grad).astype(BF16)
        low[rows, :] = attn
        proj_sum = proj_sum + colsum(attn.astype(F32))
    sum_ref[...] = jnp.zeros_like(sum_ref)
    sum_ref[0:1, :] = gain_sum
    sum_ref[1:2, :] = shift_sum
    sum_ref[2:3, :] = proj_sum
    proj_grad = tn(att_ref[...], low[...])
    for half in range(2):
        proj_ref[half] = proj_grad[:, half * HALF : (half + 1) * HALF].astype(BF16)
    dout_ref[...] = nt(low[...], projw_ref[...]).astype(BF16)


def norm_one_kernel(tok_ref, midg_ref, *refs):
    windows = tok_ref.shape[0]
    dqkv, refs = refs[: 2 * windows], refs[2 * windows :]
    w_ref, gain_ref, down_sum_ref, ub0_ref, ub1_ref, ub2_ref, ub3_ref, sum_ref, rel_ref, dep, tokg_ref, tail_ref, xs, small_ref = refs
    gain = row(gain_ref)
    xs[ROWS - 16 :, :] = jnp.zeros((16, D), F32)
    gain_sum = jnp.zeros((1, D), F32)
    shift_sum = jnp.zeros((1, D), F32)
    sums = [jnp.zeros((1, HALF), F32) for _ in range(4)]
    for w in range(windows):
        rows = slice(w * ROWS, (w + 1) * ROWS)
        e = jnp.zeros((ROWS, D), F32)
        for group in range(2):
            grad = dqkv[group * windows + w]
            for which in range(3):
                cols = slice(which * HALF, (which + 1) * HALF)
                at = which * D + group * HALF
                e = e + nt(grad[:, cols], w_ref[:, at : at + HALF])
                if which != 1:
                    sums[which + group] = sums[which + group] + colsum(grad[:, cols].astype(F32))
        xs[0:PATCH, :] = tok_ref[w].astype(F32)
        n, s = norm(xs[...])
        gain_sum = gain_sum + colsum(e * n)
        shift_sum = shift_sum + colsum(e)
        tokg_ref[rows, :] = midg_ref[rows, :] + norm_back(e, n, s, gain)

    small_ref[...] = jnp.zeros_like(small_ref)

    def put(at, value):
        small_ref[at : at + 1, :] = value[:, :HALF]
        small_ref[at + 1 : at + 2, :] = value[:, HALF:]

    put(0, down_sum_ref[...])
    small_ref[2:10, :] = ub0_ref[...] + ub1_ref[...] + ub2_ref[...] + ub3_ref[...]
    for i in range(3):
        put(10 + 2 * i, sum_ref[i : i + 1, :])
    for i in range(4):
        small_ref[16 + i : 17 + i, :] = sums[i]
    put(20, gain_sum)
    put(22, shift_sum)
    both = rel_ref[...]
    heads = both[0:64, 0:64] + both[64:128, 64:128]
    small_ref[24:40, 0:256] = jnp.concatenate([heads[0:16], heads[16:32], heads[32:48], heads[48:64]], axis=1)
    tail_ref[...] = split(small_ref[...])


def outputs_kernel(tokg_ref, mask_ref, own_ref, sib_ref, mid_ref, downb_ref, dep, grad_ref, out_ref):
    windows = mask_ref.shape[0]
    down_bias = row(downb_ref)
    outs = []
    for w in range(windows):
        rows = slice(w * ROWS, (w + 1) * ROWS)
        grad_ref[:, w, :] = tokg_ref[w * ROWS : w * ROWS + PATCH, :]
        mlp_out = own_ref[rows, :] + sib_ref[rows, :].astype(F32)
        outs.append((mid_ref[rows, :] + column_mask(mask_ref, w) * (mlp_out + down_bias))[0:PATCH])
    out_ref[...] = jnp.stack(outs, axis=1).astype(BF16)


def split(x):
    coarse = x.astype(BF16)
    return jnp.concatenate([coarse.astype(F32), x - coarse.astype(F32)], axis=0).astype(BF16)


def join(x):
    half = x.shape[0] // 2
    return x[:half].astype(F32) + x[half:].astype(F32)


def sums_kernel(plan, count, *refs):
    outs = refs[len(refs) - len(plan) :]
    for terms, out in zip(plan, outs):
        total = None
        for which, part in terms:
            value = (refs[which][...] if part is None else refs[which][part]).astype(F32)
            total = value if total is None else total + value
        out[...] = total.astype(out.dtype)


def halve_kernel(keep_ref, got_ref, stay_ref, away_ref):
    size = stay_ref.shape[0]

    def place(mine, other):
        stay_ref[...] = (keep_ref[mine, :].astype(F32) + got_ref[mine, :].astype(F32)).astype(BF16)
        away_ref[0:size, :] = (keep_ref[other, :].astype(F32) + got_ref[other, :].astype(F32)).astype(BF16)

    low, high = slice(0, size), slice(size, 2 * size)
    either(lax.rem(lax.axis_index("mp"), 2), lambda: place(low, high), lambda: place(high, low))


def tail_kernel(tail_ref, got_ref, out_ref):
    out_ref[...] = split(join(tail_ref[...]) + join(got_ref[...]))


def second_kernel(keep_ref, got_ref, tail_ref, other_ref, stay_ref, away_ref):
    size = stay_ref.shape[0]
    stay_ref[...] = (keep_ref[0:size, :].astype(F32) + got_ref[0:size, :].astype(F32)).astype(BF16)
    away_ref[0:size, :] = (keep_ref[size:, :].astype(F32) + got_ref[size:, :].astype(F32)).astype(BF16)
    away_ref[size:, :] = split(join(tail_ref[...]) + join(other_ref[...]))


def near_kernel(keep_ref, got_ref, sent_ref, stay_ref, away_ref):
    halve_kernel(keep_ref, got_ref, stay_ref, away_ref)
    size, tail = stay_ref.shape[0], keep_ref.shape[0]
    away_ref[size:, :] = split(join(sent_ref[tail:, :]) + join(got_ref[tail:, :]))


def far_kernel(keep_ref, got_ref, sent_ref, away_ref):
    size = keep_ref.shape[0]
    away_ref[0:size, :] = (keep_ref[...].astype(F32) + got_ref[0:size, :].astype(F32)).astype(BF16)
    away_ref[size:, :] = split(join(sent_ref[size:, :]) + join(got_ref[size:, :]))


def finish_kernel(own_ref, got_ref, tail_ref, last_ref, stay_ref, away_ref, mlp_ref, other_ref, qkv_ref, proj_ref, up_ref, down_ref, *refs):
    n1g, n1s, qvb, relh, relw, pb, n2g, n2s, upb, db, small, late, early = refs
    odd = lax.rem(lax.axis_index("mp"), 2)

    def place(into, first, second):
        size = first.shape[0]
        into[0:size, :] = first[...].astype(F32)
        into[size:, :] = second[...].astype(F32)

    for into, own, got in ((late, own_ref, got_ref), (early, stay_ref, away_ref)):
        either(odd, lambda into=into, own=own, got=got: place(into, own, got), lambda into=into, own=own, got=got: place(into, got, own))
    low, high = slice(0, HALF), slice(HALF, D)
    for which, ref in enumerate((up_ref, down_ref)):

        def sides(mine, other, which=which, ref=ref):
            ref[:, mine] = mlp_ref[which, 0].astype(F32)
            ref[:, other] = other_ref[which].astype(F32)

        either(position(True)[0], lambda sides=sides: sides(low, high), lambda sides=sides: sides(high, low))
    for half in range(2):
        proj_ref[:, half * HALF : (half + 1) * HALF] = early[half * 96 : (half + 1) * 96, :]
    for which in range(3):
        qkv_ref[:, which * D : which * D + HALF] = early[(2 + which) * 96 : (3 + which) * 96, :]
        qkv_ref[:, which * D + HALF : (which + 1) * D] = late[which * 96 : (which + 1) * 96, :]
    total = jnp.zeros((SMALL_ROWS, HALF), F32)
    for ref in (tail_ref, last_ref):
        at = ref.shape[0] - 2 * SMALL_ROWS
        total = total + (ref[at : at + SMALL_ROWS, :].astype(F32) + ref[at + SMALL_ROWS :, :].astype(F32))
    small[...] = total
    for ref, at, count in ((db, 0, 2), (upb, 2, 8), (n2g, 10, 2), (n2s, 12, 2), (pb, 14, 2), (qvb, 16, 4), (n1g, 20, 2), (n1s, 22, 2)):
        for i in range(count):
            ref[i * HALF : (i + 1) * HALF] = small[at + i : at + i + 1, :].reshape(HALF)
    rels = 2 * WIN - 1
    block = small[24:40, 0:256]
    for ref, at in ((relh, 0), (relw, 128)):
        ref[0:16, :] = block[:, at : at + 64]
        ref[16:rels, :] = block[0 : rels - 16, at + 64 : at + 128]


ANY = pl.BlockSpec(memory_space=pl.ANY)


def call(kernel, outs, ins, scratch=(), us=1.0, after=None, limit=12, aliases=None):
    shapes = tuple(jax.ShapeDtypeStruct(s, d) for s, d in outs)
    moved = sum(x.size * x.dtype.itemsize for x in ins) + sum(jnp.dtype(d).itemsize * functools.reduce(lambda a, b: a * b, s, 1) for s, d in outs)
    specs = [VM] * len(ins)
    if after is not None:
        ins, specs = [*ins, after], [*specs, ANY]
    return pl.pallas_call(
        kernel,
        out_shape=shapes,
        in_specs=specs,
        out_specs=tuple(VM for _ in outs),
        scratch_shapes=list(scratch),
        input_output_aliases=aliases or {},
        compiler_params=pltpu.CompilerParams(vmem_limit_bytes=limit * 2**20),
        cost_estimate=pl.CostEstimate(flops=int(us * 1.15e9), bytes_accessed=moved, transcendentals=0),
    )(*ins)


def tie(*arrays):
    return lax.optimization_barrier(arrays)


def local(tokens, window_mask, out_grad, norm1_gain, norm1_shift, qkv_weight, qv_bias, rel_height, rel_width, proj_weight, proj_bias,
          norm2_gain, norm2_shift, up_weight, up_bias, down_weight, down_bias):
    dpn, mpn = lax.axis_size("dp"), lax.axis_size("mp")
    c = lax.axis_index("dp") % 2
    windows = tokens.shape[0]
    rows = windows * ROWS
    ring = dpn == 8 and mpn == 4

    def send(x, move):
        perm = []
        for d in range(dpn):
            for m in range(mpn):
                nd, nm = move(d, m)
                perm.append((d * mpn + m, nd * mpn + nm))
        return lax.ppermute(x, AXES, perm)

    core = lambda d, m: (d ^ 1, m)
    first = lambda d, m: (d ^ (4 if d & 1 else 2), m)
    second = lambda d, m: (d ^ (2 if d & 1 else 4), m)
    up_ring = lambda d, m: (d, (m + 1) % mpn)
    down_ring = lambda d, m: (d, (m + mpn - 1) % mpn)
    near = lambda d, m: (d, m ^ 1)
    far = lambda d, m: (d, m ^ 2)
    hold = tie if ring else lambda *arrays: arrays
    narrow = pltpu.VMEM((ROWS, D), F32)
    square = pltpu.VMEM((128, 128), F32)

    def make_qkv(after):
        outs = [((rows, D), BF16), ((1, D), F32)] + [((ROWS, 3 * D), BF16)] * windows + [((ROWS, D), BF16)] * windows
        ins = [tokens, window_mask, out_grad, norm1_gain, norm1_shift, qkv_weight, qv_bias]
        res = call(qkv_kernel, outs, ins, [narrow], us=4.5, after=after)
        return res[0], res[1], res[2 : 2 + windows], res[2 + windows :]

    def attend(w, part, after):
        outs = [((PAIRS, 2 * ROWS, ROWS), BF16), ((ROWS, D), BF16)]
        return call(functools.partial(attend_kernel, w), outs, [window_mask, part, rel_height, rel_width], [square], us=0.01 if w else 8.0, after=after)

    def project(atts):
        outs = [((ROWS, D), BF16)] * windows + [((rows, D), F32), ((rows, D), BF16)]
        ins = [tokens, window_mask, proj_weight, proj_bias, norm2_gain, norm2_shift, *atts]
        res = call(project_kernel, outs, ins, [narrow], us=0.01)
        return res[:windows], *res[windows:]

    part = ((2, 2, 2, 96, HALF), BF16)

    def mlp(spots, g, g_sib, x, x_sib, acc, packs, after):
        n = len(spots)
        outs = [((2, 2 * rows, D), F32)]
        for spot in spots:
            outs += [((2, *part[0]), BF16)] if spot == 1 else [part] * 2
        outs += [((8, HALF), F32)]
        scratch = [pltpu.VMEM((D, n * HALF), BF16), pltpu.VMEM((n * HALF, D), BF16), pltpu.VMEM((8, n * HALF), F32),
                   pltpu.VMEM((2 * rows, n * HALF), BF16), pltpu.VMEM((2 * rows, n * HALF), BF16), pltpu.VMEM((2, D, n * HALF), BF16)]
        ins = [*g, *g_sib, *x, *x_sib, *acc, *packs]
        aliases = {4 * windows: 0} if spots[0] else None
        return call(functools.partial(mlp_kernel, ring, spots, windows), outs, ins, scratch, us=0.01, after=after,
                    limit=12 + 6 * n, aliases=aliases)

    def mlp_front(g, g_sib, x, x_sib, acc, packs, after):
        wide = ((2 * rows, HALF), BF16)
        outs = [((rows, D), F32), ((windows, ROWS, D), BF16), wide, wide, ((HALF, D), BF16)]
        return call(functools.partial(mlp_front_kernel, ring, windows), outs, [*g, *g_sib, *x, *x_sib, acc, *packs],
                    [pltpu.VMEM((D, HALF), BF16), pltpu.VMEM((8, HALF), F32)], us=0.01, after=after, limit=16)

    def mlp_rear(g, g_sib, x, x_sib, acc, hid, pre, down):
        outs = [((rows, D), F32), ((rows, D), BF16), part, part, ((8, HALF), F32)]
        return call(functools.partial(mlp_rear_kernel, ring, windows), outs, [*g, *g_sib, *x, *x_sib, acc, hid, pre, down],
                    [pltpu.VMEM((2, D, HALF), BF16)], us=0.01, limit=16)

    def norm_two(mine, sib, mid, att, after):
        outs = [((rows, D), F32), ((rows, D), BF16), ((2, D, HALF), BF16), ((8, D), F32)]
        ins = [mine, mid, out_grad, window_mask, att, proj_weight, norm2_gain, *sib]
        scratch = [narrow, pltpu.VMEM((rows, D), BF16)]
        return call(functools.partial(norm_two_kernel, ring), outs, ins, scratch, us=0.01, after=after)

    def heads(group, w, dout, rel, before, after):
        last = w == windows - 1
        before = before if group else [*before, proj]
        half = ((2, 2, 3 if group else 5, 96, HALF), BF16)
        outs = [((ROWS, 3 * HALF), BF16), ((128, 128), F32)] + ([half, half] if last else [])
        ins = [dout, qkvs[w], probs[w], rel_height, rel_width] + ([rel] if w or group else []) + ([first_low, *before] if last else [])
        scratch = ([pltpu.VMEM((3, D, HALF), BF16)] if last else []) + [square]
        return call(functools.partial(heads_kernel, ring, w, group, last), outs, ins, scratch, us=(6.0 if last else 3.0) if group else 0.01, after=after)

    def norm_one(mid_grad, dqkv, ubs, down_sum, sums, rel, after):
        outs = [((rows, D), F32), ((2 * SMALL_ROWS, HALF), BF16)]
        ins = [tokens, mid_grad, *dqkv, qkv_weight, norm1_gain, down_sum, *ubs, sums, rel]
        return call(norm_one_kernel, outs, ins, [narrow, pltpu.VMEM((SMALL_ROWS, HALF), F32)], us=6.0, after=after)

    def outputs(tokens_grad, mine, sib, mid, after):
        outs = [((PATCH, windows, D), F32), ((PATCH, windows, D), BF16)]
        return call(outputs_kernel, outs, [tokens_grad, window_mask, mine, sib, mid, down_bias], us=2.0, after=after)

    turn = lambda x: lax.transpose(x, (1, 0, 2))

    def adds(*plan, kind=BF16):
        ins, numbered, outs = [], [], []
        for terms in plan:
            row_of = []
            for term in terms:
                array, part = term if isinstance(term, tuple) else (term, None)
                known = [i for i, other in enumerate(ins) if other is array]
                if not known:
                    ins.append(array)
                row_of.append((known[0] if known else len(ins) - 1, part))
            array, part = terms[0] if isinstance(terms[0], tuple) else (terms[0], None)
            outs.append((array.shape if part is None else array.shape[1:] if isinstance(part, int) else (part.stop, *array.shape[1:]), kind))
            numbered.append(row_of)
        return call(functools.partial(sums_kernel, numbered, len(ins)), outs, ins, us=0.5)

    lines = lambda x: x.reshape(-1, HALF)

    if not ring:
        up_all = lax.all_gather(up_weight, "mp", axis=1, tiled=True)
        down_all = lax.all_gather(down_weight, "mp", axis=0, tiled=True)
        bias_all = lax.all_gather(up_bias, "mp", axis=0, tiled=True)
        packs = [up_all[:, :D], down_all[:D], bias_all[:D]]
        for k in range(1, 4):
            off = k * D + c * HALF
            u_part = lax.dynamic_slice(up_all, (0, off), (D, HALF))
            d_part = lax.dynamic_slice(down_all, (off, 0), (HALF, D))
            d_part = jnp.concatenate([d_part[:, :HALF], d_part[:, HALF:]], axis=0)
            b_part = jnp.broadcast_to(lax.dynamic_slice(bias_all, (off,), (HALF,))[None], (16, HALF))
            packs += [jnp.concatenate([u_part, b_part], axis=0), jnp.concatenate([d_part, b_part], axis=0)]
        first_low, down_sum, qkvs, g = make_qkv(packs[2])
        probs, atts = zip(*[attend(w, qkvs[w], first_low) for w in range(windows)])
        x, mid, att = project(atts)
        rows_of = (g, [send(part, core) for part in g], x, [send(part, core) for part in x])
        acc, keep0, send0, ub0 = mlp((0,), *rows_of, [], packs[0:3], mid)
        acc, both1, ub1 = mlp((1,), *rows_of, [acc], packs[3:5], mid)
        acc, keep2, send2, ub2 = mlp((2,), *rows_of, [acc], packs[5:7], mid)
        mine_back, back, *kept = mlp_front(*rows_of, acc, packs[7:9], mid)
        mine_out, theirs, keep3, send3, ub3 = mlp_rear(*rows_of, acc, *kept)
        mid_grad, dout, proj, sums = norm_two(mine_back, [send(back[w], core) for w in range(windows)], mid, att, mid)
        dqkv, kept, sent, rel = [], [], [], None
        for group in range(2):
            for w in range(windows):
                part, rel, *weights = heads(group, w, dout, rel, dqkv[group * windows :], mid_grad)
                dqkv.append(part)
            kept.append(weights[0])
            sent.append(weights[1])
        tokens_grad, small = norm_one(mid_grad, dqkv, (ub0, ub1, ub2, ub3), down_sum, sums, rel, mid_grad)
        tokens_grad, block_out = (turn(x) for x in outputs(tokens_grad, mine_out, send(theirs, core), mid, mid))
        dw = jnp.stack([jnp.stack([keep0, both1[0], keep2, keep3]), jnp.stack([send0, both1[1], send2, send3])])
        halves = dw.transpose(4, 0, 2, 5, 3, 1, 6).reshape(D, 2, 4, HALF)
        full = jnp.zeros((D, 2, 4, 2, HALF), BF16)
        full = lax.dynamic_update_slice(full, halves[:, :, :, None], (0, 0, 0, c, 0)).reshape(D, 2, 4 * D)
        full = lax.psum_scatter(full, "dp", scatter_dimension=0, tiled=True)
        full = lax.psum_scatter(full, "mp", scatter_dimension=2, tiled=True).astype(F32)
        up_grad, down_grad = full[:, 0], full[:, 1].T
        weights = jnp.stack([jnp.concatenate(kept, axis=2), jnp.concatenate(sent, axis=2)])
        weights = weights.transpose(0, 1, 2, 4, 3, 5).reshape(D, 8 * HALF)
        weights = lax.psum(weights, "mp")
        weights = lax.psum_scatter(weights, "dp", scatter_dimension=0, tiled=True).astype(F32)
        parts = [weights[:, i * HALF : (i + 1) * HALF] for i in range(8)]
        proj_grad = jnp.concatenate(parts[0:2], axis=1)
        qkv_grad = jnp.concatenate([parts[2], parts[5], parts[3], parts[6], parts[4], parts[7]], axis=1)
        small = lax.psum(join(small), AXES)
        vec = lambda start, count: small[start : start + count].reshape(count * HALF)
        table = small[24:40, 0:256].reshape(16, 4, 64).transpose(1, 0, 2).reshape(64, 64)
        rels = 2 * WIN - 1
        return (
            block_out, tokens_grad, vec(20, 2), vec(22, 2), qkv_grad, vec(16, 4), table[0:rels], table[32 : 32 + rels], proj_grad,
            vec(14, 2), vec(10, 2), vec(12, 2), up_grad, vec(2, 8), down_grad, vec(0, 2),
        )

    dp = lax.axis_index("dp")
    j = jnp.where(c == 0, dp // 2 % 2, dp // 4)
    off = c * HALF
    u_part = lax.dynamic_slice(up_weight, (0, off), (D, HALF))
    d_part = lax.dynamic_slice(down_weight, (off, 0), (HALF, D))
    b_part = jnp.broadcast_to(jnp.where(c == 0, up_bias[:HALF], up_bias[HALF:])[None], (32, HALF))
    halves = [jnp.where(j == 0, u_part[i * HALF : (i + 1) * HALF], d_part[:, i * HALF : (i + 1) * HALF]) for i in range(2)]
    pack = jnp.concatenate([*halves, b_part], axis=0)
    again = jnp.concatenate([*halves, b_part[:16]], axis=0)
    m1 = send(pack, up_ring)
    first_low, down_sum, qkvs, g = make_qkv(pack)
    prob0, att0 = attend(0, qkvs[0], pack)
    m1, att0 = tie(m1, att0)

    m2 = send(m1, up_ring)
    o1 = send(m1, first)
    probs, atts = zip((prob0, att0), *[attend(w, qkvs[w], m1) for w in range(1, windows)])
    x, mid, att = project(atts)
    gx = [*g, *x]
    sib = [send(part, core) for part in gx]
    m2, o1, *sib = tie(m2, o1, *sib)
    m3 = send(tie(again, m2)[0], down_ring)
    rows_of = (g, sib[:windows], x, sib[windows:])

    o2 = send(m2[:D], first)
    acc, keep0, send0, ub0 = mlp((0,), *rows_of, [], [up_weight, down_weight, up_bias], m2)
    acc, both1, ub1 = mlp((1,), *rows_of, [acc], [m1, o1], acc)
    m3, o2, acc = tie(m3, o2, acc)

    o3 = send(m3, first)
    got1 = send(both1, down_ring)
    acc, keep2, send2, ub2 = mlp((2,), *rows_of, [acc], [m2, o2], m3)
    o3, acc = tie(o3, acc)

    f2 = [send(send2[i], first) for i in range(2)]
    mine_back, back, *kept = mlp_front(*rows_of, acc, [m3, o3], o3)
    back_sib = [send(back[w], core) for w in range(windows)]
    mine_out, theirs, keep3, send3, ub3 = mlp_rear(*rows_of, acc, *kept)
    *f2, send3 = tie(*f2, send3)
    mid_grad, dout, proj, sums = norm_two(mine_back, back_sib, mid, att, f2[0])

    f3 = send(send3, first)
    s2_keep, s2_send = adds([(keep2, 0), f2[0]], [(keep2, 1), f2[1]])
    s2 = send(s2_send, second)
    part, rel = heads(0, 0, dout, None, [], dout)
    dqkv = [part]
    for w in range(1, windows):
        part, rel, *weights = heads(0, w, dout, rel, dqkv, dout)
        dqkv.append(part)
    keepq, sendq = weights
    f3, s2, got1, theirs, sendq, rel = tie(f3, s2, got1, theirs, sendq, rel)

    gotq = send(sendq, core)
    a_keep, a_send, s3_keep, s3_send, s2_keep = adds(
        [keep0, (got1, 0)], [send0, (got1, 1)], [(keep3, 0), (f3, 0)], [(keep3, 1), (f3, 1)], [s2_keep, s2])
    s3 = send(s3_send, second)
    got2 = send(s2_keep, far)
    theirs_sib = send(theirs, core)
    q_keep, q_send = adds([(keepq, 0), (gotq, 0)], [(keepq, 1), (gotq, 1)])
    q1 = send(q_send, first)
    for w in range(windows):
        part, rel, *weights = heads(1, w, dout, rel, dqkv[windows:], q_send)
        dqkv.append(part)
    keepr, sendr = weights
    q1, s3, got2, theirs_sib, rel, sendr = tie(q1, s3, got2, theirs_sib, rel, sendr)

    gotr = send(sendr, core)
    r_keep, r_send = adds([(keepr, 0), (gotr, 0)], [(keepr, 1), (gotr, 1)])
    r1 = send(lines(r_send), first)
    q_keep, q_send, s3_keep = adds([(q_keep, 0), (q1, 0)], [(q_keep, 1), (q1, 1)], [s3_keep, s3])
    got3 = send(s3_keep, up_ring)
    q2 = send(lines(q_send), second)
    tokens_grad, tail = norm_one(mid_grad, dqkv, (ub0, ub1, ub2, ub3), down_sum, sums, rel, r_send)
    stretch = [((2 * SMALL_ROWS, HALF), BF16)]
    (tail,) = call(tail_kernel, stretch, [tail, send(tail, core)], us=0.5)
    other = send(tail, first)
    r1, q2, other, got3 = tie(r1, q2, other, got3)

    size = r1.shape[0] // 2
    stay, away = call(second_kernel, [((size, HALF), BF16), ((size + 2 * SMALL_ROWS, HALF), BF16)], [lines(r_keep), r1, tail, other], us=0.5)
    r2 = send(away, second)
    half = q2.shape[0] // 2
    q_stay, q_away = call(halve_kernel, [((half, HALF), BF16)] * 2, [lines(q_keep), q2], us=0.5)
    q3 = send(q_away, near)
    tokens_grad, block_out = outputs(tokens_grad, mine_out, theirs_sib, mid, r1)
    r2, q3, tokens_grad = tie(r2, q3, tokens_grad)
    a1 = send(tie(a_send, r2)[0], first)

    size //= 2
    shapes = [((size, HALF), BF16), ((size + 2 * SMALL_ROWS, HALF), BF16)]
    stay, away = call(near_kernel, shapes, [stay, r2, away], us=0.5)
    r3 = send(away, near)
    (q_stay,) = adds([q_stay, q3])
    q4 = send(q_stay, far)
    r3, q4, a1 = tie(r3, q4, a1)

    (away,) = call(far_kernel, shapes[1:], [stay, r3, away], us=0.5)
    r4 = send(away, far)
    (q_stay,) = adds([q_stay, q4])
    q5 = send(q_stay, near)
    a_keep, a_send = adds([(a_keep, 0), (a1, 0)], [(a_keep, 1), (a1, 1)])
    a2 = send(a_send, second)
    r4, a2 = tie(r4, a2)

    (r_half,) = adds([(away, slice(0, size)), (r4, slice(0, size))])
    a2, r_half = tie(a2, r_half)
    r5 = send(r_half, near)
    mlp_part, = adds([a_keep, a2, got2, got3])
    other = send(mlp_part[:, 1], core)
    vec = lambda n: ((n,), F32)
    table = ((2 * WIN - 1, 64), F32)
    outs = [((96, 3 * D), F32)] + [((96, D), F32)] * 3 + [vec(D), vec(D), vec(2 * D), table, table, vec(D), vec(D), vec(D), vec(4 * D), vec(D)]
    qkv_grad, proj_grad, up_grad, down_grad, n1g, n1s, qvb, relh, relw, pb, n2g, n2s, upb, db = call(
        finish_kernel, outs, [r_half, r5, away, r4, q_stay, q5, mlp_part, other],
        [pltpu.VMEM((SMALL_ROWS, HALF), F32), pltpu.VMEM((3 * 96, HALF), F32), pltpu.VMEM((5 * 96, HALF), F32)], us=2.0)
    return turn(block_out), turn(tokens_grad), n1g, n1s, qkv_grad, qvb, relh, relw, proj_grad, pb, n2g, n2s, up_grad, upb, down_grad.T, db


def solution(mesh):
    split_rows = P(AXES, None, None)
    in_specs = (split_rows, P(AXES, None), split_rows) + (P(),) * 10 + (P(None, "mp"), P("mp"), P("mp", None), P())
    out_specs = (split_rows, split_rows, P(), P(), P("dp", None), P(), P(), P(), P("dp", None), P(), P(), P(), P("dp", "mp"), P(), P("mp", "dp"), P())
    return jax.shard_map(local, mesh=mesh, in_specs=in_specs, out_specs=out_specs, check_vma=False)
```

```python
import functools

import jax
import jax.numpy as jnp
from jax import lax
from jax.experimental import pallas as pl
from jax.experimental.pallas import tpu as pltpu
from jax.sharding import PartitionSpec as P

D = 768
HEADS = 12
WIN = 14
PATCH = WIN * WIN
ROWS = 208
PAIRS = HEADS // 2
EPSILON = 1e-06
HALF = 384
F32 = jnp.float32
BF16 = jnp.bfloat16
AXES = ("dp", "mp")
VM = pl.BlockSpec(memory_space=pltpu.VMEM)
SMALL_ROWS = 48


def nn(a, b):
    return lax.dot_general(a, b, (((1,), (0,)), ((), ())), preferred_element_type=F32)


def nt(a, b):
    return lax.dot_general(a, b, (((1,), (1,)), ((), ())), preferred_element_type=F32)


def tn(a, b):
    return lax.dot_general(a, b, (((0,), (0,)), ((), ())), preferred_element_type=F32)


def iota(shape, dim):
    return lax.broadcasted_iota(jnp.int32, shape, dim)


def row(ref):
    return ref[...].astype(F32).reshape(1, -1)


def column_mask(mask_ref, w):
    line = mask_ref[w : w + 1, :].astype(F32)
    here = iota((ROWS, PATCH), 0) == iota((ROWS, PATCH), 1)
    return jnp.sum(jnp.where(here, line, 0.0), axis=1, keepdims=True)


def key_mask(column):
    here = iota((ROWS, ROWS), 0) == iota((ROWS, ROWS), 1)
    return jnp.sum(jnp.where(here, column, 0.0), axis=0, keepdims=True)


def norm(x):
    average = jnp.mean(x, axis=-1, keepdims=True)
    centred = x - average
    variance = jnp.mean(centred * centred, axis=-1, keepdims=True)
    inverse = lax.rsqrt(variance + EPSILON)
    return centred * inverse, inverse


def norm_back(e, n, s, gain):
    scaled = e * gain
    mean_grad = jnp.mean(scaled, axis=-1, keepdims=True)
    mean_proj = jnp.mean(scaled * n, axis=-1, keepdims=True)
    return s * (scaled - mean_grad - n * mean_proj)


def colsum(x):
    return jnp.sum(x, axis=0, keepdims=True)


def fill_tables(table, height_ref, width_ref):
    table[...] = jnp.zeros((128, 128), F32)
    height = height_ref[...].astype(F32)
    width = width_ref[...].astype(F32)
    none = jnp.zeros_like(height)
    rels = 2 * WIN - 1
    table[0:rels, :] = jnp.concatenate([height, none], axis=1)
    table[32 : 32 + rels, :] = jnp.concatenate([width, none], axis=1)
    table[64 : 64 + rels, :] = jnp.concatenate([none, height], axis=1)
    table[96 : 96 + rels, :] = jnp.concatenate([none, width], axis=1)


def shift_bits():
    place = iota((ROWS, 128), 0)
    high = place // WIN
    wide = place - high * WIN
    return jnp.where((iota((ROWS, 128), 1) & 32) == 0, high, wide)


def shift_rows(x, amount, left):
    for bit in range(4):
        step = 1 << bit
        moved = pltpu.roll(x, 128 - step if left else step, 1)
        x = jnp.where((amount & step) != 0, moved, x)
    return x


def one_hot(both):
    place = iota((ROWS, 128), 0)
    lane = iota((ROWS, 128), 1)
    high = place // WIN
    wide = place - high * WIN
    want = jnp.where((lane & 32) == 0, high, wide)
    sub = lane & 31
    slot = (sub & 15) if both else sub
    hit = (slot == (WIN - 1) - want) & (place < PATCH)
    return jnp.where(hit, 1.0, 0.0).astype(BF16)


def qkv_kernel(tok_ref, mask_ref, cot_ref, gain_ref, shift_ref, w_ref, bias_ref, dep, first_ref, sum_ref, *refs):
    windows = tok_ref.shape[0]
    outs, gs, xs = refs[:windows], refs[windows:-1], refs[-1]
    sums = jnp.zeros((1, D), F32)
    gain, shift = row(gain_ref), row(shift_ref)
    xs[ROWS - 16 :, :] = jnp.zeros((16, D), F32)
    for w in range(windows):
        xs[0:PATCH, :] = tok_ref[w].astype(F32)
        n, _ = norm(xs[...])
        first_ref[w * ROWS : (w + 1) * ROWS, :] = (n * gain + shift).astype(BF16)
        xs[0:PATCH, :] = cot_ref[w].astype(F32)
        g = (column_mask(mask_ref, w) * xs[...]).astype(BF16)
        gs[w][...] = g
        sums = sums + colsum(g.astype(F32))
    sum_ref[...] = sums
    bias = row(bias_ref)
    for part in range(3):
        cols = slice(part * D, (part + 1) * D)
        out = nn(first_ref[...], w_ref[:, cols])
        if part == 0:
            out = out + bias[:, :D]
        if part == 2:
            out = out + bias[:, D:]
        for w in range(windows):
            outs[w][:, cols] = out[w * ROWS : (w + 1) * ROWS].astype(BF16)


def attend_kernel(w, mask_ref, qkv_ref, height_ref, width_ref, dep, prob_ref, att_ref, table):
    fill_tables(table, height_ref, width_ref)
    tab = table[...].astype(BF16)
    amount = shift_bits()
    keys_hot = one_hot(True)
    lane = iota((ROWS, 128), 1)
    lower = lane < 64
    sub = lane & 31
    valid = key_mask(column_mask(mask_ref, w)) > 0.5

    def pair(p, carry):
        at = pl.multiple_of(p * 128, 128)
        q = qkv_ref[:, pl.ds(at, 128)]
        k = qkv_ref[:, pl.ds(D + at, 128)]
        v = qkv_ref[:, pl.ds(2 * D + at, 128)]
        terms = shift_rows(nt(q, tab), amount, True)
        coarse = terms.astype(BF16).astype(F32)
        fine = pltpu.roll(terms - coarse, 16, 1)
        terms = jnp.where(sub < WIN, coarse, jnp.where((sub >= 16) & (sub < 16 + WIN), fine, 0.0))
        qs = q.astype(F32) * 0.125
        top = jnp.concatenate([jnp.where(lower, qs, 0.0), jnp.where(lower, terms, 0.0)], axis=1)
        bottom = jnp.concatenate([jnp.where(lower, 0.0, qs), jnp.where(lower, 0.0, terms)], axis=1)
        left = jnp.concatenate([top, bottom], axis=0).astype(BF16)
        right = jnp.concatenate([k, keys_hot], axis=1)
        scores = jnp.where(valid, nt(left, right), -1000000000.0)
        most = jnp.max(scores, axis=1, keepdims=True)
        weight = jnp.exp(scores - most)
        total = jnp.sum(weight, axis=1, keepdims=True)
        prob = (weight * (1.0 / total)).astype(BF16)
        prob_ref[p] = prob
        out = nn(prob, v)
        att_ref[:, pl.ds(at, 128)] = jnp.where(lower, out[:ROWS], out[ROWS:]).astype(BF16)
        return carry

    lax.fori_loop(0, PAIRS, pair, 0, unroll=2)


def project_kernel(tok_ref, mask_ref, w_ref, bias_ref, gain_ref, shift_ref, *refs):
    windows = tok_ref.shape[0]
    atts, lows = refs[:windows], refs[windows : 2 * windows]
    mid_ref, all_ref, xs = refs[2 * windows :]
    gain, shift, bias = row(gain_ref), row(shift_ref), row(bias_ref)
    xs[ROWS - 16 :, :] = jnp.zeros((16, D), F32)
    for w in range(windows):
        all_ref[w * ROWS : (w + 1) * ROWS, :] = atts[w][...]
    out = nn(all_ref[...], w_ref[...]) + bias
    for w in range(windows):
        rows = slice(w * ROWS, (w + 1) * ROWS)
        xs[0:PATCH, :] = tok_ref[w].astype(F32)
        mid = xs[...] + column_mask(mask_ref, w) * out[rows]
        mid_ref[rows, :] = mid
        n, _ = norm(mid)
        lows[w][...] = (n * gain + shift).astype(BF16)


def position(ring):
    dp, z = lax.axis_index("dp"), lax.axis_index("mp")
    c = lax.rem(dp, 2)
    if not ring:
        return c, 0, 0, 0, 0
    y, x = lax.div(dp, 4), lax.rem(lax.div(dp, 2), 2)
    return c, jnp.where(c == 0, x, y), y, x, z


def apart(a, b):
    return a ^ b if isinstance(b, int) else jnp.where(b == a, 0, 1)


def slot_of(ring, block, by_block):
    yb, xb, cb = block // 4, (block // 2) % 2, block % 2
    if not ring:
        return block // 4, (block // 2) % 2, block % 2
    c, _, y, x, _ = position(ring)
    over_y, over_x = apart(yb, y), apart(xb, x)
    if by_block:
        return apart(cb, c), *((over_y, over_x) if cb else (over_x, over_y))
    return apart(cb, c), jnp.where(c == 0, over_x, over_y), jnp.where(c == 0, over_y, over_x)


def load_half(j, k, mine, other, up, down, bias):
    cols = slice(k * HALF, (k + 1) * HALF)
    bias[0:1, cols] = mine[D : D + 16, :].astype(F32)[0:1, :]

    def place(first, second):
        up[:, cols] = first[0:D, :]
        down[cols, 0:HALF] = second[0:HALF, :]
        down[cols, HALF:D] = second[HALF:D, :]

    either(j, lambda: place(mine, other), lambda: place(other, mine))


def hidden(x, g, up, down, bias):
    u = nn(x, up) + bias
    phi = 0.5 + 0.5 * lax.erf(u * 0.7071067811865476)
    slope = phi + u * jnp.exp(-0.5 * u * u) * 0.3989422804014327
    return (u * phi).astype(BF16), (nt(g, down) * slope).astype(BF16)


def weight_grads(ring, spots, grefs, xrefs, hid, pre, outs, ub_ref, grads):
    c, _, _, _, z = position(ring)
    width = len(spots) * HALF
    blocks = [slice(block * ROWS, (block + 1) * ROWS) for block in range(len(xrefs))]
    sums = jnp.zeros((1, width), F32)
    for block in blocks:
        sums = sums + colsum(pre[block, :].astype(F32))
    for which, (left, right) in enumerate(((xrefs, pre), (grefs, hid))):
        total = jnp.zeros((D, width), F32)
        for ref, block in zip(left, blocks):
            total = total + tn(ref[...], right[block, :])
        grads[which] = total.astype(BF16)
    ub_ref[...] = jnp.zeros_like(ub_ref)
    for k, spot in enumerate(spots):
        s = lax.rem(z + 4 - spot, 4) if ring else spot
        ub_ref[pl.ds(2 * s + c, 1), :] = sums[:, k * HALF : (k + 1) * HALF]
    for b in range(8):
        cr, first, second = slot_of(ring, b, False)
        lines = slice(b * 96, (b + 1) * 96)
        for k in range(len(spots)):
            part = slice(k * HALF, (k + 1) * HALF)

            def move(target, cr=cr, second=second, lines=lines, part=part):
                for which in range(2):
                    target[second, which, cr] = grads[which, lines, part]

            if len(outs[k]) == 1:
                move(outs[k][0].at[first])
            else:
                either(first, lambda k=k, move=move: move(outs[k][0]), lambda k=k, move=move: move(outs[k][1]))


def mlp_kernel(ring, spots, windows, *refs):
    refs = list(refs)
    blocks = 2 * windows
    grefs = [refs.pop(0) for _ in range(blocks)]
    xrefs = [refs.pop(0) for _ in range(blocks)]
    c, j, *_ = position(ring)
    if spots[0] == 0:
        acc_in = None
        up_ref, down_ref, upb_ref = (refs.pop(0) for _ in range(3))
    else:
        acc_in = refs.pop(0)
    packs = [(k, refs.pop(0), refs.pop(0)) for k, spot in enumerate(spots) if spot]
    dep, acc = refs.pop(0), refs.pop(0)
    outs = [(refs.pop(0),) if spot == 1 else (refs.pop(0), refs.pop(0)) for spot in spots]
    ub_ref, up, down, bias, hid, pre, grads = refs
    if acc_in is None:
        off = pl.multiple_of(c * HALF, HALF)
        up[:, 0:HALF] = up_ref[:, pl.ds(off, HALF)]
        down[0:HALF, :] = down_ref[pl.ds(off, HALF), :]
        line = row(upb_ref)
        bias[0:1, 0:HALF] = jnp.where(c == 0, line[:, :HALF], line[:, HALF:])
    for k, mine, other in packs:
        load_half(j, k, mine, other, up, down, bias)
    up_c, down_c, bias_c = up[...], down[...], bias[0:1, :]
    for block in range(blocks):
        there = slice(block * ROWS, (block + 1) * ROWS)
        h, pg = hidden(xrefs[block][...], grefs[block][...], up_c, down_c, bias_c)
        hid[there, :] = h
        pre[there, :] = pg
        for which, value in enumerate((nn(h, down_c), nt(pg, up_c))):
            acc[which, there, :] = value if acc_in is None else acc_in[which, there, :] + value
    weight_grads(ring, spots, grefs, xrefs, hid, pre, outs, ub_ref, grads)


def mlp_front_kernel(ring, windows, *refs):
    blocks = 2 * windows
    grefs, xrefs, refs = refs[:blocks], refs[blocks : 2 * blocks], refs[2 * blocks :]
    acc, mine, other, dep, back_ref, tback_ref, hid, pre, down, up, bias = refs
    load_half(position(ring)[1], 0, mine, other, up, down, bias)
    up_c, down_c, bias_c = up[...], down[...], bias[0:1, :]
    for block in range(blocks):
        here = slice((block % windows) * ROWS, (block % windows + 1) * ROWS)
        there = slice(block * ROWS, (block + 1) * ROWS)
        h, pg = hidden(xrefs[block][...], grefs[block][...], up_c, down_c, bias_c)
        hid[there, :] = h
        pre[there, :] = pg
        back = acc[1, there, :] + nt(pg, up_c)
        if block < windows:
            back_ref[here, :] = back
        else:
            tback_ref[block - windows] = back.astype(BF16)


def mlp_rear_kernel(ring, windows, *refs):
    blocks = 2 * windows
    grefs, xrefs, refs = refs[:blocks], refs[blocks : 2 * blocks], refs[2 * blocks :]
    acc, hid, pre, down, out_ref, tout_ref, keep_ref, send_ref, ub_ref, grads = refs
    weight_grads(ring, (3,), grefs, xrefs, hid, pre, [(keep_ref, send_ref)], ub_ref, grads)
    for block in range(blocks):
        here = slice((block % windows) * ROWS, (block % windows + 1) * ROWS)
        there = slice(block * ROWS, (block + 1) * ROWS)
        out = acc[0, there, :] + nn(hid[there, :], down[...])
        if block < windows:
            out_ref[here, :] = out
        else:
            tout_ref[here, :] = out.astype(BF16)


def either(index, zero, one):
    if isinstance(index, int):
        return one() if index else zero()
    pl.when(index == 0)(zero)
    pl.when(index != 0)(one)


def store_blocks(keep_ref, send_ref, ring, index, ref):
    for b in range(8):
        cr, first, second = slot_of(ring, b, True)
        lines = slice(b * 96, (b + 1) * 96)

        def move(target, first=first, second=second, lines=lines):
            target[first, second, index] = ref[lines, :]

        either(cr, lambda move=move: move(keep_ref), lambda move=move: move(send_ref))


def heads_back(p, dout, lower, amount, hot, tab, q, k, v, prob_low, rel):
    none = jnp.zeros_like(dout)
    douts = jnp.concatenate([jnp.where(lower, dout, none), jnp.where(lower, none, dout)], axis=0)
    qs = (q.astype(F32) * 0.125).astype(BF16)
    queries = jnp.concatenate([jnp.where(lower, qs, none), jnp.where(lower, none, qs)], axis=0)
    prob = prob_low.astype(F32)
    dprob = nt(douts, v)
    delta = jnp.sum(prob * dprob, axis=1, keepdims=True)
    dscore = (prob * (dprob - delta)).astype(BF16)
    both = nn(dscore, jnp.concatenate([k, hot], axis=1))
    dq = jnp.where(lower, both[:ROWS, :128], both[ROWS:, :128]) * 0.125
    sums = shift_rows(jnp.where(lower, both[:ROWS, 128:], both[ROWS:, 128:]), amount, False).astype(BF16)
    dq = dq + nn(sums, tab)
    rel[...] += tn(sums, q)
    dk = tn(dscore, queries)
    dv = tn(prob_low, douts)
    return dq, dk, dv


def heads_kernel(ring, w, group, last, dout_ref, qkv_ref, prob_ref, height_ref, width_ref, *refs):
    refs = list(refs)
    rel_in = refs.pop(0) if w or group else None
    before = []
    if last:
        first_ref = refs.pop(0)
        before = [refs.pop(0) for _ in range(w)]
        early = [] if group else [refs.pop(0)]
    dep, dqkv, rel = refs[:3]
    table = refs[-1]
    fill_tables(table, height_ref, width_ref)
    tab = table[...].astype(BF16)
    rel[...] = jnp.zeros_like(rel) if rel_in is None else rel_in[...]
    amount = shift_bits()
    hot = one_hot(False)
    lower = iota((ROWS, 128), 1) < 64
    rows = slice(w * ROWS, (w + 1) * ROWS)
    for step in range(PAIRS // 2):
        p = group * (PAIRS // 2) + step
        at = slice(p * 128, (p + 1) * 128)
        q, k, v = (qkv_ref[:, i * D + p * 128 : i * D + (p + 1) * 128] for i in range(3))
        parts = heads_back(p, dout_ref[rows, at], lower, amount, hot, tab, q, k, v, prob_ref[p], rel)
        for which, value in enumerate(parts):
            dqkv[:, which * HALF + step * 128 : which * HALF + (step + 1) * 128] = value.astype(BF16)
    if last:
        keep_ref, send_ref, grad = refs[3:6]
        for ref in early:
            for which in range(2):
                store_blocks(keep_ref, send_ref, ring, which, ref.at[which])
        for which in range(3):
            cols = slice(which * HALF, (which + 1) * HALF)
            total = tn(first_ref[rows, :], dqkv[:, cols])
            for other, ref in enumerate(before):
                total = total + tn(first_ref[other * ROWS : (other + 1) * ROWS, :], ref[:, cols])
            grad[which] = total.astype(BF16)
            store_blocks(keep_ref, send_ref, ring, 2 * len(early) + which, grad.at[which])


def norm_two_kernel(ring, own_ref, mid_ref, cot_ref, mask_ref, att_ref, projw_ref, gain_ref, *refs):
    sibs, refs = refs[: cot_ref.shape[0]], refs[cot_ref.shape[0] :]
    dep, midg_ref, dout_ref, proj_ref, sum_ref, xs, low = refs
    windows = cot_ref.shape[0]
    gain = row(gain_ref)
    xs[ROWS - 16 :, :] = jnp.zeros((16, D), F32)
    gain_sum = jnp.zeros((1, D), F32)
    shift_sum = jnp.zeros((1, D), F32)
    proj_sum = jnp.zeros((1, D), F32)
    for w in range(windows):
        rows = slice(w * ROWS, (w + 1) * ROWS)
        n, s = norm(mid_ref[rows, :])
        e = own_ref[rows, :] + sibs[w][...].astype(F32)
        gain_sum = gain_sum + colsum(e * n)
        shift_sum = shift_sum + colsum(e)
        xs[0:PATCH, :] = cot_ref[w].astype(F32)
        grad = xs[...] + norm_back(e, n, s, gain)
        midg_ref[rows, :] = grad
        attn = (column_mask(mask_ref, w) * grad).astype(BF16)
        low[rows, :] = attn
        proj_sum = proj_sum + colsum(attn.astype(F32))
    sum_ref[...] = jnp.zeros_like(sum_ref)
    sum_ref[0:1, :] = gain_sum
    sum_ref[1:2, :] = shift_sum
    sum_ref[2:3, :] = proj_sum
    proj_grad = tn(att_ref[...], low[...])
    for half in range(2):
        proj_ref[half] = proj_grad[:, half * HALF : (half + 1) * HALF].astype(BF16)
    dout_ref[...] = nt(low[...], projw_ref[...]).astype(BF16)


def norm_one_kernel(tok_ref, midg_ref, *refs):
    windows = tok_ref.shape[0]
    dqkv, refs = refs[: 2 * windows], refs[2 * windows :]
    w_ref, gain_ref, down_sum_ref, ub0_ref, ub1_ref, ub2_ref, ub3_ref, sum_ref, rel_ref, dep, tokg_ref, tail_ref, xs, small_ref = refs
    gain = row(gain_ref)
    xs[ROWS - 16 :, :] = jnp.zeros((16, D), F32)
    gain_sum = jnp.zeros((1, D), F32)
    shift_sum = jnp.zeros((1, D), F32)
    sums = [jnp.zeros((1, HALF), F32) for _ in range(4)]
    for w in range(windows):
        rows = slice(w * ROWS, (w + 1) * ROWS)
        e = jnp.zeros((ROWS, D), F32)
        for group in range(2):
            grad = dqkv[group * windows + w]
            for which in range(3):
                cols = slice(which * HALF, (which + 1) * HALF)
                at = which * D + group * HALF
                e = e + nt(grad[:, cols], w_ref[:, at : at + HALF])
                if which != 1:
                    sums[which + group] = sums[which + group] + colsum(grad[:, cols].astype(F32))
        xs[0:PATCH, :] = tok_ref[w].astype(F32)
        n, s = norm(xs[...])
        gain_sum = gain_sum + colsum(e * n)
        shift_sum = shift_sum + colsum(e)
        tokg_ref[rows, :] = midg_ref[rows, :] + norm_back(e, n, s, gain)

    small_ref[...] = jnp.zeros_like(small_ref)

    def put(at, value):
        small_ref[at : at + 1, :] = value[:, :HALF]
        small_ref[at + 1 : at + 2, :] = value[:, HALF:]

    put(0, down_sum_ref[...])
    small_ref[2:10, :] = ub0_ref[...] + ub1_ref[...] + ub2_ref[...] + ub3_ref[...]
    for i in range(3):
        put(10 + 2 * i, sum_ref[i : i + 1, :])
    for i in range(4):
        small_ref[16 + i : 17 + i, :] = sums[i]
    put(20, gain_sum)
    put(22, shift_sum)
    both = rel_ref[...]
    heads = both[0:64, 0:64] + both[64:128, 64:128]
    small_ref[24:40, 0:256] = jnp.concatenate([heads[0:16], heads[16:32], heads[32:48], heads[48:64]], axis=1)
    tail_ref[...] = split(small_ref[...])


def outputs_kernel(tokg_ref, mask_ref, own_ref, sib_ref, mid_ref, downb_ref, dep, grad_ref, out_ref):
    windows = mask_ref.shape[0]
    down_bias = row(downb_ref)
    outs = []
    for w in range(windows):
        rows = slice(w * ROWS, (w + 1) * ROWS)
        grad_ref[:, w, :] = tokg_ref[w * ROWS : w * ROWS + PATCH, :]
        mlp_out = own_ref[rows, :] + sib_ref[rows, :].astype(F32)
        outs.append((mid_ref[rows, :] + column_mask(mask_ref, w) * (mlp_out + down_bias))[0:PATCH])
    out_ref[...] = jnp.stack(outs, axis=1).astype(BF16)


def split(x):
    coarse = x.astype(BF16)
    return jnp.concatenate([coarse.astype(F32), x - coarse.astype(F32)], axis=0).astype(BF16)


def join(x):
    half = x.shape[0] // 2
    return x[:half].astype(F32) + x[half:].astype(F32)


def sums_kernel(plan, count, *refs):
    outs = refs[len(refs) - len(plan) :]
    for terms, out in zip(plan, outs):
        total = None
        for which, part in terms:
            value = (refs[which][...] if part is None else refs[which][part]).astype(F32)
            total = value if total is None else total + value
        out[...] = total.astype(out.dtype)


def halve_kernel(keep_ref, got_ref, stay_ref, away_ref):
    size = stay_ref.shape[0]

    def place(mine, other):
        stay_ref[...] = (keep_ref[mine, :].astype(F32) + got_ref[mine, :].astype(F32)).astype(BF16)
        away_ref[0:size, :] = (keep_ref[other, :].astype(F32) + got_ref[other, :].astype(F32)).astype(BF16)

    low, high = slice(0, size), slice(size, 2 * size)
    either(lax.rem(lax.axis_index("mp"), 2), lambda: place(low, high), lambda: place(high, low))


def tail_kernel(tail_ref, got_ref, out_ref):
    out_ref[...] = split(join(tail_ref[...]) + join(got_ref[...]))


def second_kernel(keep_ref, got_ref, tail_ref, other_ref, stay_ref, away_ref):
    size = stay_ref.shape[0]
    stay_ref[...] = (keep_ref[0:size, :].astype(F32) + got_ref[0:size, :].astype(F32)).astype(BF16)
    away_ref[0:size, :] = (keep_ref[size:, :].astype(F32) + got_ref[size:, :].astype(F32)).astype(BF16)
    away_ref[size:, :] = split(join(tail_ref[...]) + join(other_ref[...]))


def near_kernel(keep_ref, got_ref, sent_ref, stay_ref, away_ref):
    halve_kernel(keep_ref, got_ref, stay_ref, away_ref)
    size, tail = stay_ref.shape[0], keep_ref.shape[0]
    away_ref[size:, :] = (join(sent_ref[tail:, :]) + join(got_ref[tail:, :])).astype(BF16)


def far_kernel(keep_ref, got_ref, sent_ref, away_ref):
    size = keep_ref.shape[0]
    away_ref[0:size, :] = (keep_ref[...].astype(F32) + got_ref[0:size, :].astype(F32)).astype(BF16)
    away_ref[size:, :] = (sent_ref[size:, :].astype(F32) + got_ref[size:, :].astype(F32)).astype(BF16)


def finish_kernel(own_ref, got_ref, tail_ref, last_ref, stay_ref, away_ref, mlp_ref, other_ref, qkv_ref, proj_ref, up_ref, down_ref, *refs):
    n1g, n1s, qvb, relh, relw, pb, n2g, n2s, upb, db, small, late, early = refs
    odd = lax.rem(lax.axis_index("mp"), 2)

    def place(into, first, second):
        size = first.shape[0]
        into[0:size, :] = first[...].astype(F32)
        into[size:, :] = second[...].astype(F32)

    for into, own, got in ((late, own_ref, got_ref), (early, stay_ref, away_ref)):
        either(odd, lambda into=into, own=own, got=got: place(into, own, got), lambda into=into, own=own, got=got: place(into, got, own))
    low, high = slice(0, HALF), slice(HALF, D)
    for which, ref in enumerate((up_ref, down_ref)):

        def sides(mine, other, which=which, ref=ref):
            ref[:, mine] = mlp_ref[which, 0].astype(F32)
            ref[:, other] = other_ref[which].astype(F32)

        either(position(True)[0], lambda sides=sides: sides(low, high), lambda sides=sides: sides(high, low))
    for half in range(2):
        proj_ref[:, half * HALF : (half + 1) * HALF] = early[half * 96 : (half + 1) * 96, :]
    for which in range(3):
        qkv_ref[:, which * D : which * D + HALF] = early[(2 + which) * 96 : (3 + which) * 96, :]
        qkv_ref[:, which * D + HALF : (which + 1) * D] = late[which * 96 : (which + 1) * 96, :]
    at = own_ref.shape[0]
    total = tail_ref[at:, :].astype(F32) + last_ref[at:, :].astype(F32)
    small[...] = total
    for ref, at, count in ((db, 0, 2), (upb, 2, 8), (n2g, 10, 2), (n2s, 12, 2), (pb, 14, 2), (qvb, 16, 4), (n1g, 20, 2), (n1s, 22, 2)):
        for i in range(count):
            ref[i * HALF : (i + 1) * HALF] = small[at + i : at + i + 1, :].reshape(HALF)
    rels = 2 * WIN - 1
    block = small[24:40, 0:256]
    for ref, at in ((relh, 0), (relw, 128)):
        ref[0:16, :] = block[:, at : at + 64]
        ref[16:rels, :] = block[0 : rels - 16, at + 64 : at + 128]


ANY = pl.BlockSpec(memory_space=pl.ANY)


def call(kernel, outs, ins, scratch=(), us=1.0, after=None, limit=12, aliases=None):
    shapes = tuple(jax.ShapeDtypeStruct(s, d) for s, d in outs)
    moved = sum(x.size * x.dtype.itemsize for x in ins) + sum(jnp.dtype(d).itemsize * functools.reduce(lambda a, b: a * b, s, 1) for s, d in outs)
    specs = [VM] * len(ins)
    if after is not None:
        ins, specs = [*ins, after], [*specs, ANY]
    return pl.pallas_call(
        kernel,
        out_shape=shapes,
        in_specs=specs,
        out_specs=tuple(VM for _ in outs),
        scratch_shapes=list(scratch),
        input_output_aliases=aliases or {},
        compiler_params=pltpu.CompilerParams(vmem_limit_bytes=limit * 2**20),
        cost_estimate=pl.CostEstimate(flops=int(us * 1.15e9), bytes_accessed=moved, transcendentals=0),
    )(*ins)


def tie(*arrays):
    return lax.optimization_barrier(arrays)


def local(tokens, window_mask, out_grad, norm1_gain, norm1_shift, qkv_weight, qv_bias, rel_height, rel_width, proj_weight, proj_bias,
          norm2_gain, norm2_shift, up_weight, up_bias, down_weight, down_bias):
    dpn, mpn = lax.axis_size("dp"), lax.axis_size("mp")
    c = lax.axis_index("dp") % 2
    windows = tokens.shape[0]
    rows = windows * ROWS
    ring = dpn == 8 and mpn == 4

    def send(x, move):
        perm = []
        for d in range(dpn):
            for m in range(mpn):
                nd, nm = move(d, m)
                perm.append((d * mpn + m, nd * mpn + nm))
        return lax.ppermute(x, AXES, perm)

    core = lambda d, m: (d ^ 1, m)
    first = lambda d, m: (d ^ (4 if d & 1 else 2), m)
    second = lambda d, m: (d ^ (2 if d & 1 else 4), m)
    up_ring = lambda d, m: (d, (m + 1) % mpn)
    down_ring = lambda d, m: (d, (m + mpn - 1) % mpn)
    near = lambda d, m: (d, m ^ 1)
    far = lambda d, m: (d, m ^ 2)
    hold = tie if ring else lambda *arrays: arrays
    narrow = pltpu.VMEM((ROWS, D), F32)
    square = pltpu.VMEM((128, 128), F32)

    def make_qkv(after):
        outs = [((rows, D), BF16), ((1, D), F32)] + [((ROWS, 3 * D), BF16)] * windows + [((ROWS, D), BF16)] * windows
        ins = [tokens, window_mask, out_grad, norm1_gain, norm1_shift, qkv_weight, qv_bias]
        res = call(qkv_kernel, outs, ins, [narrow], us=4.5, after=after)
        return res[0], res[1], res[2 : 2 + windows], res[2 + windows :]

    def attend(w, part, after):
        outs = [((PAIRS, 2 * ROWS, ROWS), BF16), ((ROWS, D), BF16)]
        return call(functools.partial(attend_kernel, w), outs, [window_mask, part, rel_height, rel_width], [square], us=0.01 if w else 8.0, after=after)

    def project(atts):
        outs = [((ROWS, D), BF16)] * windows + [((rows, D), F32), ((rows, D), BF16)]
        ins = [tokens, window_mask, proj_weight, proj_bias, norm2_gain, norm2_shift, *atts]
        res = call(project_kernel, outs, ins, [narrow], us=0.01)
        return res[:windows], *res[windows:]

    part = ((2, 2, 2, 96, HALF), BF16)

    def mlp(spots, g, g_sib, x, x_sib, acc, packs, after):
        n = len(spots)
        outs = [((2, 2 * rows, D), F32)]
        for spot in spots:
            outs += [((2, *part[0]), BF16)] if spot == 1 else [part] * 2
        outs += [((8, HALF), F32)]
        scratch = [pltpu.VMEM((D, n * HALF), BF16), pltpu.VMEM((n * HALF, D), BF16), pltpu.VMEM((8, n * HALF), F32),
                   pltpu.VMEM((2 * rows, n * HALF), BF16), pltpu.VMEM((2 * rows, n * HALF), BF16), pltpu.VMEM((2, D, n * HALF), BF16)]
        ins = [*g, *g_sib, *x, *x_sib, *acc, *packs]
        aliases = {4 * windows: 0} if spots[0] else None
        return call(functools.partial(mlp_kernel, ring, spots, windows), outs, ins, scratch, us=0.01, after=after,
                    limit=12 + 6 * n, aliases=aliases)

    def mlp_front(g, g_sib, x, x_sib, acc, packs, after):
        wide = ((2 * rows, HALF), BF16)
        outs = [((rows, D), F32), ((windows, ROWS, D), BF16), wide, wide, ((HALF, D), BF16)]
        return call(functools.partial(mlp_front_kernel, ring, windows), outs, [*g, *g_sib, *x, *x_sib, acc, *packs],
                    [pltpu.VMEM((D, HALF), BF16), pltpu.VMEM((8, HALF), F32)], us=0.01, after=after, limit=16)

    def mlp_rear(g, g_sib, x, x_sib, acc, hid, pre, down):
        outs = [((rows, D), F32), ((rows, D), BF16), part, part, ((8, HALF), F32)]
        return call(functools.partial(mlp_rear_kernel, ring, windows), outs, [*g, *g_sib, *x, *x_sib, acc, hid, pre, down],
                    [pltpu.VMEM((2, D, HALF), BF16)], us=0.01, limit=16)

    def norm_two(mine, sib, mid, att, after):
        outs = [((rows, D), F32), ((rows, D), BF16), ((2, D, HALF), BF16), ((8, D), F32)]
        ins = [mine, mid, out_grad, window_mask, att, proj_weight, norm2_gain, *sib]
        scratch = [narrow, pltpu.VMEM((rows, D), BF16)]
        return call(functools.partial(norm_two_kernel, ring), outs, ins, scratch, us=0.01, after=after)

    def heads(group, w, dout, rel, before, after):
        last = w == windows - 1
        before = before if group else [*before, proj]
        half = ((2, 2, 3 if group else 5, 96, HALF), BF16)
        outs = [((ROWS, 3 * HALF), BF16), ((128, 128), F32)] + ([half, half] if last else [])
        ins = [dout, qkvs[w], probs[w], rel_height, rel_width] + ([rel] if w or group else []) + ([first_low, *before] if last else [])
        scratch = ([pltpu.VMEM((3, D, HALF), BF16)] if last else []) + [square]
        return call(functools.partial(heads_kernel, ring, w, group, last), outs, ins, scratch, us=(6.0 if last else 3.0) if group else 0.01, after=after)

    def norm_one(mid_grad, dqkv, ubs, down_sum, sums, rel, after):
        outs = [((rows, D), F32), ((2 * SMALL_ROWS, HALF), BF16)]
        ins = [tokens, mid_grad, *dqkv, qkv_weight, norm1_gain, down_sum, *ubs, sums, rel]
        return call(norm_one_kernel, outs, ins, [narrow, pltpu.VMEM((SMALL_ROWS, HALF), F32)], us=6.0, after=after)

    def outputs(tokens_grad, mine, sib, mid, after):
        outs = [((PATCH, windows, D), F32), ((PATCH, windows, D), BF16)]
        return call(outputs_kernel, outs, [tokens_grad, window_mask, mine, sib, mid, down_bias], us=2.0, after=after)

    turn = lambda x: lax.transpose(x, (1, 0, 2))

    def adds(*plan, kind=BF16):
        ins, numbered, outs = [], [], []
        for terms in plan:
            row_of = []
            for term in terms:
                array, part = term if isinstance(term, tuple) else (term, None)
                known = [i for i, other in enumerate(ins) if other is array]
                if not known:
                    ins.append(array)
                row_of.append((known[0] if known else len(ins) - 1, part))
            array, part = terms[0] if isinstance(terms[0], tuple) else (terms[0], None)
            outs.append((array.shape if part is None else array.shape[1:] if isinstance(part, int) else (part.stop, *array.shape[1:]), kind))
            numbered.append(row_of)
        return call(functools.partial(sums_kernel, numbered, len(ins)), outs, ins, us=0.5)

    lines = lambda x: x.reshape(-1, HALF)

    if not ring:
        up_all = lax.all_gather(up_weight, "mp", axis=1, tiled=True)
        down_all = lax.all_gather(down_weight, "mp", axis=0, tiled=True)
        bias_all = lax.all_gather(up_bias, "mp", axis=0, tiled=True)
        packs = [up_all[:, :D], down_all[:D], bias_all[:D]]
        for k in range(1, 4):
            off = k * D + c * HALF
            u_part = lax.dynamic_slice(up_all, (0, off), (D, HALF))
            d_part = lax.dynamic_slice(down_all, (off, 0), (HALF, D))
            d_part = jnp.concatenate([d_part[:, :HALF], d_part[:, HALF:]], axis=0)
            b_part = jnp.broadcast_to(lax.dynamic_slice(bias_all, (off,), (HALF,))[None], (16, HALF))
            packs += [jnp.concatenate([u_part, b_part], axis=0), jnp.concatenate([d_part, b_part], axis=0)]
        first_low, down_sum, qkvs, g = make_qkv(packs[2])
        probs, atts = zip(*[attend(w, qkvs[w], first_low) for w in range(windows)])
        x, mid, att = project(atts)
        rows_of = (g, [send(part, core) for part in g], x, [send(part, core) for part in x])
        acc, keep0, send0, ub0 = mlp((0,), *rows_of, [], packs[0:3], mid)
        acc, both1, ub1 = mlp((1,), *rows_of, [acc], packs[3:5], mid)
        acc, keep2, send2, ub2 = mlp((2,), *rows_of, [acc], packs[5:7], mid)
        mine_back, back, *kept = mlp_front(*rows_of, acc, packs[7:9], mid)
        mine_out, theirs, keep3, send3, ub3 = mlp_rear(*rows_of, acc, *kept)
        mid_grad, dout, proj, sums = norm_two(mine_back, [send(back[w], core) for w in range(windows)], mid, att, mid)
        dqkv, kept, sent, rel = [], [], [], None
        for group in range(2):
            for w in range(windows):
                part, rel, *weights = heads(group, w, dout, rel, dqkv[group * windows :], mid_grad)
                dqkv.append(part)
            kept.append(weights[0])
            sent.append(weights[1])
        tokens_grad, small = norm_one(mid_grad, dqkv, (ub0, ub1, ub2, ub3), down_sum, sums, rel, mid_grad)
        tokens_grad, block_out = (turn(x) for x in outputs(tokens_grad, mine_out, send(theirs, core), mid, mid))
        dw = jnp.stack([jnp.stack([keep0, both1[0], keep2, keep3]), jnp.stack([send0, both1[1], send2, send3])])
        halves = dw.transpose(4, 0, 2, 5, 3, 1, 6).reshape(D, 2, 4, HALF)
        full = jnp.zeros((D, 2, 4, 2, HALF), BF16)
        full = lax.dynamic_update_slice(full, halves[:, :, :, None], (0, 0, 0, c, 0)).reshape(D, 2, 4 * D)
        full = lax.psum_scatter(full, "dp", scatter_dimension=0, tiled=True)
        full = lax.psum_scatter(full, "mp", scatter_dimension=2, tiled=True).astype(F32)
        up_grad, down_grad = full[:, 0], full[:, 1].T
        weights = jnp.stack([jnp.concatenate(kept, axis=2), jnp.concatenate(sent, axis=2)])
        weights = weights.transpose(0, 1, 2, 4, 3, 5).reshape(D, 8 * HALF)
        weights = lax.psum(weights, "mp")
        weights = lax.psum_scatter(weights, "dp", scatter_dimension=0, tiled=True).astype(F32)
        parts = [weights[:, i * HALF : (i + 1) * HALF] for i in range(8)]
        proj_grad = jnp.concatenate(parts[0:2], axis=1)
        qkv_grad = jnp.concatenate([parts[2], parts[5], parts[3], parts[6], parts[4], parts[7]], axis=1)
        small = lax.psum(join(small), AXES)
        vec = lambda start, count: small[start : start + count].reshape(count * HALF)
        table = small[24:40, 0:256].reshape(16, 4, 64).transpose(1, 0, 2).reshape(64, 64)
        rels = 2 * WIN - 1
        return (
            block_out, tokens_grad, vec(20, 2), vec(22, 2), qkv_grad, vec(16, 4), table[0:rels], table[32 : 32 + rels], proj_grad,
            vec(14, 2), vec(10, 2), vec(12, 2), up_grad, vec(2, 8), down_grad, vec(0, 2),
        )

    dp = lax.axis_index("dp")
    j = jnp.where(c == 0, dp // 2 % 2, dp // 4)
    off = c * HALF
    u_part = lax.dynamic_slice(up_weight, (0, off), (D, HALF))
    d_part = lax.dynamic_slice(down_weight, (off, 0), (HALF, D))
    b_part = jnp.broadcast_to(jnp.where(c == 0, up_bias[:HALF], up_bias[HALF:])[None], (32, HALF))
    halves = [jnp.where(j == 0, u_part[i * HALF : (i + 1) * HALF], d_part[:, i * HALF : (i + 1) * HALF]) for i in range(2)]
    pack = jnp.concatenate([*halves, b_part], axis=0)
    again = jnp.concatenate([*halves, b_part[:16]], axis=0)
    m1 = send(pack, up_ring)
    first_low, down_sum, qkvs, g = make_qkv(pack)
    prob0, att0 = attend(0, qkvs[0], pack)
    m1, att0 = tie(m1, att0)

    m2 = send(m1, up_ring)
    o1 = send(m1, first)
    probs, atts = zip((prob0, att0), *[attend(w, qkvs[w], m1) for w in range(1, windows)])
    x, mid, att = project(atts)
    gx = [*g, *x]
    sib = [send(part, core) for part in gx]
    m2, o1, *sib = tie(m2, o1, *sib)
    m3 = send(tie(again, m2)[0], down_ring)
    rows_of = (g, sib[:windows], x, sib[windows:])

    o2 = send(m2[:D], first)
    acc, keep0, send0, ub0 = mlp((0,), *rows_of, [], [up_weight, down_weight, up_bias], m2)
    acc, both1, ub1 = mlp((1,), *rows_of, [acc], [m1, o1], acc)
    m3, o2, acc = tie(m3, o2, acc)

    o3 = send(m3, first)
    got1 = send(both1, down_ring)
    acc, keep2, send2, ub2 = mlp((2,), *rows_of, [acc], [m2, o2], m3)
    o3, acc = tie(o3, acc)

    f2 = [send(send2[i], first) for i in range(2)]
    mine_back, back, *kept = mlp_front(*rows_of, acc, [m3, o3], o3)
    back_sib = [send(back[w], core) for w in range(windows)]
    mine_out, theirs, keep3, send3, ub3 = mlp_rear(*rows_of, acc, *kept)
    *f2, send3 = tie(*f2, send3)
    mid_grad, dout, proj, sums = norm_two(mine_back, back_sib, mid, att, f2[0])

    f3 = send(send3, first)
    s2_keep, s2_send = adds([(keep2, 0), f2[0]], [(keep2, 1), f2[1]])
    s2 = send(s2_send, second)
    part, rel = heads(0, 0, dout, None, [], dout)
    dqkv = [part]
    for w in range(1, windows):
        part, rel, *weights = heads(0, w, dout, rel, dqkv, dout)
        dqkv.append(part)
    keepq, sendq = weights
    f3, s2, got1, theirs, sendq, rel = tie(f3, s2, got1, theirs, sendq, rel)

    gotq = send(sendq, core)
    a_keep, a_send, s3_keep, s3_send, s2_keep = adds(
        [keep0, (got1, 0)], [send0, (got1, 1)], [(keep3, 0), (f3, 0)], [(keep3, 1), (f3, 1)], [s2_keep, s2])
    s3 = send(s3_send, second)
    got2 = send(s2_keep, far)
    theirs_sib = send(theirs, core)
    q_keep, q_send = adds([(keepq, 0), (gotq, 0)], [(keepq, 1), (gotq, 1)])
    q1 = send(q_send, first)
    for w in range(windows):
        part, rel, *weights = heads(1, w, dout, rel, dqkv[windows:], q_send)
        dqkv.append(part)
    keepr, sendr = weights
    q1, s3, got2, theirs_sib, rel, sendr = tie(q1, s3, got2, theirs_sib, rel, sendr)

    gotr = send(sendr, core)
    r_keep, r_send = adds([(keepr, 0), (gotr, 0)], [(keepr, 1), (gotr, 1)])
    r1 = send(lines(r_send), first)
    q_keep, q_send, s3_keep = adds([(q_keep, 0), (q1, 0)], [(q_keep, 1), (q1, 1)], [s3_keep, s3])
    got3 = send(s3_keep, up_ring)
    q2 = send(lines(q_send), second)
    tokens_grad, tail = norm_one(mid_grad, dqkv, (ub0, ub1, ub2, ub3), down_sum, sums, rel, r_send)
    stretch = [((2 * SMALL_ROWS, HALF), BF16)]
    (tail,) = call(tail_kernel, stretch, [tail, send(tail, core)], us=0.5)
    other = send(tail, first)
    r1, q2, other, got3 = tie(r1, q2, other, got3)

    size = r1.shape[0] // 2
    stay, away = call(second_kernel, [((size, HALF), BF16), ((size + 2 * SMALL_ROWS, HALF), BF16)], [lines(r_keep), r1, tail, other], us=0.5)
    r2 = send(away, second)
    half = q2.shape[0] // 2
    q_stay, q_away = call(halve_kernel, [((half, HALF), BF16)] * 2, [lines(q_keep), q2], us=0.5)
    q3 = send(q_away, near)
    tokens_grad, block_out = outputs(tokens_grad, mine_out, theirs_sib, mid, r1)
    r2, q3, tokens_grad = tie(r2, q3, tokens_grad)
    a1 = send(tie(a_send, r2)[0], first)

    size //= 2
    shapes = [((size, HALF), BF16), ((size + SMALL_ROWS, HALF), BF16)]
    stay, away = call(near_kernel, shapes, [stay, r2, away], us=0.5)
    r3 = send(away, near)
    (q_stay,) = adds([q_stay, q3])
    q4 = send(q_stay, far)
    r3, q4, a1 = tie(r3, q4, a1)

    (away,) = call(far_kernel, shapes[1:], [stay, r3, away], us=0.5)
    r4 = send(away, far)
    (q_stay,) = adds([q_stay, q4])
    q5 = send(q_stay, near)
    a_keep, a_send = adds([(a_keep, 0), (a1, 0)], [(a_keep, 1), (a1, 1)])
    a2 = send(a_send, second)
    r4, a2 = tie(r4, a2)

    (r_half,) = adds([(away, slice(0, size)), (r4, slice(0, size))])
    a2, r_half = tie(a2, r_half)
    r5 = send(r_half, near)
    mlp_part, = adds([a_keep, a2, got2, got3])
    other = send(mlp_part[:, 1], core)
    vec = lambda n: ((n,), F32)
    table = ((2 * WIN - 1, 64), F32)
    outs = [((96, 3 * D), F32)] + [((96, D), F32)] * 3 + [vec(D), vec(D), vec(2 * D), table, table, vec(D), vec(D), vec(D), vec(4 * D), vec(D)]
    qkv_grad, proj_grad, up_grad, down_grad, n1g, n1s, qvb, relh, relw, pb, n2g, n2s, upb, db = call(
        finish_kernel, outs, [r_half, r5, away, r4, q_stay, q5, mlp_part, other],
        [pltpu.VMEM((SMALL_ROWS, HALF), F32), pltpu.VMEM((3 * 96, HALF), F32), pltpu.VMEM((5 * 96, HALF), F32)], us=2.0)
    return turn(block_out), turn(tokens_grad), n1g, n1s, qkv_grad, qvb, relh, relw, proj_grad, pb, n2g, n2s, up_grad, upb, down_grad.T, db


def solution(mesh):
    split_rows = P(AXES, None, None)
    in_specs = (split_rows, P(AXES, None), split_rows) + (P(),) * 10 + (P(None, "mp"), P("mp"), P("mp", None), P())
    out_specs = (split_rows, split_rows, P(), P(), P("dp", None), P(), P(), P(), P("dp", None), P(), P(), P(), P("dp", "mp"), P(), P("mp", "dp"), P())
    return jax.shard_map(local, mesh=mesh, in_specs=in_specs, out_specs=out_specs, check_vma=False)
```

```python
import functools

import jax
import jax.numpy as jnp
from jax import lax
from jax.experimental import pallas as pl
from jax.experimental.pallas import tpu as pltpu
from jax.sharding import PartitionSpec as P

D = 768
HEADS = 12
WIN = 14
PATCH = WIN * WIN
ROWS = 208
PAIRS = HEADS // 2
EPSILON = 1e-06
HALF = 384
F32 = jnp.float32
BF16 = jnp.bfloat16
AXES = ("dp", "mp")
VM = pl.BlockSpec(memory_space=pltpu.VMEM)
SMALL_ROWS = 48


def nn(a, b):
    return lax.dot_general(a, b, (((1,), (0,)), ((), ())), preferred_element_type=F32)


def nt(a, b):
    return lax.dot_general(a, b, (((1,), (1,)), ((), ())), preferred_element_type=F32)


def tn(a, b):
    return lax.dot_general(a, b, (((0,), (0,)), ((), ())), preferred_element_type=F32)


def iota(shape, dim):
    return lax.broadcasted_iota(jnp.int32, shape, dim)


def row(ref):
    return ref[...].astype(F32).reshape(1, -1)


def column_mask(mask_ref, w):
    line = mask_ref[w : w + 1, :].astype(F32)
    here = iota((ROWS, PATCH), 0) == iota((ROWS, PATCH), 1)
    return jnp.sum(jnp.where(here, line, 0.0), axis=1, keepdims=True)


def key_mask(column):
    here = iota((ROWS, ROWS), 0) == iota((ROWS, ROWS), 1)
    return jnp.sum(jnp.where(here, column, 0.0), axis=0, keepdims=True)


def norm(x):
    average = jnp.mean(x, axis=-1, keepdims=True)
    centred = x - average
    variance = jnp.mean(centred * centred, axis=-1, keepdims=True)
    inverse = lax.rsqrt(variance + EPSILON)
    return centred * inverse, inverse


def norm_back(e, n, s, gain):
    scaled = e * gain
    mean_grad = jnp.mean(scaled, axis=-1, keepdims=True)
    mean_proj = jnp.mean(scaled * n, axis=-1, keepdims=True)
    return s * (scaled - mean_grad - n * mean_proj)


def colsum(x):
    return jnp.sum(x, axis=0, keepdims=True)


def fill_tables(table, height_ref, width_ref):
    table[...] = jnp.zeros((128, 128), F32)
    height = height_ref[...].astype(F32)
    width = width_ref[...].astype(F32)
    none = jnp.zeros_like(height)
    rels = 2 * WIN - 1
    table[0:rels, :] = jnp.concatenate([height, none], axis=1)
    table[32 : 32 + rels, :] = jnp.concatenate([width, none], axis=1)
    table[64 : 64 + rels, :] = jnp.concatenate([none, height], axis=1)
    table[96 : 96 + rels, :] = jnp.concatenate([none, width], axis=1)


def shift_bits():
    place = iota((ROWS, 128), 0)
    high = place // WIN
    wide = place - high * WIN
    return jnp.where((iota((ROWS, 128), 1) & 32) == 0, high, wide)


def shift_rows(x, amount, left):
    for bit in range(4):
        step = 1 << bit
        moved = pltpu.roll(x, 128 - step if left else step, 1)
        x = jnp.where((amount & step) != 0, moved, x)
    return x


def one_hot(both):
    place = iota((ROWS, 128), 0)
    lane = iota((ROWS, 128), 1)
    high = place // WIN
    wide = place - high * WIN
    want = jnp.where((lane & 32) == 0, high, wide)
    sub = lane & 31
    slot = (sub & 15) if both else sub
    hit = (slot == (WIN - 1) - want) & (place < PATCH)
    return jnp.where(hit, 1.0, 0.0).astype(BF16)


def qkv_kernel(tok_ref, mask_ref, cot_ref, gain_ref, shift_ref, w_ref, bias_ref, dep, first_ref, sum_ref, *refs):
    windows = tok_ref.shape[0]
    outs, gs, xs = refs[:windows], refs[windows:-1], refs[-1]
    sums = jnp.zeros((1, D), F32)
    gain, shift = row(gain_ref), row(shift_ref)
    xs[ROWS - 16 :, :] = jnp.zeros((16, D), F32)
    for w in range(windows):
        xs[0:PATCH, :] = tok_ref[w].astype(F32)
        n, _ = norm(xs[...])
        first_ref[w * ROWS : (w + 1) * ROWS, :] = (n * gain + shift).astype(BF16)
        xs[0:PATCH, :] = cot_ref[w].astype(F32)
        g = (column_mask(mask_ref, w) * xs[...]).astype(BF16)
        gs[w][...] = g
        sums = sums + colsum(g.astype(F32))
    sum_ref[...] = sums
    bias = row(bias_ref)
    for part in range(3):
        cols = slice(part * D, (part + 1) * D)
        out = nn(first_ref[...], w_ref[:, cols])
        if part == 0:
            out = out + bias[:, :D]
        if part == 2:
            out = out + bias[:, D:]
        for w in range(windows):
            outs[w][:, cols] = out[w * ROWS : (w + 1) * ROWS].astype(BF16)


def attend_kernel(w, mask_ref, qkv_ref, height_ref, width_ref, dep, prob_ref, att_ref, table):
    fill_tables(table, height_ref, width_ref)
    tab = table[...].astype(BF16)
    amount = shift_bits()
    keys_hot = one_hot(True)
    lane = iota((ROWS, 128), 1)
    lower = lane < 64
    sub = lane & 31
    valid = key_mask(column_mask(mask_ref, w)) > 0.5

    def pair(p, carry):
        at = pl.multiple_of(p * 128, 128)
        q = qkv_ref[:, pl.ds(at, 128)]
        k = qkv_ref[:, pl.ds(D + at, 128)]
        v = qkv_ref[:, pl.ds(2 * D + at, 128)]
        terms = shift_rows(nt(q, tab), amount, True)
        coarse = terms.astype(BF16).astype(F32)
        fine = pltpu.roll(terms - coarse, 16, 1)
        terms = jnp.where(sub < WIN, coarse, jnp.where((sub >= 16) & (sub < 16 + WIN), fine, 0.0))
        qs = q.astype(F32) * 0.125
        top = jnp.concatenate([jnp.where(lower, qs, 0.0), jnp.where(lower, terms, 0.0)], axis=1)
        bottom = jnp.concatenate([jnp.where(lower, 0.0, qs), jnp.where(lower, 0.0, terms)], axis=1)
        left = jnp.concatenate([top, bottom], axis=0).astype(BF16)
        right = jnp.concatenate([k, keys_hot], axis=1)
        scores = jnp.where(valid, nt(left, right), -1000000000.0)
        most = jnp.max(scores, axis=1, keepdims=True)
        weight = jnp.exp(scores - most)
        total = jnp.sum(weight, axis=1, keepdims=True)
        prob = (weight * (1.0 / total)).astype(BF16)
        prob_ref[p] = prob
        out = nn(prob, v)
        att_ref[:, pl.ds(at, 128)] = jnp.where(lower, out[:ROWS], out[ROWS:]).astype(BF16)
        return carry

    lax.fori_loop(0, PAIRS, pair, 0, unroll=2)


def project_kernel(tok_ref, mask_ref, w_ref, bias_ref, gain_ref, shift_ref, *refs):
    windows = tok_ref.shape[0]
    atts, lows = refs[:windows], refs[windows : 2 * windows]
    mid_ref, all_ref, xs = refs[2 * windows :]
    gain, shift, bias = row(gain_ref), row(shift_ref), row(bias_ref)
    xs[ROWS - 16 :, :] = jnp.zeros((16, D), F32)
    for w in range(windows):
        all_ref[w * ROWS : (w + 1) * ROWS, :] = atts[w][...]
    out = nn(all_ref[...], w_ref[...]) + bias
    for w in range(windows):
        rows = slice(w * ROWS, (w + 1) * ROWS)
        xs[0:PATCH, :] = tok_ref[w].astype(F32)
        mid = xs[...] + column_mask(mask_ref, w) * out[rows]
        mid_ref[rows, :] = mid
        n, _ = norm(mid)
        lows[w][...] = (n * gain + shift).astype(BF16)


def position(ring):
    dp, z = lax.axis_index("dp"), lax.axis_index("mp")
    c = lax.rem(dp, 2)
    if not ring:
        return c, 0, 0, 0, 0
    y, x = lax.div(dp, 4), lax.rem(lax.div(dp, 2), 2)
    return c, jnp.where(c == 0, x, y), y, x, z


def apart(a, b):
    return a ^ b if isinstance(b, int) else jnp.where(b == a, 0, 1)


def slot_of(ring, block, by_block):
    yb, xb, cb = block // 4, (block // 2) % 2, block % 2
    if not ring:
        return block // 4, (block // 2) % 2, block % 2
    c, _, y, x, _ = position(ring)
    over_y, over_x = apart(yb, y), apart(xb, x)
    if by_block:
        return apart(cb, c), *((over_y, over_x) if cb else (over_x, over_y))
    return apart(cb, c), jnp.where(c == 0, over_x, over_y), jnp.where(c == 0, over_y, over_x)


def load_half(j, k, mine, other, up, down, bias):
    cols = slice(k * HALF, (k + 1) * HALF)
    bias[0:1, cols] = mine[D : D + 16, :].astype(F32)[0:1, :]

    def place(first, second):
        up[:, cols] = first[0:D, :]
        down[cols, 0:HALF] = second[0:HALF, :]
        down[cols, HALF:D] = second[HALF:D, :]

    either(j, lambda: place(mine, other), lambda: place(other, mine))


def hidden(x, g, up, down, bias):
    u = nn(x, up) + bias
    phi = 0.5 + 0.5 * lax.erf(u * 0.7071067811865476)
    slope = phi + u * jnp.exp(-0.5 * u * u) * 0.3989422804014327
    return (u * phi).astype(BF16), (nt(g, down) * slope).astype(BF16)


def weight_grads(ring, spots, grefs, xrefs, hid, pre, outs, ub_ref, grads):
    c, _, _, _, z = position(ring)
    width = len(spots) * HALF
    blocks = [slice(block * ROWS, (block + 1) * ROWS) for block in range(len(xrefs))]
    sums = jnp.zeros((1, width), F32)
    for block in blocks:
        sums = sums + colsum(pre[block, :].astype(F32))
    for which, (left, right) in enumerate(((xrefs, pre), (grefs, hid))):
        total = jnp.zeros((D, width), F32)
        for ref, block in zip(left, blocks):
            total = total + tn(ref[...], right[block, :])
        grads[which] = total.astype(BF16)
    ub_ref[...] = jnp.zeros_like(ub_ref)
    for k, spot in enumerate(spots):
        s = lax.rem(z + 4 - spot, 4) if ring else spot
        ub_ref[pl.ds(2 * s + c, 1), :] = sums[:, k * HALF : (k + 1) * HALF]
    for b in range(8):
        cr, first, second = slot_of(ring, b, False)
        lines = slice(b * 96, (b + 1) * 96)
        for k in range(len(spots)):
            part = slice(k * HALF, (k + 1) * HALF)

            def move(target, cr=cr, second=second, lines=lines, part=part):
                for which in range(2):
                    target[second, which, cr] = grads[which, lines, part]

            if len(outs[k]) == 1:
                move(outs[k][0].at[first])
            else:
                either(first, lambda k=k, move=move: move(outs[k][0]), lambda k=k, move=move: move(outs[k][1]))


def mlp_kernel(ring, spots, windows, *refs):
    refs = list(refs)
    blocks = 2 * windows
    grefs = [refs.pop(0) for _ in range(blocks)]
    xrefs = [refs.pop(0) for _ in range(blocks)]
    c, j, *_ = position(ring)
    if spots[0] == 0:
        acc_in = None
        up_ref, down_ref, upb_ref = (refs.pop(0) for _ in range(3))
    else:
        acc_in = refs.pop(0)
    packs = [(k, refs.pop(0), refs.pop(0)) for k, spot in enumerate(spots) if spot]
    dep, acc = refs.pop(0), refs.pop(0)
    outs = [(refs.pop(0),) if spot == 1 else (refs.pop(0), refs.pop(0)) for spot in spots]
    ub_ref, up, down, bias, hid, pre, grads = refs
    if acc_in is None:
        off = pl.multiple_of(c * HALF, HALF)
        up[:, 0:HALF] = up_ref[:, pl.ds(off, HALF)]
        down[0:HALF, :] = down_ref[pl.ds(off, HALF), :]
        line = row(upb_ref)
        bias[0:1, 0:HALF] = jnp.where(c == 0, line[:, :HALF], line[:, HALF:])
    for k, mine, other in packs:
        load_half(j, k, mine, other, up, down, bias)
    up_c, down_c, bias_c = up[...], down[...], bias[0:1, :]
    for block in range(blocks):
        there = slice(block * ROWS, (block + 1) * ROWS)
        h, pg = hidden(xrefs[block][...], grefs[block][...], up_c, down_c, bias_c)
        hid[there, :] = h
        pre[there, :] = pg
        for which, value in enumerate((nn(h, down_c), nt(pg, up_c))):
            acc[which, there, :] = value if acc_in is None else acc_in[which, there, :] + value
    weight_grads(ring, spots, grefs, xrefs, hid, pre, outs, ub_ref, grads)


def mlp_front_kernel(ring, windows, *refs):
    blocks = 2 * windows
    grefs, xrefs, refs = refs[:blocks], refs[blocks : 2 * blocks], refs[2 * blocks :]
    acc, mine, other, dep, back_ref, tback_ref, hid, pre, down, up, bias = refs
    load_half(position(ring)[1], 0, mine, other, up, down, bias)
    up_c, down_c, bias_c = up[...], down[...], bias[0:1, :]
    for block in range(blocks):
        here = slice((block % windows) * ROWS, (block % windows + 1) * ROWS)
        there = slice(block * ROWS, (block + 1) * ROWS)
        h, pg = hidden(xrefs[block][...], grefs[block][...], up_c, down_c, bias_c)
        hid[there, :] = h
        pre[there, :] = pg
        back = acc[1, there, :] + nt(pg, up_c)
        if block < windows:
            back_ref[here, :] = back
        else:
            tback_ref[block - windows] = back.astype(BF16)


def mlp_rear_kernel(ring, windows, *refs):
    blocks = 2 * windows
    grefs, xrefs, refs = refs[:blocks], refs[blocks : 2 * blocks], refs[2 * blocks :]
    acc, hid, pre, down, out_ref, tout_ref, keep_ref, send_ref, ub_ref, grads = refs
    weight_grads(ring, (3,), grefs, xrefs, hid, pre, [(keep_ref, send_ref)], ub_ref, grads)
    for block in range(blocks):
        here = slice((block % windows) * ROWS, (block % windows + 1) * ROWS)
        there = slice(block * ROWS, (block + 1) * ROWS)
        out = acc[0, there, :] + nn(hid[there, :], down[...])
        if block < windows:
            out_ref[here, :] = out
        else:
            tout_ref[here, :] = out.astype(BF16)


def either(index, zero, one):
    if isinstance(index, int):
        return one() if index else zero()
    pl.when(index == 0)(zero)
    pl.when(index != 0)(one)


def store_blocks(keep_ref, send_ref, ring, index, ref):
    for b in range(8):
        cr, first, second = slot_of(ring, b, True)
        lines = slice(b * 96, (b + 1) * 96)

        def move(target, first=first, second=second, lines=lines):
            target[first, second, index] = ref[lines, :]

        either(cr, lambda move=move: move(keep_ref), lambda move=move: move(send_ref))


def heads_back(p, dout, lower, amount, hot, tab, q, k, v, prob_low, rel):
    none = jnp.zeros_like(dout)
    douts = jnp.concatenate([jnp.where(lower, dout, none), jnp.where(lower, none, dout)], axis=0)
    qs = (q.astype(F32) * 0.125).astype(BF16)
    queries = jnp.concatenate([jnp.where(lower, qs, none), jnp.where(lower, none, qs)], axis=0)
    prob = prob_low.astype(F32)
    dprob = nt(douts, v)
    delta = jnp.sum(prob * dprob, axis=1, keepdims=True)
    dscore = (prob * (dprob - delta)).astype(BF16)
    both = nn(dscore, jnp.concatenate([k, hot], axis=1))
    dq = jnp.where(lower, both[:ROWS, :128], both[ROWS:, :128]) * 0.125
    sums = shift_rows(jnp.where(lower, both[:ROWS, 128:], both[ROWS:, 128:]), amount, False).astype(BF16)
    dq = dq + nn(sums, tab)
    rel[...] += tn(sums, q)
    dk = tn(dscore, queries)
    dv = tn(prob_low, douts)
    return dq, dk, dv


def heads_kernel(ring, w, group, last, dout_ref, qkv_ref, prob_ref, height_ref, width_ref, *refs):
    refs = list(refs)
    rel_in = refs.pop(0) if w or group else None
    before = []
    if last:
        first_ref = refs.pop(0)
        before = [refs.pop(0) for _ in range(w)]
        early = [] if group else [refs.pop(0)]
    dep, dqkv, rel = refs[:3]
    table = refs[-1]
    fill_tables(table, height_ref, width_ref)
    tab = table[...].astype(BF16)
    rel[...] = jnp.zeros_like(rel) if rel_in is None else rel_in[...]
    amount = shift_bits()
    hot = one_hot(False)
    lower = iota((ROWS, 128), 1) < 64
    rows = slice(w * ROWS, (w + 1) * ROWS)
    for step in range(PAIRS // 2):
        p = group * (PAIRS // 2) + step
        at = slice(p * 128, (p + 1) * 128)
        q, k, v = (qkv_ref[:, i * D + p * 128 : i * D + (p + 1) * 128] for i in range(3))
        parts = heads_back(p, dout_ref[rows, at], lower, amount, hot, tab, q, k, v, prob_ref[p], rel)
        for which, value in enumerate(parts):
            dqkv[:, which * HALF + step * 128 : which * HALF + (step + 1) * 128] = value.astype(BF16)
    if last:
        keep_ref, send_ref, grad = refs[3:6]
        for ref in early:
            for which in range(2):
                store_blocks(keep_ref, send_ref, ring, which, ref.at[which])
        for which in range(3):
            cols = slice(which * HALF, (which + 1) * HALF)
            total = tn(first_ref[rows, :], dqkv[:, cols])
            for other, ref in enumerate(before):
                total = total + tn(first_ref[other * ROWS : (other + 1) * ROWS, :], ref[:, cols])
            grad[which] = total.astype(BF16)
            store_blocks(keep_ref, send_ref, ring, 2 * len(early) + which, grad.at[which])


def norm_two_kernel(ring, own_ref, mid_ref, cot_ref, mask_ref, att_ref, projw_ref, gain_ref, *refs):
    sibs, refs = refs[: cot_ref.shape[0]], refs[cot_ref.shape[0] :]
    dep, midg_ref, dout_ref, proj_ref, sum_ref, xs, low = refs
    windows = cot_ref.shape[0]
    gain = row(gain_ref)
    xs[ROWS - 16 :, :] = jnp.zeros((16, D), F32)
    gain_sum = jnp.zeros((1, D), F32)
    shift_sum = jnp.zeros((1, D), F32)
    proj_sum = jnp.zeros((1, D), F32)
    for w in range(windows):
        rows = slice(w * ROWS, (w + 1) * ROWS)
        n, s = norm(mid_ref[rows, :])
        e = own_ref[rows, :] + sibs[w][...].astype(F32)
        gain_sum = gain_sum + colsum(e * n)
        shift_sum = shift_sum + colsum(e)
        xs[0:PATCH, :] = cot_ref[w].astype(F32)
        grad = xs[...] + norm_back(e, n, s, gain)
        midg_ref[rows, :] = grad
        attn = (column_mask(mask_ref, w) * grad).astype(BF16)
        low[rows, :] = attn
        proj_sum = proj_sum + colsum(attn.astype(F32))
    sum_ref[...] = jnp.zeros_like(sum_ref)
    sum_ref[0:1, :] = gain_sum
    sum_ref[1:2, :] = shift_sum
    sum_ref[2:3, :] = proj_sum
    proj_grad = tn(att_ref[...], low[...])
    for half in range(2):
        proj_ref[half] = proj_grad[:, half * HALF : (half + 1) * HALF].astype(BF16)
    dout_ref[...] = nt(low[...], projw_ref[...]).astype(BF16)


def norm_one_kernel(tok_ref, midg_ref, *refs):
    windows = tok_ref.shape[0]
    dqkv, refs = refs[: 2 * windows], refs[2 * windows :]
    w_ref, gain_ref, down_sum_ref, ub0_ref, ub1_ref, ub2_ref, ub3_ref, sum_ref, rel_ref, dep, tokg_ref, tail_ref, xs, small_ref = refs
    gain = row(gain_ref)
    xs[ROWS - 16 :, :] = jnp.zeros((16, D), F32)
    gain_sum = jnp.zeros((1, D), F32)
    shift_sum = jnp.zeros((1, D), F32)
    sums = [jnp.zeros((1, HALF), F32) for _ in range(4)]
    for w in range(windows):
        rows = slice(w * ROWS, (w + 1) * ROWS)
        e = jnp.zeros((ROWS, D), F32)
        for group in range(2):
            grad = dqkv[group * windows + w]
            for which in range(3):
                cols = slice(which * HALF, (which + 1) * HALF)
                at = which * D + group * HALF
                e = e + nt(grad[:, cols], w_ref[:, at : at + HALF])
                if which != 1:
                    sums[which + group] = sums[which + group] + colsum(grad[:, cols].astype(F32))
        xs[0:PATCH, :] = tok_ref[w].astype(F32)
        n, s = norm(xs[...])
        gain_sum = gain_sum + colsum(e * n)
        shift_sum = shift_sum + colsum(e)
        tokg_ref[rows, :] = midg_ref[rows, :] + norm_back(e, n, s, gain)

    small_ref[...] = jnp.zeros_like(small_ref)

    def put(at, value):
        small_ref[at : at + 1, :] = value[:, :HALF]
        small_ref[at + 1 : at + 2, :] = value[:, HALF:]

    put(0, down_sum_ref[...])
    small_ref[2:10, :] = ub0_ref[...] + ub1_ref[...] + ub2_ref[...] + ub3_ref[...]
    for i in range(3):
        put(10 + 2 * i, sum_ref[i : i + 1, :])
    for i in range(4):
        small_ref[16 + i : 17 + i, :] = sums[i]
    put(20, gain_sum)
    put(22, shift_sum)
    both = rel_ref[...]
    heads = both[0:64, 0:64] + both[64:128, 64:128]
    small_ref[24:40, 0:256] = jnp.concatenate([heads[0:16], heads[16:32], heads[32:48], heads[48:64]], axis=1)
    tail_ref[...] = split(small_ref[...])


def outputs_kernel(tokg_ref, mask_ref, own_ref, sib_ref, mid_ref, downb_ref, dep, grad_ref, out_ref):
    windows = mask_ref.shape[0]
    down_bias = row(downb_ref)
    outs = []
    for w in range(windows):
        rows = slice(w * ROWS, (w + 1) * ROWS)
        grad_ref[:, w, :] = tokg_ref[w * ROWS : w * ROWS + PATCH, :]
        mlp_out = own_ref[rows, :] + sib_ref[rows, :].astype(F32)
        outs.append((mid_ref[rows, :] + column_mask(mask_ref, w) * (mlp_out + down_bias))[0:PATCH])
    out_ref[...] = jnp.stack(outs, axis=1).astype(BF16)


def split(x):
    coarse = x.astype(BF16)
    return jnp.concatenate([coarse.astype(F32), x - coarse.astype(F32)], axis=0).astype(BF16)


def join(x):
    half = x.shape[0] // 2
    return x[:half].astype(F32) + x[half:].astype(F32)


def sums_kernel(plan, count, *refs):
    outs = refs[len(refs) - len(plan) :]
    for terms, out in zip(plan, outs):
        total = None
        for which, part in terms:
            value = (refs[which][...] if part is None else refs[which][part]).astype(F32)
            total = value if total is None else total + value
        out[...] = total.astype(out.dtype)


def halve_kernel(keep_ref, got_ref, stay_ref, away_ref):
    size = stay_ref.shape[0]

    def place(mine, other):
        stay_ref[...] = (keep_ref[mine, :].astype(F32) + got_ref[mine, :].astype(F32)).astype(BF16)
        away_ref[0:size, :] = (keep_ref[other, :].astype(F32) + got_ref[other, :].astype(F32)).astype(BF16)

    low, high = slice(0, size), slice(size, 2 * size)
    either(lax.rem(lax.axis_index("mp"), 2), lambda: place(low, high), lambda: place(high, low))


def tail_kernel(tail_ref, got_ref, out_ref):
    out_ref[...] = split(join(tail_ref[...]) + join(got_ref[...]))


def second_kernel(keep_ref, got_ref, tail_ref, other_ref, stay_ref, away_ref):
    size = stay_ref.shape[0]
    stay_ref[...] = (keep_ref[0:size, :].astype(F32) + got_ref[0:size, :].astype(F32)).astype(BF16)
    away_ref[0:size, :] = (keep_ref[size:, :].astype(F32) + got_ref[size:, :].astype(F32)).astype(BF16)
    away_ref[size:, :] = split(join(tail_ref[...]) + join(other_ref[...]))


def near_kernel(keep_ref, got_ref, sent_ref, stay_ref, away_ref):
    halve_kernel(keep_ref, got_ref, stay_ref, away_ref)
    size, tail = stay_ref.shape[0], keep_ref.shape[0]
    away_ref[size:, :] = (join(sent_ref[tail:, :]) + join(got_ref[tail:, :])).astype(BF16)


def far_kernel(keep_ref, got_ref, sent_ref, away_ref):
    size = keep_ref.shape[0]
    away_ref[0:size, :] = (keep_ref[...].astype(F32) + got_ref[0:size, :].astype(F32)).astype(BF16)
    away_ref[size:, :] = (sent_ref[size:, :].astype(F32) + got_ref[size:, :].astype(F32)).astype(BF16)


def finish_kernel(own_ref, got_ref, tail_ref, last_ref, stay_ref, away_ref, mlp_ref, other_ref, qkv_ref, proj_ref, up_ref, down_ref, *refs):
    n1g, n1s, qvb, relh, relw, pb, n2g, n2s, upb, db, small, late, early = refs
    odd = lax.rem(lax.axis_index("mp"), 2)

    def place(into, first, second):
        size = first.shape[0]
        into[0:size, :] = first[...].astype(F32)
        into[size:, :] = second[...].astype(F32)

    for into, own, got in ((late, own_ref, got_ref), (early, stay_ref, away_ref)):
        either(odd, lambda into=into, own=own, got=got: place(into, own, got), lambda into=into, own=own, got=got: place(into, got, own))
    low, high = slice(0, HALF), slice(HALF, D)
    for which, ref in enumerate((up_ref, down_ref)):

        def sides(mine, other, which=which, ref=ref):
            ref[:, mine] = mlp_ref[which, 0].astype(F32)
            ref[:, other] = other_ref[which].astype(F32)

        either(position(True)[0], lambda sides=sides: sides(low, high), lambda sides=sides: sides(high, low))
    for half in range(2):
        proj_ref[:, half * HALF : (half + 1) * HALF] = early[half * 96 : (half + 1) * 96, :]
    for which in range(3):
        qkv_ref[:, which * D : which * D + HALF] = early[(2 + which) * 96 : (3 + which) * 96, :]
        qkv_ref[:, which * D + HALF : (which + 1) * D] = late[which * 96 : (which + 1) * 96, :]
    at = own_ref.shape[0]
    total = tail_ref[at:, :].astype(F32) + last_ref[at:, :].astype(F32)
    small[...] = total
    for ref, at, count in ((db, 0, 2), (upb, 2, 8), (n2g, 10, 2), (n2s, 12, 2), (pb, 14, 2), (qvb, 16, 4), (n1g, 20, 2), (n1s, 22, 2)):
        for i in range(count):
            ref[i * HALF : (i + 1) * HALF] = small[at + i : at + i + 1, :].reshape(HALF)
    rels = 2 * WIN - 1
    block = small[24:40, 0:256]
    for ref, at in ((relh, 0), (relw, 128)):
        ref[0:16, :] = block[:, at : at + 64]
        ref[16:rels, :] = block[0 : rels - 16, at + 64 : at + 128]


ANY = pl.BlockSpec(memory_space=pl.ANY)


def call(kernel, outs, ins, scratch=(), us=1.0, after=None, limit=12, aliases=None):
    shapes = tuple(jax.ShapeDtypeStruct(s, d) for s, d in outs)
    moved = sum(x.size * x.dtype.itemsize for x in ins) + sum(jnp.dtype(d).itemsize * functools.reduce(lambda a, b: a * b, s, 1) for s, d in outs)
    specs = [VM] * len(ins)
    if after is not None:
        ins, specs = [*ins, after], [*specs, ANY]
    return pl.pallas_call(
        kernel,
        out_shape=shapes,
        in_specs=specs,
        out_specs=tuple(VM for _ in outs),
        scratch_shapes=list(scratch),
        input_output_aliases=aliases or {},
        compiler_params=pltpu.CompilerParams(vmem_limit_bytes=limit * 2**20),
        cost_estimate=pl.CostEstimate(flops=int(us * 1.15e9), bytes_accessed=moved, transcendentals=0),
    )(*ins)


def tie(*arrays):
    return lax.optimization_barrier(arrays)


def local(tokens, window_mask, out_grad, norm1_gain, norm1_shift, qkv_weight, qv_bias, rel_height, rel_width, proj_weight, proj_bias,
          norm2_gain, norm2_shift, up_weight, up_bias, down_weight, down_bias):
    dpn, mpn = lax.axis_size("dp"), lax.axis_size("mp")
    c = lax.axis_index("dp") % 2
    windows = tokens.shape[0]
    rows = windows * ROWS
    ring = dpn == 8 and mpn == 4

    def send(x, move):
        perm = []
        for d in range(dpn):
            for m in range(mpn):
                nd, nm = move(d, m)
                perm.append((d * mpn + m, nd * mpn + nm))
        return lax.ppermute(x, AXES, perm)

    core = lambda d, m: (d ^ 1, m)
    first = lambda d, m: (d ^ (4 if d & 1 else 2), m)
    second = lambda d, m: (d ^ (2 if d & 1 else 4), m)
    up_ring = lambda d, m: (d, (m + 1) % mpn)
    down_ring = lambda d, m: (d, (m + mpn - 1) % mpn)
    near = lambda d, m: (d, m ^ 1)
    far = lambda d, m: (d, m ^ 2)
    hold = tie if ring else lambda *arrays: arrays
    narrow = pltpu.VMEM((ROWS, D), F32)
    square = pltpu.VMEM((128, 128), F32)

    def make_qkv(after):
        outs = [((rows, D), BF16), ((1, D), F32)] + [((ROWS, 3 * D), BF16)] * windows + [((ROWS, D), BF16)] * windows
        ins = [tokens, window_mask, out_grad, norm1_gain, norm1_shift, qkv_weight, qv_bias]
        res = call(qkv_kernel, outs, ins, [narrow], us=4.5, after=after)
        return res[0], res[1], res[2 : 2 + windows], res[2 + windows :]

    def attend(w, part, after):
        outs = [((PAIRS, 2 * ROWS, ROWS), BF16), ((ROWS, D), BF16)]
        return call(functools.partial(attend_kernel, w), outs, [window_mask, part, rel_height, rel_width], [square], us=0.01 if w else 8.0, after=after)

    def project(atts):
        outs = [((ROWS, D), BF16)] * windows + [((rows, D), F32), ((rows, D), BF16)]
        ins = [tokens, window_mask, proj_weight, proj_bias, norm2_gain, norm2_shift, *atts]
        res = call(project_kernel, outs, ins, [narrow], us=0.01)
        return res[:windows], *res[windows:]

    part = ((2, 2, 2, 96, HALF), BF16)

    def mlp(spots, g, g_sib, x, x_sib, acc, packs, after):
        n = len(spots)
        outs = [((2, 2 * rows, D), F32)]
        for spot in spots:
            outs += [((2, *part[0]), BF16)] if spot == 1 else [part] * 2
        outs += [((8, HALF), F32)]
        scratch = [pltpu.VMEM((D, n * HALF), BF16), pltpu.VMEM((n * HALF, D), BF16), pltpu.VMEM((8, n * HALF), F32),
                   pltpu.VMEM((2 * rows, n * HALF), BF16), pltpu.VMEM((2 * rows, n * HALF), BF16), pltpu.VMEM((2, D, n * HALF), BF16)]
        ins = [*g, *g_sib, *x, *x_sib, *acc, *packs]
        aliases = {4 * windows: 0} if spots[0] else None
        return call(functools.partial(mlp_kernel, ring, spots, windows), outs, ins, scratch, us=0.01, after=after,
                    limit=12 + 6 * n, aliases=aliases)

    def mlp_front(g, g_sib, x, x_sib, acc, packs, after):
        wide = ((2 * rows, HALF), BF16)
        outs = [((rows, D), F32), ((windows, ROWS, D), BF16), wide, wide, ((HALF, D), BF16)]
        return call(functools.partial(mlp_front_kernel, ring, windows), outs, [*g, *g_sib, *x, *x_sib, acc, *packs],
                    [pltpu.VMEM((D, HALF), BF16), pltpu.VMEM((8, HALF), F32)], us=0.01, after=after, limit=16)

    def mlp_rear(g, g_sib, x, x_sib, acc, hid, pre, down):
        outs = [((rows, D), F32), ((rows, D), BF16), part, part, ((8, HALF), F32)]
        return call(functools.partial(mlp_rear_kernel, ring, windows), outs, [*g, *g_sib, *x, *x_sib, acc, hid, pre, down],
                    [pltpu.VMEM((2, D, HALF), BF16)], us=0.01, limit=16)

    def norm_two(mine, sib, mid, att, after):
        outs = [((rows, D), F32), ((rows, D), BF16), ((2, D, HALF), BF16), ((8, D), F32)]
        ins = [mine, mid, out_grad, window_mask, att, proj_weight, norm2_gain, *sib]
        scratch = [narrow, pltpu.VMEM((rows, D), BF16)]
        return call(functools.partial(norm_two_kernel, ring), outs, ins, scratch, us=0.01, after=after)

    def heads(group, w, dout, rel, before, after):
        last = w == windows - 1
        before = before if group else [*before, proj]
        half = ((2, 2, 3 if group else 5, 96, HALF), BF16)
        outs = [((ROWS, 3 * HALF), BF16), ((128, 128), F32)] + ([half, half] if last else [])
        ins = [dout, qkvs[w], probs[w], rel_height, rel_width] + ([rel] if w or group else []) + ([first_low, *before] if last else [])
        scratch = ([pltpu.VMEM((3, D, HALF), BF16)] if last else []) + [square]
        return call(functools.partial(heads_kernel, ring, w, group, last), outs, ins, scratch, us=(6.0 if last else 3.0) if group else 0.01, after=after)

    def norm_one(mid_grad, dqkv, ubs, down_sum, sums, rel, after):
        outs = [((rows, D), F32), ((2 * SMALL_ROWS, HALF), BF16)]
        ins = [tokens, mid_grad, *dqkv, qkv_weight, norm1_gain, down_sum, *ubs, sums, rel]
        return call(norm_one_kernel, outs, ins, [narrow, pltpu.VMEM((SMALL_ROWS, HALF), F32)], us=6.0, after=after)

    def outputs(tokens_grad, mine, sib, mid, after):
        outs = [((PATCH, windows, D), F32), ((PATCH, windows, D), BF16)]
        return call(outputs_kernel, outs, [tokens_grad, window_mask, mine, sib, mid, down_bias], us=2.0, after=after)

    turn = lambda x: lax.transpose(x, (1, 0, 2))

    def adds(*plan, kind=BF16):
        ins, numbered, outs = [], [], []
        for terms in plan:
            row_of = []
            for term in terms:
                array, part = term if isinstance(term, tuple) else (term, None)
                known = [i for i, other in enumerate(ins) if other is array]
                if not known:
                    ins.append(array)
                row_of.append((known[0] if known else len(ins) - 1, part))
            array, part = terms[0] if isinstance(terms[0], tuple) else (terms[0], None)
            outs.append((array.shape if part is None else array.shape[1:] if isinstance(part, int) else (part.stop, *array.shape[1:]), kind))
            numbered.append(row_of)
        return call(functools.partial(sums_kernel, numbered, len(ins)), outs, ins, us=0.5)

    lines = lambda x: x.reshape(-1, HALF)

    if not ring:
        up_all = lax.all_gather(up_weight, "mp", axis=1, tiled=True)
        down_all = lax.all_gather(down_weight, "mp", axis=0, tiled=True)
        bias_all = lax.all_gather(up_bias, "mp", axis=0, tiled=True)
        packs = [up_all[:, :D], down_all[:D], bias_all[:D]]
        for k in range(1, 4):
            off = k * D + c * HALF
            u_part = lax.dynamic_slice(up_all, (0, off), (D, HALF))
            d_part = lax.dynamic_slice(down_all, (off, 0), (HALF, D))
            d_part = jnp.concatenate([d_part[:, :HALF], d_part[:, HALF:]], axis=0)
            b_part = jnp.broadcast_to(lax.dynamic_slice(bias_all, (off,), (HALF,))[None], (16, HALF))
            packs += [jnp.concatenate([u_part, b_part], axis=0), jnp.concatenate([d_part, b_part], axis=0)]
        first_low, down_sum, qkvs, g = make_qkv(packs[2])
        probs, atts = zip(*[attend(w, qkvs[w], first_low) for w in range(windows)])
        x, mid, att = project(atts)
        rows_of = (g, [send(part, core) for part in g], x, [send(part, core) for part in x])
        acc, keep0, send0, ub0 = mlp((0,), *rows_of, [], packs[0:3], mid)
        acc, both1, ub1 = mlp((1,), *rows_of, [acc], packs[3:5], mid)
        acc, keep2, send2, ub2 = mlp((2,), *rows_of, [acc], packs[5:7], mid)
        mine_back, back, *kept = mlp_front(*rows_of, acc, packs[7:9], mid)
        mine_out, theirs, keep3, send3, ub3 = mlp_rear(*rows_of, acc, *kept)
        mid_grad, dout, proj, sums = norm_two(mine_back, [send(back[w], core) for w in range(windows)], mid, att, mid)
        dqkv, kept, sent, rel = [], [], [], None
        for group in range(2):
            for w in range(windows):
                part, rel, *weights = heads(group, w, dout, rel, dqkv[group * windows :], mid_grad)
                dqkv.append(part)
            kept.append(weights[0])
            sent.append(weights[1])
        tokens_grad, small = norm_one(mid_grad, dqkv, (ub0, ub1, ub2, ub3), down_sum, sums, rel, mid_grad)
        tokens_grad, block_out = (turn(x) for x in outputs(tokens_grad, mine_out, send(theirs, core), mid, mid))
        dw = jnp.stack([jnp.stack([keep0, both1[0], keep2, keep3]), jnp.stack([send0, both1[1], send2, send3])])
        halves = dw.transpose(4, 0, 2, 5, 3, 1, 6).reshape(D, 2, 4, HALF)
        full = jnp.zeros((D, 2, 4, 2, HALF), BF16)
        full = lax.dynamic_update_slice(full, halves[:, :, :, None], (0, 0, 0, c, 0)).reshape(D, 2, 4 * D)
        full = lax.psum_scatter(full, "dp", scatter_dimension=0, tiled=True)
        full = lax.psum_scatter(full, "mp", scatter_dimension=2, tiled=True).astype(F32)
        up_grad, down_grad = full[:, 0], full[:, 1].T
        weights = jnp.stack([jnp.concatenate(kept, axis=2), jnp.concatenate(sent, axis=2)])
        weights = weights.transpose(0, 1, 2, 4, 3, 5).reshape(D, 8 * HALF)
        weights = lax.psum(weights, "mp")
        weights = lax.psum_scatter(weights, "dp", scatter_dimension=0, tiled=True).astype(F32)
        parts = [weights[:, i * HALF : (i + 1) * HALF] for i in range(8)]
        proj_grad = jnp.concatenate(parts[0:2], axis=1)
        qkv_grad = jnp.concatenate([parts[2], parts[5], parts[3], parts[6], parts[4], parts[7]], axis=1)
        small = lax.psum(join(small), AXES)
        vec = lambda start, count: small[start : start + count].reshape(count * HALF)
        table = small[24:40, 0:256].reshape(16, 4, 64).transpose(1, 0, 2).reshape(64, 64)
        rels = 2 * WIN - 1
        return (
            block_out, tokens_grad, vec(20, 2), vec(22, 2), qkv_grad, vec(16, 4), table[0:rels], table[32 : 32 + rels], proj_grad,
            vec(14, 2), vec(10, 2), vec(12, 2), up_grad, vec(2, 8), down_grad, vec(0, 2),
        )

    dp = lax.axis_index("dp")
    j = jnp.where(c == 0, dp // 2 % 2, dp // 4)
    off = c * HALF
    u_part = lax.dynamic_slice(up_weight, (0, off), (D, HALF))
    d_part = lax.dynamic_slice(down_weight, (off, 0), (HALF, D))
    b_part = jnp.broadcast_to(jnp.where(c == 0, up_bias[:HALF], up_bias[HALF:])[None], (32, HALF))
    halves = [jnp.where(j == 0, u_part[i * HALF : (i + 1) * HALF], d_part[:, i * HALF : (i + 1) * HALF]) for i in range(2)]
    pack = jnp.concatenate([*halves, b_part], axis=0)
    again = jnp.concatenate([*halves, b_part[:16]], axis=0)
    m1 = send(pack, up_ring)
    first_low, down_sum, qkvs, g = make_qkv(pack)
    prob0, att0 = attend(0, qkvs[0], pack)
    m1, att0 = tie(m1, att0)

    m2 = send(m1, up_ring)
    o1 = send(m1, first)
    probs, atts = zip((prob0, att0), *[attend(w, qkvs[w], m1) for w in range(1, windows)])
    x, mid, att = project(atts)
    gx = [*g, *x]
    sib = [send(part, core) for part in gx]
    m2, o1, *sib = tie(m2, o1, *sib)
    m3 = send(tie(again, m2)[0], down_ring)
    rows_of = (g, sib[:windows], x, sib[windows:])

    o2 = send(m2[:D], first)
    acc, keep0, send0, ub0 = mlp((0,), *rows_of, [], [up_weight, down_weight, up_bias], m2)
    acc, both1, ub1 = mlp((1,), *rows_of, [acc], [m1, o1], acc)
    m3, o2, acc = tie(m3, o2, acc)

    o3 = send(m3, first)
    got1 = send(both1, down_ring)
    acc, keep2, send2, ub2 = mlp((2,), *rows_of, [acc], [m2, o2], m3)
    o3, acc = tie(o3, acc)

    f2 = [send(send2[i], first) for i in range(2)]
    mine_back, back, *kept = mlp_front(*rows_of, acc, [m3, o3], o3)
    back_sib = [send(back[w], core) for w in range(windows)]
    mine_out, theirs, keep3, send3, ub3 = mlp_rear(*rows_of, acc, *kept)
    *f2, send3 = tie(*f2, send3)
    mid_grad, dout, proj, sums = norm_two(mine_back, back_sib, mid, att, f2[0])

    f3 = send(send3, first)
    s2_keep, s2_send = adds([(keep2, 0), f2[0]], [(keep2, 1), f2[1]])
    s2 = send(s2_send, second)
    part, rel = heads(0, 0, dout, None, [], dout)
    dqkv = [part]
    for w in range(1, windows):
        part, rel, *weights = heads(0, w, dout, rel, dqkv, dout)
        dqkv.append(part)
    keepq, sendq = weights
    f3, s2, got1, theirs, sendq, rel = tie(f3, s2, got1, theirs, sendq, rel)

    gotq = send(sendq, core)
    (s2_keep,) = adds([s2_keep, s2])
    got2 = send(s2_keep, far)
    f3, gotq = tie(f3, gotq)
    a_keep, a_send, s3_keep, s3_send = adds([keep0, (got1, 0)], [send0, (got1, 1)], [(keep3, 0), (f3, 0)], [(keep3, 1), (f3, 1)])
    s3 = send(s3_send, second)
    theirs_sib = send(theirs, core)
    q_keep, q_send = adds([(keepq, 0), (gotq, 0)], [(keepq, 1), (gotq, 1)])
    q1 = send(q_send, first)
    for w in range(windows):
        part, rel, *weights = heads(1, w, dout, rel, dqkv[windows:], q_send)
        dqkv.append(part)
    keepr, sendr = weights
    got2, q1, theirs_sib, rel, sendr, s3 = tie(got2, q1, theirs_sib, rel, sendr, s3)

    gotr = send(sendr, core)
    r_keep, r_send = adds([(keepr, 0), (gotr, 0)], [(keepr, 1), (gotr, 1)])
    r1 = send(lines(r_send), first)
    q_keep, q_send, s3_keep = adds([(q_keep, 0), (q1, 0)], [(q_keep, 1), (q1, 1)], [s3_keep, s3])
    got3 = send(s3_keep, up_ring)
    q2 = send(lines(q_send), second)
    tokens_grad, tail = norm_one(mid_grad, dqkv, (ub0, ub1, ub2, ub3), down_sum, sums, rel, r_send)
    stretch = [((2 * SMALL_ROWS, HALF), BF16)]
    (tail,) = call(tail_kernel, stretch, [tail, send(tail, core)], us=0.5)
    other = send(tail, first)
    r1, q2, other, got3 = tie(r1, q2, other, got3)

    size = r1.shape[0] // 2
    stay, away = call(second_kernel, [((size, HALF), BF16), ((size + 2 * SMALL_ROWS, HALF), BF16)], [lines(r_keep), r1, tail, other], us=0.5)
    r2 = send(away, second)
    half = q2.shape[0] // 2
    q_stay, q_away = call(halve_kernel, [((half, HALF), BF16)] * 2, [lines(q_keep), q2], us=0.5)
    q3 = send(q_away, near)
    tokens_grad, block_out = outputs(tokens_grad, mine_out, theirs_sib, mid, r1)
    r2, q3, tokens_grad = tie(r2, q3, tokens_grad)
    a1 = send(tie(a_send, r2)[0], first)

    size //= 2
    shapes = [((size, HALF), BF16), ((size + SMALL_ROWS, HALF), BF16)]
    stay, away = call(near_kernel, shapes, [stay, r2, away], us=0.5)
    r3 = send(away, near)
    (q_stay,) = adds([q_stay, q3])
    q4 = send(q_stay, far)
    r3, q4, a1 = tie(r3, q4, a1)

    (away,) = call(far_kernel, shapes[1:], [stay, r3, away], us=0.5)
    r4 = send(away, far)
    (q_stay,) = adds([q_stay, q4])
    q5 = send(q_stay, near)
    a_keep, a_send = adds([(a_keep, 0), (a1, 0)], [(a_keep, 1), (a1, 1)])
    a2 = send(a_send, second)
    r4, a2 = tie(r4, a2)

    (r_half,) = adds([(away, slice(0, size)), (r4, slice(0, size))])
    a2, r_half = tie(a2, r_half)
    r5 = send(r_half, near)
    mlp_part, = adds([a_keep, a2, got2, got3])
    other = send(mlp_part[:, 1], core)
    vec = lambda n: ((n,), F32)
    table = ((2 * WIN - 1, 64), F32)
    outs = [((96, 3 * D), F32)] + [((96, D), F32)] * 3 + [vec(D), vec(D), vec(2 * D), table, table, vec(D), vec(D), vec(D), vec(4 * D), vec(D)]
    qkv_grad, proj_grad, up_grad, down_grad, n1g, n1s, qvb, relh, relw, pb, n2g, n2s, upb, db = call(
        finish_kernel, outs, [r_half, r5, away, r4, q_stay, q5, mlp_part, other],
        [pltpu.VMEM((SMALL_ROWS, HALF), F32), pltpu.VMEM((3 * 96, HALF), F32), pltpu.VMEM((5 * 96, HALF), F32)], us=2.0)
    return turn(block_out), turn(tokens_grad), n1g, n1s, qkv_grad, qvb, relh, relw, proj_grad, pb, n2g, n2s, up_grad, upb, down_grad.T, db


def solution(mesh):
    split_rows = P(AXES, None, None)
    in_specs = (split_rows, P(AXES, None), split_rows) + (P(),) * 10 + (P(None, "mp"), P("mp"), P("mp", None), P())
    out_specs = (split_rows, split_rows, P(), P(), P("dp", None), P(), P(), P(), P("dp", None), P(), P(), P(), P("dp", "mp"), P(), P("mp", "dp"), P())
    return jax.shard_map(local, mesh=mesh, in_specs=in_specs, out_specs=out_specs, check_vma=False)
```
